32 devices in a mesh: rows: 8 (over z, x), tp: 4 (over y, core).
Axes of the slice: x: 2, y: 2, z: 4, core: 2. Of those that a mesh axis runs over, the one named last changes fastest.
Arguments:
- tokens: bfloat16 [24576, 768], P(('rows', 'tp')), may hold values from -6 to 6
- frame_id: int32 [24576], P(('rows', 'tp')), may hold values from 0 to 15, as said below
- lead_index: int32 [16], P('rows'), may hold values from 0 to 31
- lead_embed: bfloat16 [32, 768], replicated, may hold values from -3 to 3
- ln1_gain: bfloat16 [768], replicated, may hold values from 0.5 to 1.5
- ln1_bias: bfloat16 [768], replicated, may hold values from -1 to 1
- qkv_weight: bfloat16 [3, 768, 768], P(None, None, 'tp'), may hold values from -0.21875 to 0.21875
- qv_bias: bfloat16 [2, 768], P(None, 'tp'), may hold values from -1.5 to 1.5
- out_weight: bfloat16 [768, 768], P('tp'), may hold values from -6 to 6
- out_bias: bfloat16 [768], replicated, may hold values from -1 to 1
- ln2_gain: bfloat16 [768], replicated, may hold values from 0.5 to 1.5
- ln2_bias: bfloat16 [768], replicated, may hold values from -1 to 1
- up_weight: bfloat16 [768, 3072], P(None, 'tp'), may hold values from -0.21875 to 0.21875
- up_bias: bfloat16 [3072], P('tp'), may hold values from -1.5 to 1.5
- down_weight: bfloat16 [3072, 768], P('tp'), may hold values from -0.109375 to 0.109375
- down_bias: bfloat16 [768], replicated, may hold values from -1 to 1
- out_grad: bfloat16 [24576, 768], P(('rows', 'tp')), may hold values from -6 to 6
Outputs:
- layer_out: bfloat16 [24576, 768], P(('rows', 'tp'))
- tokens_grad: float32 [24576, 768], P(('rows', 'tp'))
- lead_embed_grad: float32 [32, 768], replicated
- ln1_gain_grad: float32 [768], replicated
- ln1_bias_grad: float32 [768], replicated
- qkv_weight_grad: float32 [3, 768, 768], P(None, None, 'tp')
- qv_bias_grad: float32 [2, 768], P(None, 'tp')
- out_weight_grad: float32 [768, 768], P('tp')
- out_bias_grad: float32 [768], replicated
- ln2_gain_grad: float32 [768], replicated
- ln2_bias_grad: float32 [768], replicated
- up_weight_grad: float32 [768, 3072], P(None, 'tp')
- up_bias_grad: float32 [3072], P('tp')
- down_weight_grad: float32 [3072, 768], P('tp')
- down_bias_grad: float32 [768], replicated
The draws below stay inside these ranges and needn't reach their ends.
Inputs may be any that keep to these rules, and one draw needn't show every extreme that they name: `frame_id`: patches 3072 * r to 3072 * r + 3071 carry frame ids 2 * r to 2 * r + 1; of these, id 2 * r names exactly 2048 patches and id 2 * r + 1 exactly 1024, in any order.
All inputs are finite; a program needn't handle non-finite values.
Results may differ from the reference program's by a relative error of at most 0.012.
Values may be sent and summed in bfloat16 or wider, within the bound.
No kernel may reach another device: no remote copies, remote signals or barrier semaphores. Data moves between devices by JAX's collectives and lax.ppermute only.
A program may use at most 192 MiB of HBM per device.

```python
import math
import jax
import jax.numpy as jnp
from jax import lax

D = 768
HEADS = 12
HEAD = 64
FF = 3072
LONG = 2048
SHORT = 1024
LEADS = 32
PAIRS = 1
GROUP_TOK = 3072
TOKENS = 24576
FRAMES = 16


def draw_frame_id(key, part):
    key = jax.random.fold_in(key, 11)
    groups = TOKENS // GROUP_TOK
    places = jnp.arange(GROUP_TOK, dtype=jnp.int32)
    labels = jnp.where(places < PAIRS * LONG, places // LONG, PAIRS + (places - PAIRS * LONG) // SHORT).astype(jnp.int32)
    group_keys = jax.random.split(key, groups)
    shuffled = jax.vmap(lambda group_key: jax.random.permutation(group_key, labels))(group_keys)
    offsets = (jnp.arange(groups, dtype=jnp.int32) * (2 * PAIRS))[:, None]
    return (shuffled + offsets).reshape(TOKENS).astype(jnp.int32)


def with_ends(array, key, smallest, largest):
    spot = [jax.random.randint(jax.random.fold_in(key, axis), (), 0, length) for axis, length in enumerate(array.shape)]
    widest = array.shape.index(max(array.shape))
    next_to = spot[:widest] + [(spot[widest] + 1) % array.shape[widest]] + spot[widest + 1:]
    return array.at[tuple(spot)].set(smallest).at[tuple(next_to)].set(largest)


def block_scale(rng, shape, shards, least, largest):
    factor_of, own = 1.0, jax.random.fold_in(rng, 6)
    for position, shards_of in shards:
        heights = jnp.exp(jax.random.uniform(jax.random.fold_in(own, position), (shards_of,), jnp.float32, least / len(shards), largest / len(shards)))
        factor_of = factor_of * jnp.repeat(heights, shape[position] // shards_of).reshape([-1 if axis == position else 1 for axis in range(len(shape))])
    return factor_of


def normal_values(rng, shape, scale, bound, pieces=(), kind=jnp.bfloat16):
    array = scale * jax.random.normal(rng, shape, jnp.float32)
    if pieces:
        array = array * block_scale(rng, shape, pieces, -0.22, 0.18)
    return jnp.clip(array, -bound, bound).astype(kind)


def setup_inputs(seed: int = 0) -> dict:
    arg_keys = jax.random.split(jax.random.key(seed), 18)
    return {
        "tokens": normal_values(arg_keys[0], (TOKENS, D), 1.0, 6.0, ((0, 32),)),
        "frame_id": draw_frame_id(jax.random.fold_in(arg_keys[17], 71), 0),
        "lead_index": with_ends(jax.random.randint(arg_keys[2], (FRAMES,), 0, LEADS), jax.random.fold_in(arg_keys[2], 1), 0, LEADS - 1).astype(jnp.int32),
        "lead_embed": normal_values(arg_keys[3], (LEADS, D), 0.5, 3.0),
        "ln1_gain": jnp.clip(1.0 + 0.1 * jax.random.normal(arg_keys[4], (D,), jnp.float32), 0.5, 1.5).astype(jnp.bfloat16),
        "ln1_bias": normal_values(arg_keys[5], (D,), 0.2, 1.0),
        "qkv_weight": normal_values(arg_keys[6], (3, D, D), D ** -0.5, 0.21875, ((2, 4),)),
        "qv_bias": normal_values(arg_keys[7], (2, D), 0.3, 1.5, ((1, 4),)),
        "out_weight": normal_values(arg_keys[8], (D, D), (max(1, (3 * D) // (2 * SHORT))) ** -0.5, 6.0, ((0, 4),)),
        "out_bias": normal_values(arg_keys[9], (D,), 0.2, 1.0),
        "ln2_gain": jnp.clip(1.0 + 0.1 * jax.random.normal(arg_keys[10], (D,), jnp.float32), 0.5, 1.5).astype(jnp.bfloat16),
        "ln2_bias": normal_values(arg_keys[11], (D,), 0.2, 1.0),
        "up_weight": normal_values(arg_keys[12], (D, FF), D ** -0.5, 0.21875, ((1, 4),)),
        "up_bias": normal_values(arg_keys[13], (FF,), 0.3, 1.5, ((0, 4),)),
        "down_weight": normal_values(arg_keys[14], (FF, D), FF ** -0.5, 0.109375, ((0, 4),)),
        "down_bias": normal_values(arg_keys[15], (D,), 0.2, 1.0),
        "out_grad": normal_values(arg_keys[16], (TOKENS, D), 1.0, 6.0, ((0, 32),)),
    }


@jax.custom_vjp
def low(v):
    return lax.optimization_barrier(v.astype(jnp.bfloat16)).astype(jnp.float32)

@jax.custom_vjp
def low_back(v):
    return v

def low_keep(v):
    return (low(v), None)

def low_pass(kept, grad):
    return (grad,)

def back_keep(v):
    return (v, None)

def back_low(kept, grad):
    return (low(grad),)
low.defvjp(low_keep, low_pass)
low_back.defvjp(back_keep, back_low)

def matmul(left, right):
    return jnp.dot(left, right, precision=lax.Precision.HIGHEST)

def norm_parts(values, norm_gain, norm_shift):
    average = lax.optimization_barrier(jnp.mean(values, axis=-1, keepdims=True))
    centred = values - average
    spread = lax.optimization_barrier(jnp.mean(centred * centred, axis=-1, keepdims=True))
    return centred * lax.rsqrt(spread + 1e-05) * norm_gain + norm_shift

def frame_layer(input_rows, frame_rows, params):
    gain_one, shift_one, qkv_all, qv_shift, out_proj, out_shift, gain_two, shift_two, up_proj, up_shift, down_proj, down_shift = params
    normed_one = low(norm_parts(input_rows, gain_one, shift_one))
    query_rows = low_back(low(matmul(normed_one, qkv_all[0]) + qv_shift[0]))
    key_rows = low_back(low(matmul(normed_one, qkv_all[1])))
    value_rows = low_back(low(matmul(normed_one, qkv_all[2]) + qv_shift[1]))
    group = input_rows.shape[0]
    query_heads = query_rows.reshape(group, HEADS, HEAD)
    key_heads = key_rows.reshape(group, HEADS, HEAD)
    value_heads = value_rows.reshape(group, HEADS, HEAD)
    block = min(512, group)
    scale = 1.0 / math.sqrt(HEAD)

    def attend(block_index):
        first_row = block_index * block
        query_block = lax.dynamic_slice_in_dim(query_heads, first_row, block, 0)
        frame_block = lax.dynamic_slice_in_dim(frame_rows, first_row, block, 0)
        scores = low_back(jnp.einsum('qhd,khd->hqk', query_block, key_heads, precision=lax.Precision.HIGHEST) * scale)
        live = frame_block[:, None] == frame_rows[None, :]
        scores = jnp.where(live[None], scores, -1e+30)
        probs = low(jax.nn.softmax(scores, axis=-1))
        return jnp.einsum('hqk,khd->qhd', probs, value_heads, precision=lax.Precision.HIGHEST)
    mixed = lax.map(jax.checkpoint(attend), jnp.arange(group // block, dtype=jnp.int32))
    attended = low_back(low(mixed.reshape(group, D)))
    x_one = input_rows + low_back(matmul(attended, out_proj) + out_shift)
    normed_two = low(norm_parts(x_one, gain_two, shift_two))
    hidden = low_back(matmul(normed_two, up_proj) + up_shift)
    activated = low(jax.nn.gelu(hidden))
    return x_one + low_back(matmul(activated, down_proj) + down_shift)

def reference(tokens, frame_id, lead_index, lead_embed, ln1_gain, ln1_bias, qkv_weight, qv_bias, out_weight, out_bias, ln2_gain, ln2_bias, up_weight, up_bias, down_weight, down_bias, out_grad):
    lead_of_token = jnp.take(lead_index, frame_id)
    floats = tuple((item.astype(jnp.float32) for item in (tokens, lead_embed, ln1_gain, ln1_bias, qkv_weight, qv_bias, out_weight, out_bias, ln2_gain, ln2_bias, up_weight, up_bias, down_weight, down_bias)))

    def forward(input_tokens, table, *params):
        input_rows = input_tokens + jnp.take(table, lead_of_token, axis=0)
        grouped = input_rows.reshape(-1, GROUP_TOK, D)
        frames = frame_id.reshape(-1, GROUP_TOK)

        def one_group(paired):
            return frame_layer(paired[0], paired[1], params)
        result = lax.map(jax.checkpoint(one_group), (grouped, frames))
        return result.reshape(-1, D)
    outcome, backward = jax.vjp(forward, *floats)
    grads = backward(out_grad.astype(jnp.float32))
    return (outcome.astype(jnp.bfloat16), grads[0], grads[1], grads[2], grads[3], grads[4], grads[5], grads[6], grads[7], grads[8], grads[9], grads[10], grads[11], grads[12], grads[13])
```

```python
import functools
import math

import jax
import jax.numpy as jnp
from jax import lax
from jax.experimental import pallas as pl
from jax.experimental.pallas import tpu as pltpu
from jax.sharding import PartitionSpec as P

HEAD = 64
EPS = 1e-05
LOG2E = math.log2(math.e)
LN2 = math.log(2.0)
TILE = 256
PAD = 16
VMEM_LIMIT = 60 * 1024 * 1024

f32 = jnp.float32
bf16 = jnp.bfloat16
i32 = jnp.int32

CORE = ((0, 1), (1, 0), (2, 3), (3, 2))
NEXT = ((0, 2), (2, 0), (1, 3), (3, 1))
DIAG = ((0, 3), (3, 0), (1, 2), (2, 1))

PARAMS = pltpu.CompilerParams(vmem_limit_bytes=VMEM_LIMIT)


def iota(shape, axis):
    return lax.broadcasted_iota(i32, shape, axis)


def dot(left, right, dims):
    return lax.dot_general(left, right, (dims, ((), ())), preferred_element_type=f32)


NN = ((1,), (0,))
NT = ((1,), (1,))
TN = ((0,), (0,))


def shape_of(shape, dtype):
    return jax.ShapeDtypeStruct(shape, dtype)


def whole_specs(count):
    return [pl.BlockSpec(memory_space=pltpu.VMEM)] * count


SMEM = pl.BlockSpec(memory_space=pltpu.SMEM)
VMEM = pl.BlockSpec(memory_space=pltpu.VMEM)
HBM = pl.BlockSpec(memory_space=pl.ANY)


def call(body, out_shape, in_specs, out_specs, name, flops=0, nbytes=0, scratch=(), grid=()):
    return pl.pallas_call(
        body,
        out_shape=out_shape,
        grid=grid,
        in_specs=in_specs,
        out_specs=out_specs,
        scratch_shapes=scratch,
        compiler_params=PARAMS,
        name=name,
        cost_estimate=pl.CostEstimate(
            flops=int(flops), bytes_accessed=int(nbytes), transcendentals=0
        ),
    )


def lead_hot(frame_ref, lead_ref, leads):
    frame = frame_ref[...]
    lead = jnp.where(frame == 0, lead_ref[0], lead_ref[1])
    return (iota((leads, frame.shape[1]), 0) == lead).astype(bf16)


def rows_with_lead(tok_ref, frame_ref, lead_ref, table_ref):
    hot = lead_hot(frame_ref, lead_ref, table_ref.shape[0])
    return tok_ref[...].astype(f32) + dot(hot, table_ref[...], TN), hot


def norm_stats(values):
    average = jnp.mean(values, axis=-1, keepdims=True)
    centred = values - average
    spread = jnp.mean(centred * centred, axis=-1, keepdims=True)
    inverse = lax.rsqrt(spread + EPS)
    return centred * inverse, inverse


def pre_kernel(tok_ref, frame_ref, lead_ref, table_ref, gain_ref, shift_ref, out_ref, perm_ref):
    rows = tok_ref.shape[0]
    values, _ = rows_with_lead(tok_ref, frame_ref, lead_ref, table_ref)
    unit, _ = norm_stats(values)
    normed = (unit * gain_ref[...] + shift_ref[...]).astype(bf16)
    first = (frame_ref[...] == 0).astype(f32)
    before = (iota((rows, rows), 0) < iota((rows, rows), 1)).astype(bf16)
    earlier = dot(jnp.broadcast_to(first, (8, rows)).astype(bf16), before, NN)[0:1]
    count = jnp.sum(first, axis=1, keepdims=True)
    place = jnp.where(first > 0, earlier, count + iota((1, rows), 1).astype(f32) - earlier)
    perm = (iota((rows, rows), 0) == place.astype(i32)).astype(bf16)
    perm_ref[...] = perm
    out_ref[0:rows, :] = dot(perm, normed, NN).astype(bf16)
    high = jnp.floor(count * (1.0 / 16))
    low = count - 16 * high
    tail = iota((PAD, out_ref.shape[1]), 0)
    out_ref[rows : rows + PAD, :] = jnp.where(
        tail == 0, high, jnp.where(tail == 1, low, 0.0)
    ).astype(bf16)


def read_count(block_ref, rows):
    part = block_ref[rows : rows + PAD, 0:128].astype(f32)
    place, lane = iota(part.shape, 0), iota(part.shape, 1)
    worth = jnp.where(place == 0, 16.0, jnp.where(place == 1, 1.0, 0.0))
    return jnp.sum(jnp.where(lane == 0, part * worth, 0.0)).astype(i32)


def tile_moves(counts, rows, long, block, tile):
    count = counts[block]
    longs_before = sum(counts[:block], jnp.int32(0))
    shorts_before = block * rows - longs_before
    limit = jnp.clip(count - tile * TILE, 0, TILE)
    moves = []
    base = longs_before + tile * TILE
    spot = base // TILE
    shift = base - spot * TILE
    moves.append((spot, shift, 0, limit, limit > 0))
    moves.append((spot + 1, shift - TILE, 0, limit, shift + limit > TILE))
    base = long + shorts_before - count + tile * TILE
    spot = base // TILE
    shift = base - spot * TILE
    some = limit < TILE
    moves.append((spot, shift, limit, TILE, some & (shift + limit < TILE)))
    moves.append((spot + 1, shift - TILE, limit, TILE, some & (shift > 0)))
    return moves


def aligned(index, size):
    return pl.ds(pl.multiple_of(index * size, size), size)


def to_group(value, dst_ref, moves, columns=slice(None)):
    for spot, shift, low, high, some in moves:

        @pl.when(some)
        def _():
            dest, source = iota((TILE, TILE), 0), iota((TILE, TILE), 1)
            hot = (dest - source == shift) & (source >= low) & (source < high)
            moved = dot(hot.astype(bf16), value, NN)
            place = (aligned(spot, TILE), columns)
            dst_ref[place] = (dst_ref[place].astype(f32) + moved).astype(dst_ref.dtype)


def from_group(src_ref, acc_ref, moves):
    acc_ref[...] = jnp.zeros(acc_ref.shape, acc_ref.dtype)
    for spot, shift, low, high, some in moves:

        @pl.when(some)
        def _():
            source, dest = iota((TILE, TILE), 0), iota((TILE, TILE), 1)
            hot = (dest - source == shift) & (source >= low) & (source < high)
            acc_ref[...] += dot(hot.astype(bf16), src_ref[aligned(spot, TILE), :], NN)


def attend_kernel(
    x0_ref, x1_ref, x2_ref, x3_ref, weight_ref, bias_ref, scale_ref,
    att_ref, attended_ref, q_ref, k_ref, v_ref, counts_ref,
    qkv_ref, acc_ref,
):
    blocks = (x0_ref, x1_ref, x2_ref, x3_ref)
    rows = x0_ref.shape[0] - PAD
    group = len(blocks) * rows
    long = 2 * group // 3
    width = weight_ref.shape[1] // 3
    heads = width // HEAD
    counts = [read_count(ref, rows) for ref in blocks]
    for index, count in enumerate(counts):
        counts_ref[index] = count
    qkv_ref[...] = jnp.zeros(qkv_ref.shape, qkv_ref.dtype)
    for index, ref in enumerate(blocks):

        def project(tile, _, index=index, ref=ref):
            value = dot(ref[aligned(tile, TILE), :], weight_ref[...], NN)
            value = ((value + bias_ref[...]) * scale_ref[...]).astype(bf16)
            to_group(value, qkv_ref, tile_moves(counts, rows, long, index, tile))
            return 0

        lax.fori_loop(0, rows // TILE, project, 0)
    for head in range(heads):
        lane = iota((group, 128), 1)
        for part, ref, fill in ((0, q_ref, 0.0), (1, k_ref, 1.0), (2, v_ref, 1.0)):
            start = part * width + head * HEAD
            first = start // 128 * 128
            piece = qkv_ref[:, first : first + 128].astype(f32) if first + 128 <= 3 * width else None
            if piece is None:
                piece = jnp.concatenate(
                    [qkv_ref[:, first : first + HEAD].astype(f32)] * 2, axis=1
                )
            if start != first:
                piece = pltpu.roll(piece, HEAD, 1)
            ref[head] = jnp.where(lane < HEAD, piece, fill).astype(bf16)

    def one_block(first, block, low, high):
        place = pl.ds(pl.multiple_of(first, block), block)
        outs = []
        lane = iota((block, 128), 1)
        for head in range(heads):
            query = q_ref[head, place, :]
            scores = dot(query, k_ref[head, low:high, :], NT)
            largest = jnp.max(scores, axis=1, keepdims=True)
            raised = jnp.exp2(scores - largest).astype(bf16)
            mixed = dot(raised, v_ref[head, low:high, :], NN)
            totals = mixed[:, HEAD : HEAD + 1]
            outs.append(jnp.where(lane < HEAD, mixed / totals, 0.0))
            less = -(largest + jnp.log2(totals))
            one = less.astype(bf16).astype(f32)
            two = (less - one).astype(bf16).astype(f32)
            three = less - one - two
            extra = jnp.where(
                lane == HEAD, one, jnp.where(lane == HEAD + 1, two, jnp.where(lane == HEAD + 2, three, 0.0))
            )
            q_ref[head, place, :] = jnp.where(lane < HEAD, query.astype(f32), extra).astype(bf16)
        for pair in range((heads + 1) // 2):
            value = outs[2 * pair]
            if 2 * pair + 1 < heads:
                value = value + pltpu.roll(outs[2 * pair + 1], HEAD, 1)
            att_ref[place, pair * 128 : (pair + 1) * 128] = value.astype(bf16)

    block = TILE

    def long_step(step, _):
        one_block(step * block, block, 0, long)
        return 0

    def short_step(step, _):
        one_block(long + step * block, block, long, group)
        return 0

    lax.fori_loop(0, long // block, long_step, 0)
    lax.fori_loop(0, (group - long) // block, short_step, 0)
    for index in range(len(blocks)):

        def hand_back(tile, _, index=index):
            from_group(att_ref, acc_ref, tile_moves(counts, rows, long, index, tile))
            attended_ref[index, aligned(tile, TILE), :] = acc_ref[:, 0:width].astype(bf16)
            return 0

        lax.fori_loop(0, rows // TILE, hand_back, 0)


def middle_kernel(
    tok_ref, frame_ref, lead_ref, table_ref, perm_ref,
    at0_ref, at1_ref, at2_ref, at3_ref,
    wo0_ref, wo1_ref, wo2_ref, wo3_ref,
    up0_ref, up1_ref, up2_ref, up3_ref,
    ub0_ref, ub1_ref, ub2_ref, ub3_ref,
    dn0_ref, dn1_ref, dn2_ref, dn3_ref,
    vec_ref, og_ref,
    layer_ref, xgrad_ref, agrad_ref, normed_ref, act_ref, hid_ref, attu_ref, send_ref, sums_ref, upb_ref,
    y_ref, back_ref,
):
    ats = (at0_ref, at1_ref, at2_ref, at3_ref)
    wos = (wo0_ref, wo1_ref, wo2_ref, wo3_ref)
    ups = (up0_ref, up1_ref, up2_ref, up3_ref)
    ubs = (ub0_ref, ub1_ref, ub2_ref, ub3_ref)
    dns = (dn0_ref, dn1_ref, dn2_ref, dn3_ref)
    gain, shift, out_bias, down_bias = (vec_ref[i : i + 1, :] for i in range(4))
    values, _ = rows_with_lead(tok_ref, frame_ref, lead_ref, table_ref)
    perm = perm_ref[...]
    x_one = values + out_bias
    for index in range(4):
        mine = dot(perm, ats[index][...], TN).astype(bf16)
        attu_ref[index] = mine
        x_one = x_one + dot(mine, wos[index][...], NN)
    unit, inverse = norm_stats(x_one)
    normed_ref[...] = (unit * gain + shift).astype(bf16)
    y_ref[...] = x_one + down_bias
    back_ref[...] = jnp.zeros(back_ref.shape, f32)
    hidden = up0_ref.shape[1]
    chunk = TILE
    for index in range(4):

        def step(part, _, index=index):
            cols = aligned(part, chunk)
            up = ups[index][:, cols]
            down = dns[index][cols, :]
            h = dot(normed_ref[...], up, NN) + ubs[index][0:1, cols].astype(f32)
            g = dot(og_ref[...], down, NT)
            c = math.sqrt(2.0 / math.pi)
            h2 = h * h
            t = jnp.tanh(h * (c + (c * 0.044715) * h2))
            half = 0.5 + 0.5 * t
            act = h * half
            slope = half + act * (1.0 - t) * (c + (3 * c * 0.044715) * h2)
            hid = (slope * g).astype(bf16)
            actb = act.astype(bf16)
            act_ref[index, :, cols] = actb
            hid_ref[index, :, cols] = hid
            upb_ref[index, 0:8, cols] = jnp.broadcast_to(
                jnp.sum(hid.astype(f32), axis=0, keepdims=True), (8, chunk)
            )
            y_ref[...] += dot(actb, down, NN)
            back_ref[...] += dot(hid, up, NT)
            return 0

        lax.fori_loop(0, hidden // chunk, step, 0)
    layer_ref[...] = y_ref[...].astype(bf16)
    grad = back_ref[...]
    e = grad * gain
    spread_mean = jnp.mean(e, axis=-1, keepdims=True)
    along = jnp.mean(e * unit, axis=-1, keepdims=True)
    og = og_ref[...].astype(f32)
    xgrad = og + inverse * (e - spread_mean - unit * along)
    xgrad_ref[...] = xgrad
    agrad = xgrad.astype(bf16)
    agrad_ref[...] = agrad
    sums_ref[...] = jnp.concatenate(
        [
            jnp.sum(grad * unit, axis=0, keepdims=True),
            jnp.sum(grad, axis=0, keepdims=True),
            jnp.sum(agrad.astype(f32), axis=0, keepdims=True),
            jnp.sum(og, axis=0, keepdims=True),
            jnp.zeros((4, og.shape[1]), f32),
        ],
        axis=0,
    )
    for index in range(4):
        back = dot(agrad, wos[index][...], NT).astype(bf16)
        send_ref[index] = dot(perm, back, NN).astype(bf16)


def down_grad_kernel(act_ref, og_ref, send_ref, keep_ref):
    value = dot(act_ref[0], og_ref[...], TN).astype(bf16)
    step = pl.program_id(0)

    @pl.when(step < 2)
    def _():
        send_ref[0] = value

    @pl.when(step >= 2)
    def _():
        keep_ref[0] = value


def up_grad_kernel(normed_ref, hid_ref, attu_ref, agrad_ref, send_ref, keep_ref):
    one = dot(normed_ref[...], hid_ref[0], TN).astype(bf16)
    two = dot(attu_ref[0], agrad_ref[...], TN).astype(bf16)
    rows = one.shape[0]
    step = pl.program_id(0)

    @pl.when(step < 2)
    def _():
        send_ref[0, 0:rows, :] = one
        send_ref[0, rows:, :] = two

    @pl.when(step >= 2)
    def _():
        keep_ref[0, 0:rows, :] = one
        keep_ref[0, rows:, :] = two


def gather_grad_kernel(counts_ref, b0_ref, b1_ref, b2_ref, b3_ref, att_ref, out_ref, sorted_ref):
    blocks = (b0_ref, b1_ref, b2_ref, b3_ref)
    rows, width = b0_ref.shape
    group = 4 * rows
    long = 2 * group // 3
    heads = width // HEAD
    counts = [counts_ref[i] for i in range(4)]
    sorted_ref[...] = jnp.zeros(sorted_ref.shape, sorted_ref.dtype)
    for index, ref in enumerate(blocks):

        def place(tile, _, index=index, ref=ref):
            to_group(
                ref[aligned(tile, TILE), :], sorted_ref,
                tile_moves(counts, rows, long, index, tile), slice(0, width),
            )
            return 0

        lax.fori_loop(0, rows // TILE, place, 0)
    lane = iota((group, 128), 1)
    for head in range(heads):
        first = head // 2 * 128
        grad = sorted_ref[:, first : first + 128].astype(f32)
        value = att_ref[:, first : first + 128].astype(f32)
        inside = (lane >= (head % 2) * HEAD) & (lane < (head % 2 + 1) * HEAD)
        less = -jnp.sum(jnp.where(inside, grad * value, 0.0), axis=1, keepdims=True)
        if head % 2:
            grad = pltpu.roll(grad, HEAD, 1)
        one = less.astype(bf16).astype(f32)
        two = less - one
        extra = jnp.where(lane == HEAD, one, jnp.where(lane == HEAD + 1, two, 0.0))
        out_ref[head] = jnp.where(lane < HEAD, grad, extra).astype(bf16)


def attend_back_kernel(q_ref, k_ref, v_ref, g_ref, out_ref, dq_ref):
    group = q_ref.shape[1]
    long = 2 * group // 3
    block = 512
    lane = iota((block, 128), 1)

    def frame(low, high):
        count = (high - low) // block

        def key_step(kb, _):
            keys = pl.ds(pl.multiple_of(low + kb * block, block), block)
            key = k_ref[0, keys, :]
            value = v_ref[0, keys, :]

            def query_step(qb, carry):
                key_grad, value_grad = carry
                queries = pl.ds(pl.multiple_of(low + qb * block, block), block)
                query = q_ref[0, queries, :]
                grad = g_ref[0, queries, :]
                probs = jnp.exp2(dot(key, query, NT))
                score_grad = (probs * dot(value, grad, NT)).astype(bf16)
                value_grad = value_grad + dot(probs.astype(bf16), grad, NN)
                key_grad = key_grad + dot(score_grad, query, NN)
                dq_ref[queries, :] += dot(score_grad, key, TN)
                return key_grad, value_grad

            empty = jnp.zeros((block, 128), f32)
            key_grad, value_grad = lax.fori_loop(0, count, query_step, (empty, empty))
            key_grad = jnp.where(lane < HEAD, key_grad * LN2, 0.0)
            out_ref[keys, 0:128] = pltpu.roll(key_grad, HEAD, 1).astype(bf16)
            out_ref[keys, 128:256] = jnp.where(lane < HEAD, value_grad, 0.0).astype(bf16)
            return 0

        lax.fori_loop(0, count, key_step, 0)

    dq_ref[...] = jnp.zeros(dq_ref.shape, f32)
    frame(0, long)
    frame(long, group)
    wide = iota((group, 128), 1)
    query_grad = jnp.where(wide < HEAD, dq_ref[...] * (1.0 / math.sqrt(HEAD)), 0.0)
    out_ref[:, 0:128] = (query_grad + out_ref[:, 0:128].astype(f32)).astype(bf16)


def project_back_kernel(counts_ref, h0_ref, h1_ref, h2_ref, weight_ref, local_ref, back_ref, acc_ref):
    heads = (h0_ref, h1_ref, h2_ref)
    rows = local_ref.shape[1]
    group = 4 * rows
    long = 2 * group // 3
    counts = [counts_ref[i] for i in range(4)]
    for index in (3, 1, 2, 0):

        def step(tile, _, index=index):
            moves = tile_moves(counts, rows, long, index, tile)
            here = aligned(tile, TILE)
            total = None
            for head, ref in enumerate(heads):
                from_group(ref, acc_ref, moves)
                local = acc_ref[...].astype(bf16)
                local_ref[index, here, head * 256 : (head + 1) * 256] = local
                part = dot(local, weight_ref[:, head * 256 : (head + 1) * 256], NT)
                total = part if total is None else total + part
            back_ref[index, here, :] = total.astype(bf16)
            return 0

        lax.fori_loop(0, rows // TILE, step, 0)


def project_grad_kernel(x0_ref, x1_ref, x2_ref, x3_ref, local_ref, out_ref, sums_ref):
    rows = local_ref.shape[1]
    total, sums = None, None
    for index, ref in enumerate((x0_ref, x1_ref, x2_ref, x3_ref)):
        part = dot(ref[0:rows, :], local_ref[index], TN)
        total = part if total is None else total + part
        one = jnp.sum(local_ref[index].astype(f32), axis=0, keepdims=True)
        sums = one if sums is None else sums + one
    out_ref[...] = total.astype(bf16)
    sums_ref[...] = jnp.broadcast_to(sums, sums_ref.shape)


def last_kernel(
    tok_ref, frame_ref, lead_ref, table_ref, gain_ref, perm_ref, mine_ref, other_ref, xgrad_ref, out_ref, sums_ref,
):
    values, hot = rows_with_lead(tok_ref, frame_ref, lead_ref, table_ref)
    unit, inverse = norm_stats(values)
    local = (mine_ref[...].astype(f32) + other_ref[...].astype(f32)).astype(bf16)
    grad = dot(perm_ref[...], local, TN)
    e = grad * gain_ref[...]
    mean_e = jnp.mean(e, axis=-1, keepdims=True)
    along = jnp.mean(e * unit, axis=-1, keepdims=True)
    out = xgrad_ref[...] + inverse * (e - mean_e - unit * along)
    out_ref[...] = out
    leads = table_ref.shape[0]
    one = out.astype(bf16)
    rest = out - one.astype(f32)
    two = rest.astype(bf16)
    three = (rest - two.astype(f32)).astype(bf16)
    sums_ref[0:leads, :] = dot(hot, one, NN) + dot(hot, two, NN) + dot(hot, three, NN)
    sums_ref[leads : leads + 8, :] = jnp.concatenate(
        [
            jnp.sum(grad * unit, axis=0, keepdims=True),
            jnp.sum(grad, axis=0, keepdims=True),
            jnp.zeros((6, grad.shape[1]), f32),
        ],
        axis=0,
    )


def bits_of(size):
    bits = []
    step = 1
    while step < size:
        bits.append(step)
        step *= 2
    return bits


def swap(value, axis, size, bit):
    return lax.ppermute(value, axis, [(i, i ^ bit) for i in range(size)])


def add_low(left, right):
    return (left.astype(f32) + right.astype(f32)).astype(bf16)


def sum_over_tp(send, keep):
    got = lax.ppermute(send, "tp", CORE)
    other = add_low(keep[1], got[1])
    far = lax.ppermute(other, "tp", NEXT)
    return add_low(add_low(keep[0], got[0]), far)


def sum_over_rows(value, size):
    me = lax.axis_index("rows")
    bits = bits_of(size)
    for bit in bits:
        half = value.shape[0] // 2
        high = (me // bit) % 2
        away = lax.dynamic_slice_in_dim(value, (1 - high) * half, half, 0)
        here = lax.dynamic_slice_in_dim(value, high * half, half, 0)
        value = add_low(here, swap(away, "rows", size, bit))
    for bit in reversed(bits):
        half = value.shape[0]
        high = (me // bit) % 2
        got = swap(value, "rows", size, bit)
        value = jnp.where(
            high == 1, jnp.concatenate([got, value], 0), jnp.concatenate([value, got], 0)
        )
    return value


def sum_everywhere(value, size):
    for pairs in (CORE, NEXT):
        value = value + lax.ppermute(value, "tp", pairs)
    for bit in bits_of(size):
        value = value + swap(value, "rows", size, bit)
    return value


def on_device(
    rows_size,
    tokens, frame_id, lead_index, lead_embed, ln1_gain, ln1_bias, qkv_weight, qv_bias,
    out_weight, out_bias, ln2_gain, ln2_bias, up_weight, up_bias, down_weight, down_bias, out_grad,
):
    rows, width_all = tokens.shape
    width = qkv_weight.shape[2]
    heads = width // HEAD
    hidden = up_weight.shape[1]
    leads = lead_embed.shape[0]
    group = 4 * rows
    long = 2 * group // 3
    pairs = long * long + (group - long) * (group - long)
    frames_here = lead_index.shape[0]
    frame = (frame_id - lax.axis_index("rows") * frames_here).reshape(1, rows)
    gain_one = ln1_gain.astype(f32).reshape(1, width_all)
    shift_one = ln1_bias.astype(f32).reshape(1, width_all)

    mine, perm = call(
        pre_kernel,
        (shape_of((rows + PAD, width_all), bf16), shape_of((rows, rows), bf16)),
        [VMEM, VMEM, SMEM, VMEM, VMEM, VMEM], (VMEM, VMEM), "pre",
        4 * rows * rows * width_all, 4 * rows * width_all * 2,
    )(tokens, frame, lead_index, lead_embed, gain_one, shift_one)

    near = lax.ppermute(mine, "tp", CORE)
    far = lax.ppermute(mine, "tp", NEXT)
    across = lax.ppermute(far, "tp", CORE)
    parts = (mine, near, far, across)

    up_bias_row = jnp.broadcast_to(up_bias.reshape(1, hidden), (PAD, hidden))

    def weight_set(value):
        near_w = lax.ppermute(value, "tp", CORE)
        far_w = lax.ppermute(value, "tp", NEXT)
        across_w = lax.ppermute(far_w, "tp", CORE)
        return (value, near_w, far_w, across_w)

    outs_w = weight_set(out_weight)
    ups_w = weight_set(up_weight)
    ubs_w = weight_set(up_bias_row)
    downs_w = weight_set(down_weight)

    weight_qkv = jnp.concatenate([qkv_weight[0], qkv_weight[1], qkv_weight[2]], axis=1)
    zero = jnp.zeros((width,), f32)
    bias_qkv = jnp.concatenate([qv_bias[0].astype(f32), zero, qv_bias[1].astype(f32)]).reshape(1, 3 * width)
    scale_qkv = jnp.concatenate(
        [jnp.full((width,), LOG2E / math.sqrt(HEAD), f32), jnp.ones((2 * width,), f32)]
    ).reshape(1, 3 * width)
    headed = qkv_weight.reshape(3, width_all, heads, HEAD).transpose(1, 2, 0, 3)
    weight_heads = jnp.pad(headed, ((0, 0), (0, 0), (0, 1), (0, 0))).reshape(width_all, heads * 4 * HEAD)

    wide = (heads + 1) // 2 * 128
    att, attended, q_all, k_all, v_all, counts = call(
        attend_kernel,
        (
            shape_of((group, wide), bf16),
            shape_of((4, rows, width), bf16),
            shape_of((heads, group, 128), bf16),
            shape_of((heads, group, 128), bf16),
            shape_of((heads, group, 128), bf16),
            shape_of((8,), i32),
        ),
        whole_specs(7), (VMEM,) * 5 + (SMEM,), "attend",
        4 * pairs * 256 * heads, 20 * group * width,
        scratch=[pltpu.VMEM((group, 3 * width), bf16), pltpu.VMEM((TILE, wide), f32)],
    )(*parts, weight_qkv, bias_qkv, scale_qkv)

    got = [attended[0]] + [
        lax.ppermute(attended[i], "tp", ring) for i, ring in ((1, CORE), (2, NEXT), (3, DIAG))
    ]

    vectors = jnp.concatenate(
        [item.astype(f32).reshape(1, width_all) for item in (ln2_gain, ln2_bias, out_bias, down_bias)]
        + [jnp.zeros((4, width_all), f32)]
    )
    layer_out, xgrad, agrad, normed_two, act, hid, attu, back_send, sums_two, up_b = call(
        middle_kernel,
        (
            shape_of((rows, width_all), bf16),
            shape_of((rows, width_all), f32),
            shape_of((rows, width_all), bf16),
            shape_of((rows, width_all), bf16),
            shape_of((4, rows, hidden), bf16),
            shape_of((4, rows, hidden), bf16),
            shape_of((4, rows, width), bf16),
            shape_of((4, rows, width), bf16),
            shape_of((8, width_all), f32),
            shape_of((4, 8, hidden), f32),
        ),
        [VMEM, VMEM, SMEM] + whole_specs(24), (VMEM,) * 10, "middle",
        32 * rows * width_all * hidden, 40 * rows * width_all,
        scratch=[pltpu.VMEM((rows, width_all), f32), pltpu.VMEM((rows, width_all), f32)],
    )(
        tokens, frame, lead_index, lead_embed, perm, *got, *outs_w, *ups_w, *ubs_w, *downs_w, vectors, out_grad,
    )

    got_grad = [back_send[0]] + [
        lax.ppermute(back_send[i], "tp", ring) for i, ring in ((1, CORE), (2, NEXT), (3, DIAG))
    ]

    def block_of(step):
        return jnp.where(step < 2, 2 * step + 1, 2 * step - 4)

    def share_specs(shape):
        return (
            pl.BlockSpec((1,) + shape, lambda s: (jnp.minimum(s, 1), 0, 0)),
            pl.BlockSpec((1,) + shape, lambda s: (jnp.maximum(s - 2, 0), 0, 0)),
        )

    def full(shape):
        return pl.BlockSpec(shape, lambda s: (0,) * len(shape))

    def picked(shape):
        return pl.BlockSpec((1,) + shape, lambda s: (block_of(s), 0, 0))

    down_send, down_keep = call(
        down_grad_kernel,
        (shape_of((2, hidden, width_all), bf16),) * 2,
        [picked((rows, hidden)), full((rows, width_all))],
        share_specs((hidden, width_all)), "down_grad",
        8 * rows * hidden * width_all, 16 * rows * width_all, grid=(4,),
    )(act, out_grad)
    tall = width_all + width
    up_send, up_keep = call(
        up_grad_kernel,
        (shape_of((2, tall, hidden), bf16),) * 2,
        [full((rows, width_all)), picked((rows, hidden)), picked((rows, width)), full((rows, width_all))],
        share_specs((tall, hidden)), "up_grad",
        10 * rows * hidden * width_all, 20 * rows * width_all, grid=(4,),
    )(normed_two, hid, attu, agrad)

    down_sum = sum_over_rows(sum_over_tp(down_send, down_keep), rows_size)
    up_sum = sum_over_rows(sum_over_tp(up_send, up_keep), rows_size)

    grad_all = call(
        gather_grad_kernel,
        shape_of((heads, group, 128), bf16),
        [SMEM] + whole_specs(5), VMEM, "gather_grad",
        2 * 4 * TILE * group * 256, 6 * group * 256,
        scratch=[pltpu.VMEM((group, wide), bf16)],
    )(counts, *got_grad, att)

    head_grads = []
    for head in range(heads):
        spec = pl.BlockSpec((1, group, 128), lambda s, head=head: (head, 0, 0))
        head_grads.append(
            call(
                attend_back_kernel,
                shape_of((group, 256), bf16),
                [spec] * 4, pl.BlockSpec((group, 256), lambda s: (0, 0)), "attend_back",
                10 * pairs * 256, 12 * group * 128,
                scratch=[pltpu.VMEM((group, 128), f32)], grid=(1,),
            )(q_all, k_all, v_all, grad_all)
        )

    local, back = call(
        project_back_kernel,
        (shape_of((4, rows, heads * 256), bf16), shape_of((4, rows, width_all), bf16)),
        [SMEM] + whole_specs(4), (VMEM, VMEM), "project_back",
        4 * group * width_all * 256 * heads, 8 * group * width_all,
        scratch=[pltpu.VMEM((TILE, 256), f32)],
    )(counts, *head_grads, weight_heads)

    over_core = lax.ppermute(back[3], "tp", CORE)
    over_core_two = lax.ppermute(back[1], "tp", CORE)
    from_far = lax.ppermute(add_low(back[2], over_core), "tp", NEXT)
    here = add_low(back[0], over_core_two)

    qkv_grad, qkv_sums = call(
        project_grad_kernel,
        (shape_of((width_all, heads * 256), bf16), shape_of((8, heads * 256), f32)),
        whole_specs(5), (VMEM, VMEM), "project_grad",
        2 * group * width_all * 256 * heads, 4 * group * width_all,
    )(*parts, local)

    tokens_grad, sums_one = call(
        last_kernel,
        (shape_of((rows, width_all), f32), shape_of((leads + 8, width_all), f32)),
        [VMEM, VMEM, SMEM] + whole_specs(6), (VMEM, VMEM), "last",
        2 * rows * rows * width_all, 16 * rows * width_all,
    )(tokens, frame, lead_index, lead_embed, gain_one, perm, here, from_far, xgrad)

    qkv_sum = sum_over_rows(qkv_grad, rows_size)
    small = jnp.concatenate([sums_one, sums_two], axis=0)
    small = sum_everywhere(small, rows_size)

    up_b = up_b[:, 0:1, :]
    near_b = lax.ppermute(jnp.stack([up_b[1], up_b[3]]), "tp", CORE)
    far_b = lax.ppermute(up_b[2] + near_b[1], "tp", NEXT)
    up_b_here = up_b[0] + near_b[0] + far_b
    split_sums = jnp.concatenate([up_b_here, qkv_sums[0:1]], axis=1)
    for bit in bits_of(rows_size):
        split_sums = split_sums + swap(split_sums, "rows", rows_size, bit)

    up_b_sum = split_sums[0, 0:hidden]
    qkv_bias = split_sums[0, hidden:].reshape(heads, 4, HEAD)
    qv_sum = jnp.stack([qkv_bias[:, 0].reshape(width), qkv_bias[:, 2].reshape(width)])
    qkv_out = (
        qkv_sum.reshape(width_all, heads, 4, HEAD)[:, :, 0:3]
        .transpose(2, 0, 1, 3)
        .reshape(3, width_all, width)
        .astype(f32)
    )
    return (
        layer_out,
        tokens_grad,
        small[0:leads],
        small[leads],
        small[leads + 1],
        qkv_out,
        qv_sum,
        up_sum[width_all:].astype(f32),
        small[leads + 10],
        small[leads + 8],
        small[leads + 9],
        up_sum[0:width_all].astype(f32),
        up_b_sum,
        down_sum.astype(f32),
        small[leads + 11],
    )


def solution(mesh):
    rows_size = mesh.shape["rows"]
    split = P(("rows", "tp"), None)
    placed = (
        split, P(("rows", "tp")), P("rows"), P(), P(), P(), P(None, None, "tp"), P(None, "tp"),
        P("tp", None), P(), P(), P(), P(None, "tp"), P("tp"), P("tp", None), P(), split,
    )
    return jax.shard_map(
        functools.partial(on_device, rows_size),
        mesh=mesh,
        in_specs=placed,
        out_specs=(
            split, split, P(), P(), P(), P(None, None, "tp"), P(None, "tp"), P("tp", None), P(), P(), P(),
            P(None, "tp"), P("tp"), P("tp", None), P(),
        ),
        check_vma=False,
    )
```

```python
import functools
import math

import jax
import jax.numpy as jnp
from jax import lax
from jax.experimental import pallas as pl
from jax.experimental.pallas import tpu as pltpu
from jax.sharding import PartitionSpec as P

HEAD = 64
EPS = 1e-05
LOG2E = math.log2(math.e)
LN2 = math.log(2.0)
TILE = 256
PAD = 16
VMEM_LIMIT = 60 * 1024 * 1024

f32 = jnp.float32
bf16 = jnp.bfloat16
i32 = jnp.int32

CORE = ((0, 1), (1, 0), (2, 3), (3, 2))
NEXT = ((0, 2), (2, 0), (1, 3), (3, 1))
DIAG = ((0, 3), (3, 0), (1, 2), (2, 1))

PARAMS = pltpu.CompilerParams(vmem_limit_bytes=VMEM_LIMIT)


def iota(shape, axis):
    return lax.broadcasted_iota(i32, shape, axis)


def dot(left, right, dims):
    return lax.dot_general(left, right, (dims, ((), ())), preferred_element_type=f32)


NN = ((1,), (0,))
NT = ((1,), (1,))
TN = ((0,), (0,))


def shape_of(shape, dtype):
    return jax.ShapeDtypeStruct(shape, dtype)


def whole_specs(count):
    return [pl.BlockSpec(memory_space=pltpu.VMEM)] * count


SMEM = pl.BlockSpec(memory_space=pltpu.SMEM)
VMEM = pl.BlockSpec(memory_space=pltpu.VMEM)
HBM = pl.BlockSpec(memory_space=pl.ANY)


def call(body, out_shape, in_specs, out_specs, name, micros, scratch=(), grid=()):
    return pl.pallas_call(
        body,
        out_shape=out_shape,
        grid=grid,
        in_specs=in_specs,
        out_specs=out_specs,
        scratch_shapes=scratch,
        compiler_params=PARAMS,
        name=name,
        cost_estimate=pl.CostEstimate(
            flops=int(micros * 1.15e9), bytes_accessed=1024, transcendentals=0
        ),
    )


def local_frame(frame_ref):
    return frame_ref[...].reshape(1, frame_ref.shape[0]) % 2


def row_of(ref):
    return ref[...].astype(f32).reshape(1, ref.shape[0])


def rows_with_lead(tok_ref, frame_ref, lead_ref, table_ref):
    frame = local_frame(frame_ref)
    lead = jnp.where(frame == 0, lead_ref[0], lead_ref[1])
    hot = (iota((table_ref.shape[0], frame.shape[1]), 0) == lead).astype(bf16)
    return tok_ref[...].astype(f32) + dot(hot, table_ref[...], TN), hot


def norm_stats(values):
    average = jnp.mean(values, axis=-1, keepdims=True)
    centred = values - average
    spread = jnp.mean(centred * centred, axis=-1, keepdims=True)
    inverse = lax.rsqrt(spread + EPS)
    return centred * inverse, inverse


def pre_kernel(tok_ref, frame_ref, lead_ref, table_ref, gain_ref, shift_ref, out_ref, perm_ref):
    rows = tok_ref.shape[0]
    values, _ = rows_with_lead(tok_ref, frame_ref, lead_ref, table_ref)
    unit, _ = norm_stats(values)
    normed = (unit * row_of(gain_ref) + row_of(shift_ref)).astype(bf16)
    first = (local_frame(frame_ref) == 0).astype(f32)
    before = (iota((rows, rows), 0) < iota((rows, rows), 1)).astype(bf16)
    earlier = dot(jnp.broadcast_to(first, (8, rows)).astype(bf16), before, NN)[0:1]
    count = jnp.sum(first, axis=1, keepdims=True)
    place = jnp.where(first > 0, earlier, count + iota((1, rows), 1).astype(f32) - earlier)
    perm = (iota((rows, rows), 0) == place.astype(i32)).astype(bf16)
    perm_ref[...] = perm
    out_ref[0:rows, :] = dot(perm, normed, NN).astype(bf16)
    high = jnp.floor(count * (1.0 / 16))
    low = count - 16 * high
    tail = iota((PAD, out_ref.shape[1]), 0)
    out_ref[rows : rows + PAD, :] = jnp.where(
        tail == 0, high, jnp.where(tail == 1, low, 0.0)
    ).astype(bf16)


def read_count(block_ref, rows):
    part = block_ref[rows : rows + PAD, 0:128].astype(f32)
    place, lane = iota(part.shape, 0), iota(part.shape, 1)
    worth = jnp.where(place == 0, 16.0, jnp.where(place == 1, 1.0, 0.0))
    return jnp.sum(jnp.where(lane == 0, part * worth, 0.0)).astype(i32)


def tile_moves(counts, rows, block, tile):
    group = 4 * rows
    count = counts[block]
    longs_before = sum(counts[:block], jnp.int32(0))
    limit = jnp.clip(count - tile * TILE, 0, TILE)
    moves = []
    for some, base, low, high in (
        (limit > 0, longs_before + tile * TILE, 0, limit),
        (limit < TILE, 2 * group // 3 + block * rows - longs_before - count + tile * TILE, limit, TILE),
    ):
        spot = jnp.minimum(base // TILE, group // TILE - 2)
        window = pl.ds(pl.multiple_of(spot * TILE, TILE), 2 * TILE)
        moves.append((some, window, base - spot * TILE, low, high))
    return moves


def aligned(index, size):
    return pl.ds(pl.multiple_of(index * size, size), size)


def to_group(value, dst_ref, moves):
    width = value.shape[1]
    for some, window, shift, low, high in moves:

        @pl.when(some)
        def _():
            dest, source = iota((2 * TILE, TILE), 0), iota((2 * TILE, TILE), 1)
            hot = (dest - source == shift) & (source >= low) & (source < high)
            moved = dot(hot.astype(bf16), value, NN).astype(bf16)
            dst_ref[window, 0:width] = dst_ref[window, 0:width] + moved


def from_group(src_refs, acc_refs, moves):
    (some_long, *long), (some_short, *short) = moves

    def moved(window, shift, low, high):
        source, dest = iota((TILE, 2 * TILE), 0), iota((TILE, 2 * TILE), 1)
        hot = ((dest - source == shift) & (source >= low) & (source < high)).astype(bf16)
        return [dot(hot, ref[window, :], NN).astype(bf16) for ref in src_refs]

    @pl.when(some_long)
    def _():
        for ref, value in zip(acc_refs, moved(*long)):
            ref[...] = value

    @pl.when(jnp.logical_not(some_long))
    def _():
        for ref, value in zip(acc_refs, moved(*short)):
            ref[...] = value

    @pl.when(some_long & some_short)
    def _():
        for ref, value in zip(acc_refs, moved(*short)):
            ref[...] = ref[...] + value


def head_columns(ref, start, width):
    first = start // 128 * 128
    if first + 128 <= width:
        piece = ref[:, first : first + 128].astype(f32)
    else:
        piece = jnp.concatenate([ref[:, first : first + HEAD].astype(f32)] * 2, axis=1)
    return pltpu.roll(piece, HEAD, 1) if start != first else piece


def attend_kernel(
    weight_ref, bias_ref, scale_ref, x0_ref, x1_ref, x2_ref, x3_ref,
    att_ref, lse_ref, counts_ref, a0_ref, a1_ref, a2_ref, a3_ref, q_out, k_out, v_out,
    x_buf, qkv_ref, q_ref, k_ref, v_ref, scores_ref, load_sems, store_sems,
):
    blocks = (x0_ref, x1_ref, x2_ref, x3_ref)
    rows = x0_ref.shape[0] - PAD
    group = len(blocks) * rows
    long = 2 * group // 3
    width = weight_ref.shape[1] // 3
    heads = width // HEAD
    loads = [pltpu.make_async_copy(blocks[i], x_buf.at[i], load_sems.at[i]) for i in range(4)]
    for load in loads:
        load.start()
    qkv_ref[...] = jnp.zeros(qkv_ref.shape, qkv_ref.dtype)
    for load in loads:
        load.wait()
    counts = [read_count(x_buf.at[i], rows) for i in range(4)]
    for index, count in enumerate(counts):
        counts_ref[index] = count
    for index in range(4):

        def project(tile, _, index=index):
            value = dot(x_buf[index, aligned(tile, TILE), :], weight_ref[...], NN)
            value = ((value + bias_ref[...]) * scale_ref[...]).astype(bf16)
            to_group(value, qkv_ref, tile_moves(counts, rows, index, tile))
            return 0

        lax.fori_loop(0, rows // TILE, project, 0)
    lane = iota((group, 128), 1)
    stores = []
    for part, ref, out, fill in ((1, k_ref, k_out, 0.0), (2, v_ref, v_out, 1.0), (0, q_ref, q_out, 0.0)):
        for head in range(heads):
            piece = head_columns(qkv_ref, part * width + head * HEAD, 3 * width)
            ref[head] = jnp.where(lane < HEAD, piece, fill).astype(bf16)
        store = pltpu.make_async_copy(ref, out, store_sems.at[part])
        store.start()
        stores.append(store)

    block = 512
    row = iota((128, block), 0)
    half = iota((block, 128), 1)
    tasks = [
        (head, first, low, high)
        for low, high in ((0, long), (long, group))
        for first in range(low, high, block)
        for head in range(heads)
    ]

    def scores(task, part):
        head, first, low, high = tasks[task]
        keys = slice(low + part * block, low + (part + 1) * block)
        value = dot(k_ref[head, keys, :], q_ref[head, first : first + block, :], NT)
        scores_ref[task % 2, part * block : (part + 1) * block, :] = value
        return jnp.max(value.reshape(block // 8, 8, block), axis=0)

    def parts_of(task):
        return (tasks[task][3] - tasks[task][2]) // block if task < len(tasks) else 0

    largest = functools.reduce(jnp.maximum, [scores(0, part) for part in range(parts_of(0))])
    outs = []
    for task, (head, first, low, high) in enumerate(tasks):
        top = jnp.max(largest, axis=0, keepdims=True)
        following, mixed = [], None
        for part in range(max(parts_of(task), parts_of(task + 1))):
            if part < parts_of(task + 1):
                following.append(scores(task + 1, part))
            if part < parts_of(task):
                raised = jnp.exp2(scores_ref[task % 2, part * block : (part + 1) * block, :] - top)
                keys = slice(low + part * block, low + (part + 1) * block)
                value = dot(v_ref[head, keys, :], raised.astype(bf16), TN)
                mixed = value if mixed is None else mixed + value
        if following:
            largest = functools.reduce(jnp.maximum, following)
        totals = mixed[HEAD : HEAD + 1, :]
        lse_ref[head : head + 1, first : first + block] = top + jnp.log2(totals)
        outs.append(jnp.where(row < HEAD, mixed / totals, 0.0))
        if head == heads - 1:
            for pair in range((heads + 1) // 2):
                value = outs[2 * pair].T
                if 2 * pair + 1 < heads:
                    value = value + pltpu.roll(outs[2 * pair + 1].T, HEAD, 1)
                att_ref[first : first + block, pair * 128 : (pair + 1) * 128] = value.astype(bf16)
            outs = []
    for index, out in enumerate((a0_ref, a1_ref, a2_ref, a3_ref)):

        def hand_back(tile, _, index=index, out=out):
            moves = tile_moves(counts, rows, index, tile)
            from_group((att_ref,), (qkv_ref.at[0:TILE, 0 : att_ref.shape[1]],), moves)
            out[aligned(tile, TILE), :] = qkv_ref[0:TILE, 0:width]
            return 0

        lax.fori_loop(0, rows // TILE, hand_back, 0)
    for store in stores:
        store.wait()


def middle_kernel(
    tok_ref, frame_ref, lead_ref, table_ref, perm_ref,
    at0_ref, at1_ref, at2_ref, at3_ref,
    wo0_ref, wo1_ref, wo2_ref, wo3_ref,
    gain_ref, shift_ref, out_bias_ref, down_bias_ref, og_ref, side_ref,
    up0_ref, up1_ref, ff2_ref, ff3_ref, dn0_ref, dn1_ref, dx2_ref, dx3_ref,
    layer_ref, xgrad_ref, agrad_ref, normed_ref, attu_ref, s0_ref, s1_ref, s2_ref, s3_ref, sums_ref, upb_ref,
    act_out, hid_out,
    y_ref, back_ref, up_buf, dn_buf, act_ref, hid_ref, load_sems, store_sems,
):
    ats = (at0_ref, at1_ref, at2_ref, at3_ref)
    wos = (wo0_ref, wo1_ref, wo2_ref, wo3_ref)
    upper = up0_ref.shape[0]
    ups = (up0_ref, up1_ref, ff2_ref.at[0:upper], ff3_ref.at[0:upper])
    dn2_ref, dn3_ref = ff2_ref.at[upper:], ff3_ref.at[upper:]
    sends = (s0_ref, s1_ref, s2_ref, s3_ref)
    rows, wide = tok_ref.shape
    hidden = act_ref.shape[2]
    half = hidden // 2
    side = side_ref[0]
    mine = pl.ds(pl.multiple_of(side * half, half), half)
    other = pl.ds(pl.multiple_of((1 - side) * half, half), half)
    loads = [[pltpu.make_async_copy(ups[i], up_buf.at[i], load_sems.at[i])] for i in range(4)]
    for index, ref, target, sem in (
        (0, dn0_ref, dn_buf.at[0], 4),
        (1, dn1_ref, dn_buf.at[1], 5),
        (2, dn2_ref, dn_buf.at[2, mine], 6),
        (2, dx2_ref, dn_buf.at[2, other], 7),
        (3, dn3_ref, dn_buf.at[3, mine], 8),
        (3, dx3_ref, dn_buf.at[3, other], 9),
    ):
        loads[index].append(pltpu.make_async_copy(ref, target, load_sems.at[sem]))
    for load in sum(loads, []):
        load.start()
    gain = row_of(gain_ref)
    values, _ = rows_with_lead(tok_ref, frame_ref, lead_ref, table_ref)
    perm = perm_ref[...]
    x_one = values + row_of(out_bias_ref)
    for index in range(4):
        mine = dot(perm, ats[index][...], TN).astype(bf16)
        attu_ref[index] = mine
        x_one = x_one + dot(mine, wos[index][...], NN)
    unit, inverse = norm_stats(x_one)
    normed_ref[...] = (unit * gain + row_of(shift_ref)).astype(bf16)
    y_ref[...] = x_one + row_of(down_bias_ref)
    back_ref[...] = jnp.zeros(back_ref.shape, f32)
    stores = []
    for index in range(4):
        for load in loads[index]:
            load.wait()
        up = up_buf[index, 0:wide, :]
        down = dn_buf[index]
        h = dot(normed_ref[...], up, NN) + up_buf[index, wide : wide + PAD, :][0:1].astype(f32)
        g = dot(og_ref[...], down, NT)
        c = math.sqrt(2.0 / math.pi)
        h2 = h * h
        t = jnp.tanh(h * (c + (c * 0.044715) * h2))
        half = 0.5 + 0.5 * t
        act = h * half
        slope = half + act * (1.0 - t) * (c + (3 * c * 0.044715) * h2)
        hid = (slope * g).astype(bf16)
        actb = act.astype(bf16)
        act_ref[index] = actb
        hid_ref[index] = hid
        upb_ref[index] = jnp.broadcast_to(jnp.sum(hid.astype(f32), axis=0, keepdims=True), (8, hidden))
        y_ref[...] += dot(actb, down, NN)
        back_ref[...] += dot(hid, up, NT)
        for source, target, sem in ((act_ref, act_out, 0), (hid_ref, hid_out, 4)):
            store = pltpu.make_async_copy(source.at[index], target.at[index], store_sems.at[sem + index])
            store.start()
            stores.append(store)
    layer_ref[...] = y_ref[...].astype(bf16)
    grad = back_ref[...]
    e = grad * gain
    spread_mean = jnp.mean(e, axis=-1, keepdims=True)
    along = jnp.mean(e * unit, axis=-1, keepdims=True)
    og = og_ref[...].astype(f32)
    xgrad = og + inverse * (e - spread_mean - unit * along)
    xgrad_ref[...] = xgrad
    agrad = xgrad.astype(bf16)
    agrad_ref[...] = agrad
    for index in range(4):
        back = dot(agrad, wos[index][...], NT).astype(bf16)
        sends[index][...] = dot(perm, back, NN).astype(bf16)
    sums_ref[...] = jnp.concatenate(
        [
            jnp.sum(grad * unit, axis=0, keepdims=True),
            jnp.sum(grad, axis=0, keepdims=True),
            jnp.sum(agrad.astype(f32), axis=0, keepdims=True),
            jnp.sum(og, axis=0, keepdims=True),
            jnp.zeros((4, og.shape[1]), f32),
        ],
        axis=0,
    )
    for store in stores:
        store.wait()


def weight_grad_kernel(normed_ref, og_ref, agrad_ref, act_ref, hid_ref, attu_ref, send_ref, keep_ref):
    up = dot(normed_ref[...], hid_ref[0], TN).astype(bf16)
    out = dot(attu_ref[0], agrad_ref[...], TN).astype(bf16)
    down = dot(act_ref[0], og_ref[...], TN).astype(bf16)
    rows, more = up.shape[0], out.shape[0]
    step = pl.program_id(0)
    for chosen, ref in ((step < 2, send_ref), (step >= 2, keep_ref)):

        @pl.when(chosen)
        def _(ref=ref):
            ref[0, 0:rows, :] = up
            ref[0, rows : rows + more, :] = out
            ref[0, rows + more :, :] = down


def gather_grad_kernel(counts_ref, b0_ref, b1_ref, b2_ref, b3_ref, att_ref, out_ref, inner_ref, sorted_ref):
    blocks = (b0_ref, b1_ref, b2_ref, b3_ref)
    rows, width = b0_ref.shape
    group = 4 * rows
    heads = width // HEAD
    counts = [counts_ref[i] for i in range(4)]
    sorted_ref[...] = jnp.zeros(sorted_ref.shape, sorted_ref.dtype)
    for index, ref in enumerate(blocks):

        def place(tile, _, index=index, ref=ref):
            to_group(ref[aligned(tile, TILE), :], sorted_ref, tile_moves(counts, rows, index, tile))
            return 0

        lax.fori_loop(0, rows // TILE, place, 0)
    lane = iota((group, 128), 1)
    pick_row, pick_lane = iota((8, 128), 0), iota((8, 128), 1)
    inner_ref[...] = jnp.zeros(inner_ref.shape, f32)
    for pair in range((heads + 1) // 2):
        columns = slice(pair * 128, (pair + 1) * 128)
        grad = sorted_ref[:, columns].astype(f32)
        product = grad * att_ref[:, columns].astype(f32)
        high = product.astype(bf16)
        low = (product - high.astype(f32)).astype(bf16)
        pick = (pick_row == 2 * pair + pick_lane // HEAD).astype(bf16)
        inner_ref[...] += dot(pick, high, NT) + dot(pick, low, NT)
        out_ref[2 * pair] = jnp.where(lane < HEAD, grad, 0.0).astype(bf16)
        if 2 * pair + 1 < heads:
            out_ref[2 * pair + 1] = jnp.where(lane < HEAD, pltpu.roll(grad, HEAD, 1), 0.0).astype(bf16)


def attend_back_kernel(first_head, lse_ref, inner_ref, q_ref, k_ref, v_ref, g_ref, out_ref, dq_ref):
    group = q_ref.shape[1]
    long = 2 * group // 3
    block = 1024
    lane = iota((block, 128), 1)
    head = first_head + pl.program_id(0)
    lse = jnp.sum(jnp.where(iota(lse_ref.shape, 0) == head, lse_ref[...], 0.0), axis=0, keepdims=True)
    inner = jnp.sum(jnp.where(iota(inner_ref.shape, 0) == head, inner_ref[...], 0.0), axis=0, keepdims=True)
    done = set()
    for low, high in ((0, long), (long, group)):
        for keys in range(low, high, block):
            key = k_ref[0, keys : keys + block, :]
            value = v_ref[0, keys : keys + block, :]
            key_grad, value_grad = None, None
            for queries in range(low, high, block):
                query = q_ref[0, queries : queries + block, :]
                grad = g_ref[0, queries : queries + block, :]
                probs = jnp.exp2(dot(key, query, NT) - lse[:, queries : queries + block])
                inside = dot(value, grad, NT) - inner[:, queries : queries + block]
                score_grad = (probs * inside).astype(bf16)
                value_part = dot(probs.astype(bf16), grad, NN)
                key_part = dot(score_grad, query, NN)
                query_part = dot(key, score_grad, TN)
                value_grad = value_part if value_grad is None else value_grad + value_part
                key_grad = key_part if key_grad is None else key_grad + key_part
                place = (slice(None), slice(queries, queries + block))
                dq_ref[place] = query_part if queries not in done else dq_ref[place] + query_part
                done.add(queries)
            out_ref[0, keys : keys + block, 0:128] = pltpu.roll(key_grad * LN2, HEAD, 1).astype(bf16)
            out_ref[0, keys : keys + block, 128:256] = value_grad.astype(bf16)
    wide = iota((group, 128), 1)
    query_grad = dq_ref[...].T * (1.0 / math.sqrt(HEAD))
    pair = jnp.where(wide < HEAD, query_grad, out_ref[0, :, 0:128].astype(f32))
    out_ref[0, :, 0:128] = pair.astype(bf16)


def project_back_kernel(
    counts_ref, h01_ref, h2_ref, weight_ref, local_ref, b0_ref, b1_ref, b2_ref, b3_ref, *acc_refs
):
    refs = [h01_ref.at[i] for i in range(h01_ref.shape[0])] + [h2_ref.at[i] for i in range(h2_ref.shape[0])]
    backs = (b0_ref, b1_ref, b2_ref, b3_ref)
    rows = local_ref.shape[1]
    counts = [counts_ref[i] for i in range(4)]
    pairs = len(refs) * 128
    lane = iota((TILE, 128), 1)
    for index in (3, 1, 2, 0):

        def step(tile, _, index=index):
            here = aligned(tile, TILE)
            from_group(refs, acc_refs, tile_moves(counts, rows, index, tile))
            for head, ref in enumerate(acc_refs):
                local_ref[index, here, head * 128 : (head + 1) * 128] = ref[:, 0:128]
            for pair in range((len(refs) + 1) // 2):
                value = acc_refs[2 * pair][:, 128:256]
                if 2 * pair + 1 < len(refs):
                    other = acc_refs[2 * pair + 1][:, 128:256].astype(f32)
                    value = jnp.where(lane < HEAD, value.astype(f32), pltpu.roll(other, HEAD, 1)).astype(bf16)
                first = pairs + pair * 128
                local_ref[index, here, first : first + 128] = value
            return 0

        lax.fori_loop(0, rows // TILE, step, 0)
        backs[index][...] = dot(local_ref[index], weight_ref[...], NT).astype(bf16)


def project_grad_kernel(first, x0_ref, x1_ref, x2_ref, x3_ref, local_ref, out_ref, sums_ref):
    rows = local_ref.shape[1]
    columns = slice(first, first + out_ref.shape[1])
    total, sums = None, None
    for index, ref in enumerate((x0_ref, x1_ref, x2_ref, x3_ref)):
        value = local_ref[index, :, columns]
        part = dot(ref[0:rows, :], value, TN)
        total = part if total is None else total + part
        one = jnp.sum(value.astype(f32), axis=0, keepdims=True)
        sums = one if sums is None else sums + one
    out_ref[...] = total.astype(bf16)
    sums_ref[...] = jnp.broadcast_to(sums, sums_ref.shape)


def last_kernel(
    tok_ref, frame_ref, lead_ref, table_ref, gain_ref, perm_ref, mine_ref, one_ref, more_ref, rest_ref, xgrad_ref,
    two_ref, upb_ref, qk_ref, v_ref, me_ref, out_ref, sums_ref,
):
    values, hot = rows_with_lead(tok_ref, frame_ref, lead_ref, table_ref)
    unit, inverse = norm_stats(values)
    other = jnp.concatenate([one_ref[...], more_ref[...], rest_ref[...]], axis=0)
    local = (mine_ref[...].astype(f32) + other.astype(f32)).astype(bf16)
    grad = dot(perm_ref[...], local, TN)
    e = grad * row_of(gain_ref)
    mean_e = jnp.mean(e, axis=-1, keepdims=True)
    along = jnp.mean(e * unit, axis=-1, keepdims=True)
    out = xgrad_ref[...] + inverse * (e - mean_e - unit * along)
    out_ref[...] = out
    leads = table_ref.shape[0]
    one = out.astype(bf16)
    rest = out - one.astype(f32)
    two = rest.astype(bf16)
    three = (rest - two.astype(f32)).astype(bf16)
    sums_ref[0:leads, :] = dot(hot, one, NN) + dot(hot, two, NN) + dot(hot, three, NN)
    row = iota((16, grad.shape[1]), 0)
    me = me_ref[0]
    small = jnp.zeros((16, grad.shape[1]), f32)
    small = jnp.where(row == 0, jnp.sum(grad * unit, axis=0, keepdims=True), small)
    small = jnp.where(row == 1, jnp.sum(grad, axis=0, keepdims=True), small)
    for i in range(4):
        small = jnp.where(row == 2 + i, two_ref[i : i + 1, :], small)
        small = jnp.where(row == 6 + (me ^ i), upb_ref[i, 0:1, :], small)
    heads = qk_ref.shape[1] // 128
    bias = [qk_ref[0:1, head * 128 : head * 128 + HEAD] for head in range(heads)]
    bias.append(v_ref[0:1, 0 : heads * HEAD])
    bias.append(jnp.zeros((1, grad.shape[1] - 2 * heads * HEAD), f32))
    small = jnp.where(row == 10 + me, jnp.concatenate(bias, axis=1), small)
    sums_ref[leads : leads + 16, :] = small


def finish_kernel(left_ref, right_ref, me_ref, lead_ref, g1_ref, b1_ref, g2_ref, b2_ref, ob_ref, db_ref, ub_ref, qv_ref):
    total = left_ref[...] + right_ref[...]
    leads = lead_ref.shape[0]
    lead_ref[...] = total[0:leads]
    for place, ref in enumerate((g1_ref, b1_ref, g2_ref, b2_ref, ob_ref, db_ref)):
        ref[...] = total[leads + place].reshape(ref.shape)
    me = me_ref[0]
    up, qv = total[leads + 6 : leads + 7], total[leads + 10 : leads + 11]
    for i in range(1, 4):
        up = jnp.where(me == i, total[leads + 6 + i : leads + 7 + i], up)
        qv = jnp.where(me == i, total[leads + 10 + i : leads + 11 + i], qv)
    ub_ref[...] = up.reshape(ub_ref.shape)
    width = qv_ref.shape[1]
    qv_ref[...] = jnp.concatenate([qv[:, 0:width], qv[:, width : 2 * width]], axis=0)


def bits_of(size):
    bits = []
    step = 1
    while step < size:
        bits.append(step)
        step *= 2
    return bits


def after(value, *others):
    return lax.optimization_barrier((value, *others))[0]


def swap(value, size, bit):
    return lax.ppermute(value, "rows", [(i, i ^ bit) for i in range(size)])


def add_low(left, right):
    return (left.astype(f32) + right.astype(f32)).astype(bf16)


def halves(value, bit, axis=0):
    half = value.shape[axis] // 2
    high = (lax.axis_index("rows") // bit) % 2
    return (
        lax.dynamic_slice_in_dim(value, high * half, half, axis),
        lax.dynamic_slice_in_dim(value, (1 - high) * half, half, axis),
    )


def joined(mine, other, bit, axis=0):
    high = (lax.axis_index("rows") // bit) % 2
    low_part, high_part = jnp.where(high == 1, other, mine), jnp.where(high == 1, mine, other)
    return jnp.concatenate([low_part, high_part], axis)


def on_device(
    rows_size,
    tokens, frame_id, lead_index, lead_embed, ln1_gain, ln1_bias, qkv_weight, qv_bias,
    out_weight, out_bias, ln2_gain, ln2_bias, up_weight, up_bias, down_weight, down_bias, out_grad,
):
    rows, width_all = tokens.shape
    width = qkv_weight.shape[2]
    heads = width // HEAD
    hidden = up_weight.shape[1]
    leads = lead_embed.shape[0]
    group = 4 * rows
    wide = (heads + 1) // 2 * 128
    bits = bits_of(rows_size)
    me = lax.axis_index("tp").reshape(1)
    side = (lax.axis_index("rows") % 2).reshape(1)

    def over(value, ring):
        return lax.ppermute(value, "tp", ring)

    up_rows = jnp.concatenate([up_weight, jnp.broadcast_to(up_bias.reshape(1, hidden), (PAD, hidden))], axis=0)
    out_far = over(out_weight, NEXT)
    mine, perm = call(
        pre_kernel,
        (shape_of((rows + PAD, width_all), bf16), shape_of((rows, rows), bf16)),
        [VMEM, VMEM, SMEM, VMEM, VMEM, VMEM], (VMEM, VMEM), "pre", 5,
    )(tokens, frame_id, lead_index, lead_embed, ln1_gain, ln1_bias)
    mine = after(mine, out_far)
    near = over(mine, CORE)
    far = over(mine, NEXT)

    out_near = over(out_weight, CORE)
    up_near = over(up_rows, CORE)
    down_near = over(down_weight, CORE)
    out_across = over(out_far, CORE)
    ff_rows = jnp.concatenate([up_rows, halves(down_weight, 1)[0]], axis=0)
    weight_qkv = jnp.concatenate([qkv_weight[0], qkv_weight[1], qkv_weight[2]], axis=1)
    zero = jnp.zeros((width,), f32)
    bias_qkv = jnp.concatenate([qv_bias[0].astype(f32), zero, qv_bias[1].astype(f32)]).reshape(1, 3 * width)
    scale_qkv = jnp.concatenate(
        [jnp.full((width,), LOG2E / math.sqrt(HEAD), f32), jnp.ones((2 * width,), f32)]
    ).reshape(1, 3 * width)
    pair_weight = qkv_weight[0:2].reshape(2, width_all, heads, HEAD).transpose(1, 2, 0, 3)
    weight_heads = jnp.concatenate(
        [
            pair_weight.reshape(width_all, heads * 128),
            jnp.pad(qkv_weight[2], ((0, 0), (0, wide - width))),
        ],
        axis=1,
    )
    far, weight_qkv, weight_heads, bias_qkv, scale_qkv, ff_rows, *_ = lax.optimization_barrier(
        (
            far, weight_qkv, weight_heads, bias_qkv, scale_qkv, ff_rows,
            out_near, out_across, up_near, down_near,
        )
    )
    across = over(far, CORE)
    parts = (mine, near, far, across)

    ff_far = over(ff_rows, NEXT)

    att, lse, counts, a0, a1, a2, a3, q_all, k_all, v_all = call(
        attend_kernel,
        (
            shape_of((group, wide), bf16),
            shape_of((8, group), f32),
            shape_of((8,), i32),
        )
        + (shape_of((rows, width), bf16),) * 4
        + (shape_of((heads, group, 128), bf16),) * 3,
        whole_specs(3) + [HBM] * 4, (VMEM, VMEM, SMEM) + (VMEM,) * 4 + (HBM,) * 3, "attend", 40,
        scratch=[
            pltpu.VMEM((4, rows + PAD, width_all), bf16),
            pltpu.VMEM((group, 3 * width), bf16),
            pltpu.VMEM((heads, group, 128), bf16),
            pltpu.VMEM((heads, group, 128), bf16),
            pltpu.VMEM((heads, group, 128), bf16),
            pltpu.VMEM((2, 2 * group // 3, 512), f32),
            pltpu.SemaphoreType.DMA((4,)),
            pltpu.SemaphoreType.DMA((3,)),
        ],
    )(weight_qkv, bias_qkv, scale_qkv, *parts)

    got = [a0, over(a1, CORE), over(a2, NEXT), over(a3, DIAG)]
    ff_far = after(ff_far, counts)
    down_side = swap(ff_far[up_rows.shape[0] :], rows_size, 1)
    ff_across = over(after(ff_far, got[1]), CORE)
    down_side, *got[2:] = lax.optimization_barrier((down_side, *got[2:]))
    down_side_across = over(down_side, CORE)

    layer_out, xgrad, agrad, normed_two, attu, s0, s1, s2, s3, sums_two, up_b, act, hid = call(
        middle_kernel,
        (
            shape_of((rows, width_all), bf16),
            shape_of((rows, width_all), f32),
            shape_of((rows, width_all), bf16),
            shape_of((rows, width_all), bf16),
            shape_of((4, rows, width), bf16),
        )
        + (shape_of((rows, width), bf16),) * 4
        + (
            shape_of((8, width_all), f32),
            shape_of((4, 8, hidden), f32),
            shape_of((4, rows, hidden), bf16),
            shape_of((4, rows, hidden), bf16),
        ),
        [VMEM, VMEM, SMEM] + whole_specs(15) + [SMEM] + [HBM] * 8, (VMEM,) * 11 + (HBM,) * 2, "middle", 32,
        scratch=[
            pltpu.VMEM((rows, width_all), f32),
            pltpu.VMEM((rows, width_all), f32),
            pltpu.VMEM((4, width_all + PAD, hidden), bf16),
            pltpu.VMEM((4, hidden, width_all), bf16),
            pltpu.VMEM((4, rows, hidden), bf16),
            pltpu.VMEM((4, rows, hidden), bf16),
            pltpu.SemaphoreType.DMA((10,)),
            pltpu.SemaphoreType.DMA((8,)),
        ],
    )(
        tokens, frame_id, lead_index, lead_embed, perm, *got, out_weight, out_near, out_far, out_across,
        ln2_gain, ln2_bias, out_bias, down_bias, out_grad, side,
        up_rows, up_near, ff_far, ff_across, down_weight, down_near, down_side, down_side_across,
    )

    got_grad = [s0, over(s1, CORE), over(s2, NEXT), over(s3, DIAG)]

    def block_of(step):
        return jnp.where(step < 2, 2 * step + 1, 2 * step - 4)

    def full(shape):
        return pl.BlockSpec(shape, lambda s: (0,) * len(shape))

    def picked(shape):
        return pl.BlockSpec((1,) + shape, lambda s: (block_of(s), 0, 0))

    tall = width_all + width + hidden
    send, keep = call(
        weight_grad_kernel,
        (shape_of((2, tall, width_all), bf16),) * 2,
        [full((rows, width_all))] * 3 + [picked((rows, hidden))] * 2 + [picked((rows, width))],
        (
            pl.BlockSpec((1, tall, width_all), lambda s: (jnp.minimum(s, 1), 0, 0)),
            pl.BlockSpec((1, tall, width_all), lambda s: (jnp.maximum(s - 2, 0), 0, 0)),
        ),
        "weight_grad", 18, grid=(4,),
    )(normed_two, out_grad, agrad, act, hid, attu)
    *got_grad[1:], send, keep = lax.optimization_barrier((*got_grad[1:], send, keep))

    from_core = over(send, CORE)
    grad_all, inner = call(
        gather_grad_kernel,
        (shape_of((heads, group, 128), bf16), shape_of((8, group), f32)),
        [SMEM] + whole_specs(5), (VMEM, VMEM), "gather_grad", 6,
        scratch=[pltpu.VMEM((group, wide), bf16)],
    )(after(counts, send), *got_grad, att)

    cut = width_all + width
    from_core = after(from_core, inner)
    down_mine = add_low(keep[0, cut:], from_core[0, cut:])
    down_other = add_low(keep[1, cut:], from_core[1, cut:])
    up_keep, up_give = halves(keep[:, :cut], 1, 1)
    up_keep_two, up_give_two = halves(from_core[:, :cut], 1, 1)
    up_mine, up_away = add_low(up_keep, up_keep_two), add_low(up_give, up_give_two)
    down_y = over(down_other, NEXT)
    up_x = swap(up_away, rows_size, 1)

    def attend_back(first, count, grads):
        spec = pl.BlockSpec((1, group, 128), lambda s: (first + s, 0, 0))
        return call(
            functools.partial(attend_back_kernel, first),
            shape_of((count, group, 256), bf16),
            [full((8, group))] * 2 + [spec] * 4,
            pl.BlockSpec((1, group, 256), lambda s: (s, 0, 0)), "attend_back", 15 * count,
            scratch=[pltpu.VMEM((128, group), f32)], grid=(count,),
        )(lse, inner, q_all, k_all, v_all, grads)

    back_01 = attend_back(0, heads - 1, after(grad_all, down_other, up_away, down_mine, up_mine))
    down_y, up_x = after(down_y, back_01), after(up_x, back_01)
    (down_keep, down_give), (down_keep_two, down_give_two) = halves(down_mine, 1), halves(down_y, 1)
    down_half_sum, down_away = add_low(down_keep, down_keep_two), add_low(down_give, down_give_two)
    up_half_sum = add_low(up_mine[0], up_x[0])
    up_other = add_low(up_mine[1], up_x[1])
    down_x = swap(down_away, rows_size, 1)
    up_y = over(up_other, NEXT)
    back_2 = attend_back(heads - 1, 1, after(grad_all, back_01, down_away, up_other, up_half_sum, down_half_sum))
    steps = bits[1:]
    down_x, up_y = after(down_x, back_2), after(up_y, back_2)

    def both(pick):
        return jnp.concatenate(
            [
                add_low(halves(down_half_sum, steps[0])[pick], halves(down_x, steps[0])[pick]),
                add_low(halves(up_half_sum, steps[0])[pick], halves(up_y, steps[0])[pick]),
            ],
            axis=0,
        )

    mixed, away = both(0), both(1)
    arrived = swap(away, rows_size, steps[0])

    local, b0, b1, b2, b3 = call(
        project_back_kernel,
        (shape_of((4, rows, heads * 128 + wide), bf16),) + (shape_of((rows, width_all), bf16),) * 4,
        [SMEM] + whole_specs(3), (VMEM,) * 5, "project_back", 12,
        scratch=[pltpu.VMEM((TILE, 256), bf16)] * heads,
    )(after(counts, away, mixed), back_01, back_2, weight_heads)

    arrived, b3, b1 = lax.optimization_barrier((arrived, b3, b1))
    over_far = over(b3, CORE)
    over_near = over(b1, CORE)
    back_far = add_low(b2, over_far)
    here = add_low(b0, over_near)
    (keep_z, give_z), (keep_z_two, give_z_two) = halves(mixed, steps[1]), halves(arrived, steps[1])
    mixed, away = add_low(keep_z, keep_z_two), add_low(give_z, give_z_two)
    arrived = swap(away, rows_size, steps[1])
    third = rows // 3
    far_one = over(back_far[:third], NEXT)

    def project_grad(first, count, local):
        return call(
            functools.partial(project_grad_kernel, first),
            (shape_of((width_all, count), bf16), shape_of((8, count), f32)),
            whole_specs(5), (VMEM, VMEM), "project_grad", 4,
        )(*parts, local)

    qk_grad, qk_sums = project_grad(0, heads * 128, after(local, back_far, away, mixed, here))
    far_one, arrived = after(far_one, qk_grad), after(arrived, qk_grad)
    far_two = over(after(back_far[third : 2 * third], far_one), NEXT)
    mixed = add_low(mixed, arrived)
    for bit in steps[2:]:
        mixed, away = halves(mixed, bit)
        mixed = add_low(mixed, swap(away, rows_size, bit))
    for bit in reversed(steps[2:]):
        mixed = joined(mixed, swap(mixed, rows_size, bit), bit)
    arrived = swap(mixed, rows_size, steps[1])
    v_grad, v_sums = project_grad(heads * 128, wide, after(local, mixed, far_one))
    far_two, arrived = after(far_two, v_grad), after(arrived, v_grad)
    far_three = over(after(back_far[2 * third :], far_two), NEXT)
    mixed = joined(mixed, arrived, steps[1])
    split = down_half_sum.shape[0] // 2
    down_part, up_part = mixed[0:split], mixed[split:]
    down_got, up_got = swap(down_part, rows_size, steps[0]), swap(up_part, rows_size, 1)
    keep_q, away_q = halves(jnp.concatenate([qk_grad, v_grad], axis=1), bits[0])
    arrived_q = swap(after(away_q, far_two), rows_size, bits[0])
    far_three, arrived_q = lax.optimization_barrier((far_three, arrived_q))
    qkv_sum = add_low(keep_q, arrived_q)

    tokens_grad, small = call(
        last_kernel,
        (shape_of((rows, width_all), f32), shape_of((leads + 16, width_all), f32)),
        [VMEM, VMEM, SMEM] + whole_specs(12) + [SMEM], (VMEM, VMEM), "last", 7,
    )(
        tokens, frame_id, lead_index, lead_embed, ln1_gain, perm, here, far_one, far_two, far_three, xgrad,
        sums_two, up_b, qk_sums, v_sums, me,
    )

    down_got, up_got = after(down_got, small), after(up_got, small)
    down_part = joined(down_part, down_got, steps[0])
    up_part = joined(up_part[None], up_got[None], 1)
    down_sum = joined(down_part, swap(down_part, rows_size, 1), 1).astype(f32)
    up_sum = joined(up_part, swap(up_part, rows_size, steps[0]), steps[0], 1).astype(f32)
    up_sum = up_sum.reshape(cut, width_all)

    for bit in bits[1:]:
        (keep_q, away) = halves(qkv_sum, bit)
        qkv_sum = add_low(keep_q, swap(away, rows_size, bit))
    for bit in reversed(bits):
        qkv_sum = joined(qkv_sum, swap(qkv_sum, rows_size, bit), bit)

    for pairs in (CORE, NEXT):
        small = small + over(small, pairs)
    for bit in bits[:-1]:
        small = small + swap(small, rows_size, bit)
    vector = shape_of((width_all,), f32)
    lead_sum, g1, b1, g2, b2, out_b, down_b, up_b_sum, qv_sum = call(
        finish_kernel,
        (shape_of((leads, width_all), f32),) + (vector,) * 6 + (shape_of((hidden,), f32), shape_of((2, width), f32)),
        [VMEM, VMEM, SMEM], (VMEM,) * 9, "finish", 1,
    )(small, swap(small, rows_size, bits[-1]), me)

    pairs_sum = qkv_sum[:, 0 : heads * 128].reshape(width_all, heads, 2, HEAD).transpose(2, 0, 1, 3)
    qkv_out = jnp.concatenate(
        [
            pairs_sum.reshape(2, width_all, width),
            qkv_sum[:, heads * 128 : heads * 128 + width].reshape(1, width_all, width),
        ],
        axis=0,
    ).astype(f32)
    return (
        layer_out, tokens_grad, lead_sum, g1, b1, qkv_out, qv_sum, up_sum[width_all:], out_b, g2, b2,
        up_sum[0:width_all], up_b_sum, down_sum, down_b,
    )


def solution(mesh):
    rows_size = mesh.shape["rows"]
    split = P(("rows", "tp"), None)
    placed = (
        split, P(("rows", "tp")), P("rows"), P(), P(), P(), P(None, None, "tp"), P(None, "tp"),
        P("tp", None), P(), P(), P(), P(None, "tp"), P("tp"), P("tp", None), P(), split,
    )
    return jax.shard_map(
        functools.partial(on_device, rows_size),
        mesh=mesh,
        in_specs=placed,
        out_specs=(
            split, split, P(), P(), P(), P(None, None, "tp"), P(None, "tp"), P("tp", None), P(), P(), P(),
            P(None, "tp"), P("tp"), P("tp", None), P(),
        ),
        check_vma=False,
    )
```

```python
import functools
import math

import jax
import jax.numpy as jnp
from jax import lax
from jax.experimental import pallas as pl
from jax.experimental.pallas import tpu as pltpu
from jax.sharding import PartitionSpec as P

HEAD = 64
EPS = 1e-05
LOG2E = math.log2(math.e)
LN2 = math.log(2.0)
TILE = 256
PAD = 16
VMEM_LIMIT = 60 * 1024 * 1024

f32 = jnp.float32
bf16 = jnp.bfloat16
i32 = jnp.int32

CORE = ((0, 1), (1, 0), (2, 3), (3, 2))
NEXT = ((0, 2), (2, 0), (1, 3), (3, 1))
DIAG = ((0, 3), (3, 0), (1, 2), (2, 1))

LIMITS = {
    "pre": 60, "project": 60, "attend": 48, "middle": 60, "weight_grad": 60, "gather_grad": 24, "attend_back": 48,
    "project_back": 32, "project_grad": 60, "last": 32, "finish": 8,
}


def iota(shape, axis):
    return lax.broadcasted_iota(i32, shape, axis)


def dot(left, right, dims):
    return lax.dot_general(left, right, (dims, ((), ())), preferred_element_type=f32)


NN = ((1,), (0,))
NT = ((1,), (1,))
TN = ((0,), (0,))


def shape_of(shape, dtype):
    return jax.ShapeDtypeStruct(shape, dtype)


def whole_specs(count):
    return [pl.BlockSpec(memory_space=pltpu.VMEM)] * count


SMEM = pl.BlockSpec(memory_space=pltpu.SMEM)
VMEM = pl.BlockSpec(memory_space=pltpu.VMEM)
HBM = pl.BlockSpec(memory_space=pl.ANY)


def call(body, out_shape, in_specs, out_specs, name, micros, scratch=(), grid=()):
    return pl.pallas_call(
        body,
        out_shape=out_shape,
        grid=grid,
        in_specs=in_specs,
        out_specs=out_specs,
        scratch_shapes=scratch,
        compiler_params=pltpu.CompilerParams(vmem_limit_bytes=LIMITS[name] * 1024 * 1024),
        name=name,
        cost_estimate=pl.CostEstimate(
            flops=int(micros * 1.15e9), bytes_accessed=1024, transcendentals=0
        ),
    )


def local_frame(frame_ref):
    return frame_ref[...].reshape(1, frame_ref.shape[0]) % 2


def row_of(ref):
    return ref[...].astype(f32).reshape(1, ref.shape[0])


def rows_with_lead(tok_ref, frame_ref, lead_ref, table_ref):
    frame = local_frame(frame_ref)
    lead = jnp.where(frame == 0, lead_ref[0], lead_ref[1])
    hot = (iota((table_ref.shape[0], frame.shape[1]), 0) == lead).astype(bf16)
    return tok_ref[...].astype(f32) + dot(hot, table_ref[...], TN), hot


def norm_stats(values):
    average = jnp.mean(values, axis=-1, keepdims=True)
    centred = values - average
    spread = jnp.mean(centred * centred, axis=-1, keepdims=True)
    inverse = lax.rsqrt(spread + EPS)
    return centred * inverse, inverse


def pre_kernel(tok_ref, frame_ref, lead_ref, table_ref, gain_ref, shift_ref, up_bias_ref, out_ref, perm_ref):
    rows = tok_ref.shape[0]
    values, _ = rows_with_lead(tok_ref, frame_ref, lead_ref, table_ref)
    unit, _ = norm_stats(values)
    normed = (unit * row_of(gain_ref) + row_of(shift_ref)).astype(bf16)
    first = (local_frame(frame_ref) == 0).astype(f32)
    before = (iota((rows, rows), 0) < iota((rows, rows), 1)).astype(bf16)
    earlier = dot(jnp.broadcast_to(first, (8, rows)).astype(bf16), before, NN)[0:1]
    count = jnp.sum(first, axis=1, keepdims=True)
    place = jnp.where(first > 0, earlier, count + iota((1, rows), 1).astype(f32) - earlier)
    perm = (iota((rows, rows), 0) == place.astype(i32)).astype(bf16)
    perm_ref[...] = perm
    out_ref[0:rows, :] = dot(perm, normed, NN).astype(bf16)
    high = jnp.floor(count * (1.0 / 16))
    low = count - 16 * high
    tail = iota((PAD, out_ref.shape[1]), 0)
    out_ref[rows : rows + PAD, :] = jnp.where(
        tail == 0, high, jnp.where(tail == 1, low, jnp.where(tail == 2, row_of(up_bias_ref), 0.0))
    ).astype(bf16)


def read_count(block_ref, rows):
    part = block_ref[rows : rows + PAD, 0:128].astype(f32)
    place, lane = iota(part.shape, 0), iota(part.shape, 1)
    worth = jnp.where(place == 0, 16.0, jnp.where(place == 1, 1.0, 0.0))
    return jnp.sum(jnp.where(lane == 0, part * worth, 0.0)).astype(i32)


def tile_moves(counts, rows, block, tile):
    group = 4 * rows
    count = counts[block]
    longs_before = sum(counts[:block], jnp.int32(0))
    limit = jnp.clip(count - tile * TILE, 0, TILE)
    moves = []
    for some, base, low, high in (
        (limit > 0, longs_before + tile * TILE, 0, limit),
        (limit < TILE, 2 * group // 3 + block * rows - longs_before - count + tile * TILE, limit, TILE),
    ):
        spot = jnp.minimum(base // TILE, group // TILE - 2)
        window = pl.ds(pl.multiple_of(spot * TILE, TILE), 2 * TILE)
        moves.append((some, window, base - spot * TILE, low, high))
    return moves


def aligned(index, size):
    return pl.ds(pl.multiple_of(index * size, size), size)


def to_group(value, dst_ref, moves):
    width = value.shape[1]
    for some, window, shift, low, high in moves:

        @pl.when(some)
        def _():
            dest, source = iota((2 * TILE, TILE), 0), iota((2 * TILE, TILE), 1)
            hot = (dest - source == shift) & (source >= low) & (source < high)
            moved = dot(hot.astype(bf16), value, NN).astype(bf16)
            dst_ref[window, 0:width] = dst_ref[window, 0:width] + moved


def from_group(src_refs, acc_refs, moves):
    (some_long, *long), (some_short, *short) = moves

    def moved(window, shift, low, high):
        source, dest = iota((TILE, 2 * TILE), 0), iota((TILE, 2 * TILE), 1)
        hot = ((dest - source == shift) & (source >= low) & (source < high)).astype(bf16)
        return [dot(hot, ref[window, :], NN).astype(bf16) for ref in src_refs]

    @pl.when(some_long)
    def _():
        for ref, value in zip(acc_refs, moved(*long)):
            ref[...] = value

    @pl.when(jnp.logical_not(some_long))
    def _():
        for ref, value in zip(acc_refs, moved(*short)):
            ref[...] = value

    @pl.when(some_long & some_short)
    def _():
        for ref, value in zip(acc_refs, moved(*short)):
            ref[...] = ref[...] + value


def pack_heads(src_ref, out_ref):
    rows = src_ref.shape[0]
    half = rows // 2
    lane = iota((half, 128), 1)
    out_ref[0:rows, :] = src_ref[:, 0:128]
    upper = src_ref[0:half, 128:256].astype(f32)
    lower = pltpu.roll(src_ref[half:rows, 128:256].astype(f32), HEAD, 1)
    out_ref[rows:, :] = jnp.where(lane < HEAD, upper, lower).astype(bf16)


def unpack_heads(src_ref, out_ref):
    rows = out_ref.shape[0]
    half = rows // 2
    lane = iota((half, 128), 1)
    out_ref[:, 0:128] = src_ref[0:rows, :]
    both = src_ref[rows:, :].astype(f32)
    out_ref[0:half, 128:256] = jnp.where(lane < HEAD, both, 0.0).astype(bf16)
    out_ref[half:rows, 128:256] = jnp.where(lane < HEAD, pltpu.roll(both, HEAD, 1), 0.0).astype(bf16)


def head_columns(ref, start, width):
    first = start // 128 * 128
    if first + 128 <= width:
        piece = ref[:, first : first + 128].astype(f32)
    else:
        piece = jnp.concatenate([ref[:, first : first + HEAD].astype(f32)] * 2, axis=1)
    return pltpu.roll(piece, HEAD, 1) if start != first else piece


def project_rows(x_ref, index, counts, weight_ref, bias_ref, value_ref, qkv_ref):
    rows = value_ref.shape[0]
    width = weight_ref.shape[2]
    for part in range(3):
        value = dot(x_ref[0:rows, :], weight_ref[part], NN)
        if part == 0:
            value = (value + bias_ref[0:1, :].astype(f32)) * (LOG2E / math.sqrt(HEAD))
        if part == 2:
            value = value + bias_ref[1:2, :].astype(f32)
        value_ref[:, part * width : (part + 1) * width] = value.astype(bf16)

    def place(tile, _):
        to_group(value_ref[aligned(tile, TILE), :], qkv_ref, tile_moves(counts, rows, index, tile))
        return 0

    lax.fori_loop(0, rows // TILE, place, 0)


def project_kernel(weight_ref, bias_ref, x0_ref, x1_ref, qkv_ref, counts_ref, value_ref):
    qkv_ref[...] = jnp.zeros(qkv_ref.shape, qkv_ref.dtype)
    counts = []
    for index, ref in enumerate((x0_ref, x1_ref)):
        counts.append(read_count(ref, value_ref.shape[0]))
        counts_ref[index] = counts[index]
        project_rows(ref, index, counts, weight_ref, bias_ref, value_ref, qkv_ref)


def attend_kernel(
    weight_ref, bias_ref, early_ref, part_ref, x2_ref, x3_ref,
    att_ref, lse_ref, counts_ref, a0_ref, a1_ref, a2_ref, a3_ref, q_out, k_out, v_out,
    x_buf, qkv_ref, value_ref, q_ref, k_ref, v_ref, scores_ref, load_sems, store_sems,
):
    rows = x2_ref.shape[0] - PAD
    group = 4 * rows
    long = 2 * group // 3
    width = weight_ref.shape[2]
    heads = width // HEAD
    loads = [
        pltpu.make_async_copy(source, target, load_sems.at[i])
        for i, (source, target) in enumerate(
            ((part_ref, qkv_ref), (x2_ref, x_buf.at[0]), (x3_ref, x_buf.at[1]))
        )
    ]
    for load in loads:
        load.start()
    loads[0].wait()
    counts = [early_ref[0], early_ref[1]]
    for index in (2, 3):
        loads[index - 1].wait()
        block_ref = x_buf.at[index - 2]
        counts.append(read_count(block_ref, rows))
        project_rows(block_ref, index, counts, weight_ref, bias_ref, value_ref, qkv_ref)
    for index, count in enumerate(counts):
        counts_ref[index] = count
    lane = iota((group, 128), 1)
    stores = []
    for part, ref, out, fill in ((1, k_ref, k_out, 0.0), (2, v_ref, v_out, 1.0), (0, q_ref, q_out, 0.0)):
        for head in range(heads):
            piece = head_columns(qkv_ref, part * width + head * HEAD, 3 * width)
            ref[head] = jnp.where(lane < HEAD, piece, fill).astype(bf16)
        store = pltpu.make_async_copy(ref, out, store_sems.at[part])
        store.start()
        stores.append(store)

    block = 512
    row = iota((128, block), 0)
    half = iota((block, 128), 1)
    tasks = [
        (head, first, low, high)
        for low, high in ((0, long), (long, group))
        for first in range(low, high, block)
        for head in range(heads)
    ]

    def scores(task, part):
        head, first, low, high = tasks[task]
        keys = slice(low + part * block, low + (part + 1) * block)
        value = dot(k_ref[head, keys, :], q_ref[head, first : first + block, :], NT)
        scores_ref[task % 2, part * block : (part + 1) * block, :] = value
        return jnp.max(value.reshape(block // 8, 8, block), axis=0)

    def parts_of(task):
        return (tasks[task][3] - tasks[task][2]) // block if task < len(tasks) else 0

    largest = functools.reduce(jnp.maximum, [scores(0, part) for part in range(parts_of(0))])
    outs = []
    for task, (head, first, low, high) in enumerate(tasks):
        top = jnp.max(largest, axis=0, keepdims=True)
        following, mixed = [], None
        for part in range(max(parts_of(task), parts_of(task + 1))):
            if part < parts_of(task + 1):
                following.append(scores(task + 1, part))
            if part < parts_of(task):
                raised = jnp.exp2(scores_ref[task % 2, part * block : (part + 1) * block, :] - top)
                keys = slice(low + part * block, low + (part + 1) * block)
                value = dot(v_ref[head, keys, :], raised.astype(bf16), TN)
                mixed = value if mixed is None else mixed + value
        if following:
            largest = functools.reduce(jnp.maximum, following)
        totals = mixed[HEAD : HEAD + 1, :]
        lse_ref[head : head + 1, first : first + block] = top + jnp.log2(totals)
        outs.append(jnp.where(row < HEAD, mixed / totals, 0.0))
        if head == heads - 1:
            for pair in range((heads + 1) // 2):
                value = outs[2 * pair].T
                if 2 * pair + 1 < heads:
                    value = value + pltpu.roll(outs[2 * pair + 1].T, HEAD, 1)
                att_ref[first : first + block, pair * 128 : (pair + 1) * 128] = value.astype(bf16)
            outs = []
    for index, out in enumerate((a0_ref, a1_ref, a2_ref, a3_ref)):

        def hand_back(tile, _, index=index):
            moves = tile_moves(counts, rows, index, tile)
            from_group((att_ref,), (qkv_ref.at[aligned(tile, TILE), 0 : att_ref.shape[1]],), moves)
            return 0

        lax.fori_loop(0, rows // TILE, hand_back, 0)
        pack_heads(qkv_ref.at[0:rows, 0 : att_ref.shape[1]], out)
    for store in stores:
        store.wait()


def middle_kernel(
    tok_ref, frame_ref, lead_ref, table_ref, perm_ref,
    at0_ref, at1_ref, at2_ref, at3_ref,
    wo0_ref, wo1_ref, wo2_ref, wo3_ref,
    gain_ref, shift_ref, out_bias_ref, down_bias_ref, og_ref, side_ref,
    x0_ref, x1_ref, x2_ref, x3_ref, up0_ref, up1_ref, up2_ref, up3_ref,
    dn0_ref, dn1_ref, dn2_ref, dn3_ref, dx2_ref, dx3_ref,
    layer_ref, xgrad_ref, agrad_ref, normed_ref, attu_ref, s0_ref, s1_ref, s2_ref, s3_ref, sums_ref, upb_ref,
    act_out, hid_out,
    y_ref, back_ref, at_ref, bias_buf, up_buf, dn_buf, act_ref, hid_ref, load_sems, store_sems,
):
    ats = (at0_ref, at1_ref, at2_ref, at3_ref)
    wos = (wo0_ref, wo1_ref, wo2_ref, wo3_ref)
    ups = (up0_ref, up1_ref, up2_ref, up3_ref)
    blocks = (x0_ref, x1_ref, x2_ref, x3_ref)
    sends = (s0_ref, s1_ref, s2_ref, s3_ref)
    rows, wide = tok_ref.shape
    hidden = act_ref.shape[2]
    half = hidden // 2
    side = side_ref[0]
    mine = pl.ds(pl.multiple_of(side * half, half), half)
    other = pl.ds(pl.multiple_of((1 - side) * half, half), half)
    loads = [[pltpu.make_async_copy(ups[i], up_buf.at[i], load_sems.at[i])] for i in range(4)]
    for index, ref, target, sem in (
        (0, dn0_ref, dn_buf.at[0], 4),
        (1, dn1_ref, dn_buf.at[1], 5),
        (2, dn2_ref, dn_buf.at[2, mine], 6),
        (2, dx2_ref, dn_buf.at[2, other], 7),
        (3, dn3_ref, dn_buf.at[3, mine], 8),
        (3, dx3_ref, dn_buf.at[3, other], 9),
    ):
        loads[index].append(pltpu.make_async_copy(ref, target, load_sems.at[sem]))
    for index in range(4):
        tail = blocks[index].at[rows : rows + PAD]
        loads[index].append(pltpu.make_async_copy(tail, bias_buf.at[index], load_sems.at[10 + index]))
    for load in sum(loads, []):
        load.start()
    gain = row_of(gain_ref)
    values, _ = rows_with_lead(tok_ref, frame_ref, lead_ref, table_ref)
    perm = perm_ref[...]
    x_one = values + row_of(out_bias_ref)
    for index in range(4):
        unpack_heads(ats[index], at_ref)
        mine = dot(perm, at_ref[...], TN).astype(bf16)[:, 0 : wos[index].shape[0]]
        attu_ref[index] = mine
        x_one = x_one + dot(mine, wos[index][...], NN)
    unit, inverse = norm_stats(x_one)
    normed_ref[...] = (unit * gain + row_of(shift_ref)).astype(bf16)
    y_ref[...] = x_one + row_of(down_bias_ref)
    back_ref[...] = jnp.zeros(back_ref.shape, f32)
    stores = []
    for index in range(4):
        for load in loads[index]:
            load.wait()
        up = up_buf[index]
        down = dn_buf[index]
        h = dot(normed_ref[...], up, NN) + bias_buf[index][2:3].astype(f32)
        g = dot(og_ref[...], down, NT)
        c = math.sqrt(2.0 / math.pi)
        h2 = h * h
        t = jnp.tanh(h * (c + (c * 0.044715) * h2))
        half = 0.5 + 0.5 * t
        act = h * half
        slope = half + act * (1.0 - t) * (c + (3 * c * 0.044715) * h2)
        hid = (slope * g).astype(bf16)
        actb = act.astype(bf16)
        act_ref[index] = actb
        hid_ref[index] = hid
        upb_ref[index] = jnp.broadcast_to(jnp.sum(hid.astype(f32), axis=0, keepdims=True), (8, hidden))
        y_ref[...] += dot(actb, down, NN)
        back_ref[...] += dot(hid, up, NT)
        for source, target, sem in ((act_ref, act_out, 0), (hid_ref, hid_out, 4)):
            store = pltpu.make_async_copy(source.at[index], target.at[index], store_sems.at[sem + index])
            store.start()
            stores.append(store)
    layer_ref[...] = y_ref[...].astype(bf16)
    grad = back_ref[...]
    e = grad * gain
    spread_mean = jnp.mean(e, axis=-1, keepdims=True)
    along = jnp.mean(e * unit, axis=-1, keepdims=True)
    og = og_ref[...].astype(f32)
    xgrad = og + inverse * (e - spread_mean - unit * along)
    xgrad_ref[...] = xgrad
    agrad = xgrad.astype(bf16)
    agrad_ref[...] = agrad
    for index in range(4):
        back = dot(agrad, wos[index][...], NT).astype(bf16)
        at_ref[:, 0 : back.shape[1]] = dot(perm, back, NN).astype(bf16)
        pack_heads(at_ref, sends[index])
    sums_ref[...] = jnp.concatenate(
        [
            jnp.sum(grad * unit, axis=0, keepdims=True),
            jnp.sum(grad, axis=0, keepdims=True),
            jnp.sum(agrad.astype(f32), axis=0, keepdims=True),
            jnp.sum(og, axis=0, keepdims=True),
            jnp.zeros((4, og.shape[1]), f32),
        ],
        axis=0,
    )
    for store in stores:
        store.wait()


def weight_grad_kernel(
    normed_ref, og_ref, agrad_ref, act_ref, hid_ref, attu_ref, up_send_ref, up_keep_ref, down_send_ref, down_keep_ref,
    turned_ref,
):
    @pl.when(pl.program_id(0) == 0)
    def _():
        turned_ref[...] = normed_ref[...].T

    up = dot(turned_ref[...], hid_ref[0], NN).astype(bf16)
    out = dot(attu_ref[0], agrad_ref[...], TN).astype(bf16)
    down = dot(act_ref[0], og_ref[...], TN).astype(bf16)
    rows = up.shape[0]
    step = pl.program_id(0)
    for chosen, up_ref, down_ref in (
        (step < 2, up_send_ref, down_send_ref), (step >= 2, up_keep_ref, down_keep_ref),
    ):

        @pl.when(chosen)
        def _(up_ref=up_ref, down_ref=down_ref):
            up_ref[0, 0:rows, :] = up
            up_ref[0, rows:, :] = out
            down_ref[0] = down


def gather_grad_kernel(counts_ref, b0_ref, b1_ref, b2_ref, b3_ref, att_ref, out_ref, inner_ref, sorted_ref, block_ref):
    blocks = (b0_ref, b1_ref, b2_ref, b3_ref)
    rows = block_ref.shape[0]
    group = 4 * rows
    heads = out_ref.shape[0]
    counts = [counts_ref[i] for i in range(4)]
    sorted_ref[...] = jnp.zeros(sorted_ref.shape, sorted_ref.dtype)
    for index, ref in enumerate(blocks):

        unpack_heads(ref, block_ref)

        def place(tile, _, index=index):
            to_group(block_ref[aligned(tile, TILE), :], sorted_ref, tile_moves(counts, rows, index, tile))
            return 0

        lax.fori_loop(0, rows // TILE, place, 0)
    lane = iota((group, 128), 1)
    pick_row, pick_lane = iota((8, 128), 0), iota((8, 128), 1)
    inner_ref[...] = jnp.zeros(inner_ref.shape, f32)
    for pair in range((heads + 1) // 2):
        columns = slice(pair * 128, (pair + 1) * 128)
        grad = sorted_ref[:, columns].astype(f32)
        product = grad * att_ref[:, columns].astype(f32)
        high = product.astype(bf16)
        low = (product - high.astype(f32)).astype(bf16)
        pick = (pick_row == 2 * pair + pick_lane // HEAD).astype(bf16)
        inner_ref[...] += dot(pick, high, NT) + dot(pick, low, NT)
        out_ref[2 * pair] = jnp.where(lane < HEAD, grad, 0.0).astype(bf16)
        if 2 * pair + 1 < heads:
            out_ref[2 * pair + 1] = jnp.where(lane < HEAD, pltpu.roll(grad, HEAD, 1), 0.0).astype(bf16)


def attend_back_kernel(first_head, lse_ref, inner_ref, q_ref, k_ref, v_ref, g_ref, out_ref, dq_ref):
    group = q_ref.shape[1]
    long = 2 * group // 3
    block = 1024
    lane = iota((block, 128), 1)
    head = first_head + pl.program_id(0)
    lse = jnp.sum(jnp.where(iota(lse_ref.shape, 0) == head, lse_ref[...], 0.0), axis=0, keepdims=True)
    inner = jnp.sum(jnp.where(iota(inner_ref.shape, 0) == head, inner_ref[...], 0.0), axis=0, keepdims=True)
    done = set()
    for low, high in ((0, long), (long, group)):
        for keys in range(low, high, block):
            key = k_ref[0, keys : keys + block, :]
            value = v_ref[0, keys : keys + block, :]
            key_grad, value_grad = None, None
            for queries in range(low, high, block):
                query = q_ref[0, queries : queries + block, :]
                grad = g_ref[0, queries : queries + block, :]
                probs = jnp.exp2(dot(key, query, NT) - lse[:, queries : queries + block])
                inside = dot(value, grad, NT) - inner[:, queries : queries + block]
                score_grad = (probs * inside).astype(bf16)
                value_part = dot(probs.astype(bf16), grad, NN)
                key_part = dot(score_grad, query, NN)
                query_part = dot(key, score_grad, TN)
                value_grad = value_part if value_grad is None else value_grad + value_part
                key_grad = key_part if key_grad is None else key_grad + key_part
                place = (slice(None), slice(queries, queries + block))
                dq_ref[place] = query_part if queries not in done else dq_ref[place] + query_part
                done.add(queries)
            out_ref[0, keys : keys + block, 0:128] = pltpu.roll(key_grad * LN2, HEAD, 1).astype(bf16)
            out_ref[0, keys : keys + block, 128:256] = value_grad.astype(bf16)
    wide = iota((group, 128), 1)
    query_grad = dq_ref[...].T * (1.0 / math.sqrt(HEAD))
    pair = jnp.where(wide < HEAD, query_grad, out_ref[0, :, 0:128].astype(f32))
    out_ref[0, :, 0:128] = pair.astype(bf16)


def project_back_kernel(chosen, counts_ref, h01_ref, h2_ref, weight_ref, local_ref, one_ref, two_ref, *acc_refs):
    refs = [h01_ref.at[i] for i in range(h01_ref.shape[0])] + [h2_ref.at[i] for i in range(h2_ref.shape[0])]
    rows = local_ref.shape[1]
    counts = [counts_ref[i] for i in range(4)]
    pairs = len(refs) * 128
    lane = iota((TILE, 128), 1)
    for slot, (index, back_ref) in enumerate(zip(chosen, (one_ref, two_ref))):

        def step(tile, _, index=index, slot=slot):
            here = aligned(tile, TILE)
            from_group(refs, acc_refs, tile_moves(counts, rows, index, tile))
            for head, ref in enumerate(acc_refs):
                local_ref[slot, here, head * 128 : (head + 1) * 128] = ref[:, 0:128]
            for pair in range((len(refs) + 1) // 2):
                value = acc_refs[2 * pair][:, 128:256]
                if 2 * pair + 1 < len(refs):
                    other = acc_refs[2 * pair + 1][:, 128:256].astype(f32)
                    value = jnp.where(lane < HEAD, value.astype(f32), pltpu.roll(other, HEAD, 1)).astype(bf16)
                first = pairs + pair * 128
                local_ref[slot, here, first : first + 128] = value
            return 0

        lax.fori_loop(0, rows // TILE, step, 0)
        back_ref[...] = dot(local_ref[slot], weight_ref[...], NT).astype(bf16)


def project_grad_kernel(x3_ref, x2_ref, x1_ref, x0_ref, far_ref, near_ref, out_ref, sums_ref):
    rows = far_ref.shape[1]
    total, sums = None, None
    for ref, local_ref, slot in (
        (x3_ref, far_ref, 0), (x2_ref, far_ref, 1), (x1_ref, near_ref, 0), (x0_ref, near_ref, 1)
    ):
        value = local_ref[slot]
        part = dot(ref[0:rows, :], value, TN)
        total = part if total is None else total + part
        one = jnp.sum(value.astype(f32), axis=0, keepdims=True)
        sums = one if sums is None else sums + one
    out_ref[...] = total.astype(bf16)
    sums_ref[...] = jnp.broadcast_to(sums, sums_ref.shape)


def last_kernel(
    tok_ref, frame_ref, lead_ref, table_ref, gain_ref, perm_ref, mine_ref, one_ref, more_ref, xgrad_ref,
    two_ref, upb_ref, qkv_ref, me_ref, out_ref, sums_ref,
):
    values, hot = rows_with_lead(tok_ref, frame_ref, lead_ref, table_ref)
    unit, inverse = norm_stats(values)
    other = jnp.concatenate([one_ref[...], more_ref[...]], axis=0)
    local = (mine_ref[...].astype(f32) + other.astype(f32)).astype(bf16)
    grad = dot(perm_ref[...], local, TN)
    e = grad * row_of(gain_ref)
    mean_e = jnp.mean(e, axis=-1, keepdims=True)
    along = jnp.mean(e * unit, axis=-1, keepdims=True)
    out = xgrad_ref[...] + inverse * (e - mean_e - unit * along)
    out_ref[...] = out
    leads = table_ref.shape[0]
    one = out.astype(bf16)
    rest = out - one.astype(f32)
    two = rest.astype(bf16)
    three = (rest - two.astype(f32)).astype(bf16)
    sums_ref[0:leads, :] = (dot(hot, one, NN) + dot(hot, two, NN) + dot(hot, three, NN)).astype(bf16)
    row = iota((16, grad.shape[1]), 0)
    me = me_ref[0]
    small = jnp.zeros((16, grad.shape[1]), f32)
    small = jnp.where(row == 0, jnp.sum(grad * unit, axis=0, keepdims=True), small)
    small = jnp.where(row == 1, jnp.sum(grad, axis=0, keepdims=True), small)
    for i in range(4):
        small = jnp.where(row == 2 + i, two_ref[i : i + 1, :], small)
        small = jnp.where(row == 6 + (me ^ i), upb_ref[i, 0:1, :], small)
    heads = (qkv_ref.shape[1] * 2 // 128) // 3
    bias = [qkv_ref[0:1, head * 128 : head * 128 + HEAD] for head in range(heads)]
    bias.append(qkv_ref[0:1, heads * 128 : heads * 128 + heads * HEAD])
    bias.append(jnp.zeros((1, grad.shape[1] - 2 * heads * HEAD), f32))
    small = jnp.where(row == 10 + me, jnp.concatenate(bias, axis=1), small)
    sums_ref[leads : leads + 16, :] = small.astype(bf16)


def finish_kernel(left_ref, right_ref, me_ref, lead_ref, g1_ref, b1_ref, g2_ref, b2_ref, ob_ref, db_ref, ub_ref, qv_ref):
    total = left_ref[...].astype(f32) + right_ref[...].astype(f32)
    leads = lead_ref.shape[0]
    lead_ref[...] = total[0:leads]
    for place, ref in enumerate((g1_ref, b1_ref, g2_ref, b2_ref, ob_ref, db_ref)):
        ref[...] = total[leads + place].reshape(ref.shape)
    me = me_ref[0]
    up, qv = total[leads + 6 : leads + 7], total[leads + 10 : leads + 11]
    for i in range(1, 4):
        up = jnp.where(me == i, total[leads + 6 + i : leads + 7 + i], up)
        qv = jnp.where(me == i, total[leads + 10 + i : leads + 11 + i], qv)
    ub_ref[...] = up.reshape(ub_ref.shape)
    width = qv_ref.shape[1]
    qv_ref[...] = jnp.concatenate([qv[:, 0:width], qv[:, width : 2 * width]], axis=0)


def bits_of(size):
    bits = []
    step = 1
    while step < size:
        bits.append(step)
        step *= 2
    return bits


def after(value, *others):
    return lax.optimization_barrier((value, *others))[0]


def swap(value, size, bit):
    return lax.ppermute(value, "rows", [(i, i ^ bit) for i in range(size)])


def add_low(left, right):
    return (left.astype(f32) + right.astype(f32)).astype(bf16)


def halves(value, bit, axis=0):
    half = value.shape[axis] // 2
    high = (lax.axis_index("rows") // bit) % 2
    return (
        lax.dynamic_slice_in_dim(value, high * half, half, axis),
        lax.dynamic_slice_in_dim(value, (1 - high) * half, half, axis),
    )


def joined(mine, other, bit, axis=0):
    high = (lax.axis_index("rows") // bit) % 2
    low_part, high_part = jnp.where(high == 1, other, mine), jnp.where(high == 1, mine, other)
    return jnp.concatenate([low_part, high_part], axis)


def on_device(
    rows_size,
    tokens, frame_id, lead_index, lead_embed, ln1_gain, ln1_bias, qkv_weight, qv_bias,
    out_weight, out_bias, ln2_gain, ln2_bias, up_weight, up_bias, down_weight, down_bias, out_grad,
):
    rows, width_all = tokens.shape
    width = qkv_weight.shape[2]
    heads = width // HEAD
    hidden = up_weight.shape[1]
    leads = lead_embed.shape[0]
    group = 4 * rows
    wide = (heads + 1) // 2 * 128
    bits = bits_of(rows_size)
    me = lax.axis_index("tp").reshape(1)
    side = (lax.axis_index("rows") % 2).reshape(1)

    def over(value, ring):
        return lax.ppermute(value, "tp", ring)

    out_far = over(out_weight, NEXT)
    mine, perm = call(
        pre_kernel,
        (shape_of((rows + PAD, width_all), bf16), shape_of((rows, rows), bf16)),
        [VMEM, VMEM, SMEM, VMEM, VMEM, VMEM, VMEM], (VMEM, VMEM), "pre", 5,
    )(tokens, frame_id, lead_index, lead_embed, ln1_gain, ln1_bias, up_bias)
    mine = after(mine, out_far)
    near = over(mine, CORE)
    far = over(mine, NEXT)
    early, early_counts = call(
        project_kernel,
        (shape_of((group, 3 * width), bf16), shape_of((8,), i32)),
        whole_specs(4), (VMEM, SMEM), "project", 8,
        scratch=[pltpu.VMEM((rows, 3 * width), bf16)],
    )(qkv_weight, qv_bias, mine, near)
    far, up_weight, down_weight, out_weight, out_far = lax.optimization_barrier(
        (far, up_weight, down_weight, out_weight, out_far, early)
    )[:5]
    across = over(far, CORE)
    parts = (mine, near, far, across)

    up_far = over(up_weight, NEXT)
    down_far = over(halves(down_weight, 1)[0], NEXT)
    out_near, out_across = over(out_weight, CORE), over(out_far, CORE)
    across, up_weight, down_weight, out_near, out_across = lax.optimization_barrier(
        (across, up_weight, down_weight, out_near, out_across)
    )
    up_near, down_near = over(up_weight, CORE), over(down_weight, CORE)

    att, lse, counts, a0, a1, a2, a3, q_all, k_all, v_all = call(
        attend_kernel,
        (
            shape_of((group, wide), bf16),
            shape_of((8, group), f32),
            shape_of((8,), i32),
        )
        + (shape_of((rows * 3 // 2, 128), bf16),) * 4
        + (shape_of((heads, group, 128), bf16),) * 3,
        whole_specs(2) + [SMEM] + [HBM] * 3, (VMEM, VMEM, SMEM) + (VMEM,) * 4 + (HBM,) * 3, "attend", 40,
        scratch=[
            pltpu.VMEM((2, rows + PAD, width_all), bf16),
            pltpu.VMEM((group, 3 * width), bf16),
            pltpu.VMEM((rows, 3 * width), bf16),
            pltpu.VMEM((heads, group, 128), bf16),
            pltpu.VMEM((heads, group, 128), bf16),
            pltpu.VMEM((heads, group, 128), bf16),
            pltpu.VMEM((2, 2 * group // 3, 512), f32),
            pltpu.SemaphoreType.DMA((3,)),
            pltpu.SemaphoreType.DMA((3,)),
        ],
    )(qkv_weight, qv_bias, early_counts, early, far, across)

    got = [a0, over(a1, CORE), over(a2, NEXT), over(a3, DIAG)]
    up_far, down_far, out_near, out_across, up_near, down_near, pair_weight = lax.optimization_barrier(
        (up_far, down_far, out_near, out_across, up_near, down_near, qkv_weight, counts)
    )[:7]
    down_side = swap(down_far, rows_size, 1)
    got[1], up_far, down_far, pair_weight = lax.optimization_barrier((got[1], up_far, down_far, pair_weight))
    up_across, down_across = over(up_far, CORE), over(down_far, CORE)
    value_weight = pair_weight[2]
    pair_weight = pair_weight[0:2].reshape(2, width_all, heads, HEAD).transpose(1, 2, 0, 3)
    weight_heads = jnp.concatenate(
        [pair_weight.reshape(width_all, heads * 128), jnp.pad(value_weight, ((0, 0), (0, wide - width)))], axis=1
    )
    down_side, *got[2:] = lax.optimization_barrier((down_side, *got[2:]))
    down_side_across = over(down_side, CORE)

    layer_out, xgrad, agrad, normed_two, attu, s0, s1, s2, s3, sums_two, up_b, act, hid = call(
        middle_kernel,
        (
            shape_of((rows, width_all), bf16),
            shape_of((rows, width_all), f32),
            shape_of((rows, width_all), bf16),
            shape_of((rows, width_all), bf16),
            shape_of((4, rows, width), bf16),
        )
        + (shape_of((rows * 3 // 2, 128), bf16),) * 4
        + (
            shape_of((8, width_all), f32),
            shape_of((4, 8, hidden), f32),
            shape_of((4, rows, hidden), bf16),
            shape_of((4, rows, hidden), bf16),
        ),
        [VMEM, VMEM, SMEM] + whole_specs(15) + [SMEM] + [HBM] * 14, (VMEM,) * 11 + (HBM,) * 2, "middle", 32,
        scratch=[
            pltpu.VMEM((rows, width_all), f32),
            pltpu.VMEM((rows, width_all), f32),
            pltpu.VMEM((rows, wide), bf16),
            pltpu.VMEM((4, PAD, width_all), bf16),
            pltpu.VMEM((4, width_all, hidden), bf16),
            pltpu.VMEM((4, hidden, width_all), bf16),
            pltpu.VMEM((4, rows, hidden), bf16),
            pltpu.VMEM((4, rows, hidden), bf16),
            pltpu.SemaphoreType.DMA((14,)),
            pltpu.SemaphoreType.DMA((8,)),
        ],
    )(
        tokens, frame_id, lead_index, lead_embed, perm, *got, out_weight, out_near, out_far, out_across,
        ln2_gain, ln2_bias, out_bias, down_bias, out_grad, side,
        *parts, up_weight, up_near, up_far, up_across,
        down_weight, down_near, down_far, down_across, down_side, down_side_across,
    )

    got_grad = [s0, over(s1, CORE), over(s2, NEXT), over(s3, DIAG)]

    def block_of(step):
        return jnp.where(step < 2, 2 * step + 1, 2 * step - 4)

    def full(shape):
        return pl.BlockSpec(shape, lambda s: (0,) * len(shape))

    def picked(shape):
        return pl.BlockSpec((1,) + shape, lambda s: (block_of(s), 0, 0))

    cut = width_all + width
    first_two, last_two = lambda s: (jnp.minimum(s, 1), 0, 0), lambda s: (jnp.maximum(s - 2, 0), 0, 0)
    up_share, down_share = (1, cut, hidden), (1, hidden, width_all)
    up_send, up_keep, down_send, down_keep = call(
        weight_grad_kernel,
        (shape_of((2, cut, hidden), bf16),) * 2 + (shape_of((2, hidden, width_all), bf16),) * 2,
        [full((rows, width_all))] * 3 + [picked((rows, hidden))] * 2 + [picked((rows, width))],
        (
            pl.BlockSpec(up_share, first_two), pl.BlockSpec(up_share, last_two),
            pl.BlockSpec(down_share, first_two), pl.BlockSpec(down_share, last_two),
        ),
        "weight_grad", 18, grid=(4,), scratch=[pltpu.VMEM((width_all, rows), bf16)],
    )(normed_two, out_grad, agrad, act, hid, attu)
    *got_grad[1:], up_send, up_keep, down_send, down_keep = lax.optimization_barrier(
        (*got_grad[1:], up_send, up_keep, down_send, down_keep)
    )
    up_got, down_got = over(up_send, CORE), over(down_send, CORE)
    grad_all, inner = call(
        gather_grad_kernel,
        (shape_of((heads, group, 128), bf16), shape_of((8, group), f32)),
        [SMEM] + whole_specs(5), (VMEM, VMEM), "gather_grad", 6,
        scratch=[pltpu.VMEM((group, wide), bf16), pltpu.VMEM((rows, wide), bf16)],
    )(after(counts, up_send), *got_grad, att)

    up_got, down_got = after(up_got, inner), after(down_got, inner)
    down_mine = add_low(down_keep[0], down_got[0])
    down_other = add_low(down_keep[1], down_got[1])
    (up_keep, up_give), (up_keep_two, up_give_two) = halves(up_keep, 1, 1), halves(up_got, 1, 1)
    up_mine, up_away = add_low(up_keep, up_keep_two), add_low(up_give, up_give_two)
    down_y = over(down_other, NEXT)
    up_x = swap(up_away, rows_size, 1)

    def attend_back(first, count, grads):
        spec = pl.BlockSpec((1, group, 128), lambda s: (first + s, 0, 0))
        return call(
            functools.partial(attend_back_kernel, first),
            shape_of((count, group, 256), bf16),
            [full((8, group))] * 2 + [spec] * 4,
            pl.BlockSpec((1, group, 256), lambda s: (s, 0, 0)), "attend_back", 15 * count,
            scratch=[pltpu.VMEM((128, group), f32)], grid=(count,),
        )(lse, inner, q_all, k_all, v_all, grads)

    back_01 = attend_back(0, heads - 1, after(grad_all, down_other, up_away, down_mine, up_mine))
    down_y, up_x = after(down_y, back_01), after(up_x, back_01)
    near_z, far_z = bits[1], bits[2:]
    (down_keep, down_give), (down_keep_two, down_give_two) = halves(down_mine, near_z), halves(down_y, near_z)
    down_half_sum, down_away = add_low(down_keep, down_keep_two), add_low(down_give, down_give_two)
    up_half_sum = add_low(up_mine[0], up_x[0])
    up_other = add_low(up_mine[1], up_x[1])
    down_x = swap(down_away, rows_size, near_z)
    up_y = over(up_other, NEXT)
    back_2 = attend_back(heads - 1, 1, after(grad_all, back_01, down_away, up_other, up_half_sum, down_half_sum))
    down_x, up_y = after(down_x, back_2), after(up_y, back_2)
    (down_keep, down_give), (down_keep_two, down_give_two) = halves(down_half_sum, 1), halves(down_x, 1)
    (up_keep, up_give), (up_keep_two, up_give_two) = halves(up_half_sum, near_z), halves(up_y, near_z)
    down_z, down_away = add_low(down_keep, down_keep_two), add_low(down_give, down_give_two)
    up_z, up_away = add_low(up_keep, up_keep_two), add_low(up_give, up_give_two)
    up_got, down_got = swap(up_away, rows_size, near_z), swap(down_away, rows_size, 1)

    def project_back(chosen, counts):
        return call(
            functools.partial(project_back_kernel, chosen),
            (shape_of((2, rows, heads * 128 + wide), bf16),) + (shape_of((rows, width_all), bf16),) * 2,
            [SMEM] + whole_specs(3), (VMEM,) * 3, "project_back", 6,
            scratch=[pltpu.VMEM((TILE, 256), bf16)] * heads,
        )(counts, back_01, back_2, weight_heads)

    local_far, b3, b2 = project_back((3, 2), after(counts, up_away, up_z, down_away, down_z))

    up_got, down_got, b3 = lax.optimization_barrier((up_got, down_got, b3))
    split = down_z.shape[0]
    mixed = jnp.concatenate([add_low(down_z, down_got), add_low(up_z, up_got)], axis=0)

    def over_far_z(value):
        for bit in far_z:
            value = add_low(value, swap(value, rows_size, bit))
        return value

    over_far = over(b3, CORE)
    mixed_z = over_far_z(mixed)
    local_near, b1, b0 = project_back((1, 0), after(counts, mixed, b2))
    over_far, b2, b1 = lax.optimization_barrier((over_far, b2, b1))
    over_near = over(b1, CORE)
    first = rows * 3 // 4
    back_one, back_two = add_low(b2[:first], over_far[:first]), add_low(b2[first:], over_far[first:])
    far_one = over(back_one, NEXT)
    qkv_grad, qkv_sums = call(
        project_grad_kernel,
        (shape_of((width_all, heads * 128 + wide), bf16), shape_of((8, heads * 128 + wide), f32)),
        whole_specs(6), (VMEM, VMEM), "project_grad", 6,
    )(*parts[::-1], after(local_far, back_one), local_near)
    far_one, b0 = lax.optimization_barrier((far_one, b0, qkv_grad))[:2]
    q_keep, q_give = halves(qkv_grad, 1)
    q_got = swap(q_give, rows_size, 1)
    here = add_low(b0, over_near)
    far_one, back_two, mixed, q_got = lax.optimization_barrier((far_one, back_two, mixed_z, q_got))
    down_z, up_z = mixed[:split], mixed[split:]
    far_two = over(back_two, NEXT)
    q_keep, q_give = halves(add_low(q_keep, q_got), near_z)
    q_got = swap(q_give, rows_size, near_z)
    down_got = swap(down_z, rows_size, near_z)
    far_two, q_got = lax.optimization_barrier((far_two, q_got))
    q_z = add_low(q_keep, q_got)
    cut_up = up_z.shape[0] // 2
    up_one, up_two = up_z[:cut_up], up_z[cut_up:]
    one_got, two_got = swap(up_one, rows_size, 1), swap(up_two, rows_size, near_z)
    q_far = swap(q_z, rows_size, far_z[0])

    tokens_grad, small = call(
        last_kernel,
        (shape_of((rows, width_all), f32), shape_of((leads + 16, width_all), bf16)),
        [VMEM, VMEM, SMEM] + whole_specs(10) + [SMEM], (VMEM, VMEM), "last", 7,
    )(
        tokens, frame_id, lead_index, lead_embed, ln1_gain, perm, after(here, up_one, up_two, q_z), far_one, far_two, xgrad,
        sums_two, up_b, qkv_sums, me,
    )

    small, one_got, down_got = lax.optimization_barrier((small, one_got, down_got))
    down_z = joined(down_z[None], down_got[None], near_z)
    down_got = swap(down_z, rows_size, 1)
    up_one = joined(up_one[None], one_got[None], 1)
    small = add_low(small, over(small, CORE))
    small = add_low(small, over(small, NEXT))
    small, two_got, q_far = lax.optimization_barrier((small, two_got, q_far))
    up_two = joined(up_two[None], two_got[None], near_z)
    two_got = swap(up_two, rows_size, 1)
    q_z = add_low(q_z, q_far)
    for bit in far_z[1:]:
        q_z = add_low(q_z, swap(q_z, rows_size, bit))
    q_got = swap(q_z, rows_size, near_z)
    small = add_low(small, swap(small, rows_size, near_z))
    small, up_one = lax.optimization_barrier((small, up_one))
    one_got = swap(up_one, rows_size, near_z)
    for bit in far_z:
        small = add_low(small, swap(small, rows_size, bit))
    q_z = joined(q_z, q_got, near_z)
    q_got = swap(q_z, rows_size, 1)
    down_sum = joined(down_z, down_got, 1, 1).astype(f32).reshape(hidden, width_all)
    up_sum = jnp.concatenate(
        [joined(up_one[:, None], one_got[:, None], near_z, 1), joined(up_two[None], two_got[None], 1)], axis=2
    )
    up_sum = up_sum.astype(f32).reshape(cut, width_all)
    qkv_sum = joined(q_z, q_got, 1)

    pairs_sum = qkv_sum[:, 0 : heads * 128].reshape(width_all, heads, 2, HEAD).transpose(2, 0, 1, 3)
    qkv_out = jnp.concatenate(
        [
            pairs_sum.reshape(2, width_all, width),
            qkv_sum[:, heads * 128 : heads * 128 + width].reshape(1, width_all, width),
        ],
        axis=0,
    ).astype(f32)
    vector = shape_of((width_all,), f32)
    lead_sum, g1, b1, g2, b2, out_b, down_b, up_b_sum, qv_sum = call(
        finish_kernel,
        (shape_of((leads, width_all), f32),) + (vector,) * 6 + (shape_of((hidden,), f32), shape_of((2, width), f32)),
        [VMEM, VMEM, SMEM], (VMEM,) * 9, "finish", 1,
    )(after(small, qkv_out), swap(small, rows_size, 1), me)
    return (
        layer_out, tokens_grad, lead_sum, g1, b1, qkv_out, qv_sum, up_sum[width_all:], out_b, g2, b2,
        up_sum[0:width_all], up_b_sum, down_sum, down_b,
    )


def solution(mesh):
    rows_size = mesh.shape["rows"]
    split = P(("rows", "tp"), None)
    placed = (
        split, P(("rows", "tp")), P("rows"), P(), P(), P(), P(None, None, "tp"), P(None, "tp"),
        P("tp", None), P(), P(), P(), P(None, "tp"), P("tp"), P("tp", None), P(), split,
    )
    return jax.shard_map(
        functools.partial(on_device, rows_size),
        mesh=mesh,
        in_specs=placed,
        out_specs=(
            split, split, P(), P(), P(), P(None, None, "tp"), P(None, "tp"), P("tp", None), P(), P(), P(),
            P(None, "tp"), P("tp"), P("tp", None), P(),
        ),
        check_vma=False,
    )
```

```python
import functools
import math

import jax
import jax.numpy as jnp
from jax import lax
from jax.experimental import pallas as pl
from jax.experimental.pallas import tpu as pltpu
from jax.sharding import PartitionSpec as P

HEAD = 64
EPS = 1e-05
LOG2E = math.log2(math.e)
LN2 = math.log(2.0)
TILE = 256
PAD = 16
VMEM_LIMIT = 60 * 1024 * 1024

f32 = jnp.float32
bf16 = jnp.bfloat16
i32 = jnp.int32

CORE = ((0, 1), (1, 0), (2, 3), (3, 2))
NEXT = ((0, 2), (2, 0), (1, 3), (3, 1))
DIAG = ((0, 3), (3, 0), (1, 2), (2, 1))

LIMITS = {
    "pre": 60, "project": 60, "attend": 48, "attend_last": 60, "middle": 60, "weight_grad": 60, "gather_grad": 24, "attend_back": 48,
    "project_back": 32, "project_grad": 60, "last": 32, "join": 16, "finish": 8,
}


def iota(shape, axis):
    return lax.broadcasted_iota(i32, shape, axis)


def dot(left, right, dims):
    return lax.dot_general(left, right, (dims, ((), ())), preferred_element_type=f32)


NN = ((1,), (0,))
NT = ((1,), (1,))
TN = ((0,), (0,))


def shape_of(shape, dtype):
    return jax.ShapeDtypeStruct(shape, dtype)


def whole_specs(count):
    return [pl.BlockSpec(memory_space=pltpu.VMEM)] * count


SMEM = pl.BlockSpec(memory_space=pltpu.SMEM)
VMEM = pl.BlockSpec(memory_space=pltpu.VMEM)
HBM = pl.BlockSpec(memory_space=pl.ANY)


def call(body, out_shape, in_specs, out_specs, name, micros, scratch=(), grid=()):
    return pl.pallas_call(
        body,
        out_shape=out_shape,
        grid=grid,
        in_specs=in_specs,
        out_specs=out_specs,
        scratch_shapes=scratch,
        compiler_params=pltpu.CompilerParams(vmem_limit_bytes=LIMITS[name] * 1024 * 1024),
        name=name,
        cost_estimate=pl.CostEstimate(
            flops=int(micros * 1.15e9), bytes_accessed=1024, transcendentals=0
        ),
    )


def local_frame(frame_ref):
    return frame_ref[...].reshape(1, frame_ref.shape[0]) % 2


def row_of(ref):
    return ref[...].astype(f32).reshape(1, ref.shape[0])


def rows_with_lead(tok_ref, frame_ref, lead_ref, table_ref):
    frame = local_frame(frame_ref)
    lead = jnp.where(frame == 0, lead_ref[0], lead_ref[1])
    hot = (iota((table_ref.shape[0], frame.shape[1]), 0) == lead).astype(bf16)
    return tok_ref[...].astype(f32) + dot(hot, table_ref[...], TN), hot


def norm_stats(values):
    average = jnp.mean(values, axis=-1, keepdims=True)
    centred = values - average
    spread = jnp.mean(centred * centred, axis=-1, keepdims=True)
    inverse = lax.rsqrt(spread + EPS)
    return centred * inverse, inverse


def pre_kernel(tok_ref, frame_ref, lead_ref, table_ref, gain_ref, shift_ref, up_bias_ref, out_ref, perm_ref):
    rows = tok_ref.shape[0]
    values, _ = rows_with_lead(tok_ref, frame_ref, lead_ref, table_ref)
    unit, _ = norm_stats(values)
    normed = (unit * row_of(gain_ref) + row_of(shift_ref)).astype(bf16)
    first = (local_frame(frame_ref) == 0).astype(f32)
    before = (iota((rows, rows), 0) < iota((rows, rows), 1)).astype(bf16)
    earlier = dot(jnp.broadcast_to(first, (8, rows)).astype(bf16), before, NN)[0:1]
    count = jnp.sum(first, axis=1, keepdims=True)
    place = jnp.where(first > 0, earlier, count + iota((1, rows), 1).astype(f32) - earlier)
    perm = (iota((rows, rows), 0) == place.astype(i32)).astype(bf16)
    perm_ref[...] = perm
    out_ref[0:rows, :] = dot(perm, normed, NN).astype(bf16)
    high = jnp.floor(count * (1.0 / 16))
    low = count - 16 * high
    tail = iota((PAD, out_ref.shape[1]), 0)
    out_ref[rows : rows + PAD, :] = jnp.where(
        tail == 0, high, jnp.where(tail == 1, low, jnp.where(tail == 2, row_of(up_bias_ref), 0.0))
    ).astype(bf16)


def read_count(block_ref, rows):
    part = block_ref[rows : rows + PAD, 0:128].astype(f32)
    place, lane = iota(part.shape, 0), iota(part.shape, 1)
    worth = jnp.where(place == 0, 16.0, jnp.where(place == 1, 1.0, 0.0))
    return jnp.sum(jnp.where(lane == 0, part * worth, 0.0)).astype(i32)


def tile_moves(counts, rows, block, tile):
    group = 4 * rows
    count = counts[block]
    longs_before = sum(counts[:block], jnp.int32(0))
    limit = jnp.clip(count - tile * TILE, 0, TILE)
    moves = []
    for some, base, low, high in (
        (limit > 0, longs_before + tile * TILE, 0, limit),
        (limit < TILE, 2 * group // 3 + block * rows - longs_before - count + tile * TILE, limit, TILE),
    ):
        spot = jnp.minimum(base // TILE, group // TILE - 2)
        window = pl.ds(pl.multiple_of(spot * TILE, TILE), 2 * TILE)
        moves.append((some, window, base - spot * TILE, low, high))
    return moves


def aligned(index, size):
    return pl.ds(pl.multiple_of(index * size, size), size)


def to_group(value, dst_ref, moves):
    width = value.shape[1]
    for some, window, shift, low, high in moves:

        @pl.when(some)
        def _():
            dest, source = iota((2 * TILE, TILE), 0), iota((2 * TILE, TILE), 1)
            hot = (dest - source == shift) & (source >= low) & (source < high)
            moved = dot(hot.astype(bf16), value, NN).astype(bf16)
            dst_ref[window, 0:width] = dst_ref[window, 0:width] + moved


def from_group(src_refs, acc_refs, moves):
    (some_long, *long), (some_short, *short) = moves

    def moved(window, shift, low, high):
        source, dest = iota((TILE, 2 * TILE), 0), iota((TILE, 2 * TILE), 1)
        hot = ((dest - source == shift) & (source >= low) & (source < high)).astype(bf16)
        return [dot(hot, ref[window, :], NN).astype(bf16) for ref in src_refs]

    @pl.when(some_long)
    def _():
        for ref, value in zip(acc_refs, moved(*long)):
            ref[...] = value

    @pl.when(jnp.logical_not(some_long))
    def _():
        for ref, value in zip(acc_refs, moved(*short)):
            ref[...] = value

    @pl.when(some_long & some_short)
    def _():
        for ref, value in zip(acc_refs, moved(*short)):
            ref[...] = ref[...] + value


def pack_heads(src_ref, out_ref):
    rows = src_ref.shape[0]
    half = rows // 2
    lane = iota((half, 128), 1)
    out_ref[0:rows, :] = src_ref[:, 0:128]
    upper = src_ref[0:half, 128:256].astype(f32)
    lower = pltpu.roll(src_ref[half:rows, 128:256].astype(f32), HEAD, 1)
    out_ref[rows:, :] = jnp.where(lane < HEAD, upper, lower).astype(bf16)


def unpack_heads(src_ref, out_ref):
    rows = out_ref.shape[0]
    half = rows // 2
    lane = iota((half, 128), 1)
    out_ref[:, 0:128] = src_ref[0:rows, :]
    both = src_ref[rows:, :].astype(f32)
    out_ref[0:half, 128:256] = jnp.where(lane < HEAD, both, 0.0).astype(bf16)
    out_ref[half:rows, 128:256] = jnp.where(lane < HEAD, pltpu.roll(both, HEAD, 1), 0.0).astype(bf16)


def head_columns(ref, start, width):
    first = start // 128 * 128
    if first + 128 <= width:
        piece = ref[:, first : first + 128].astype(f32)
    else:
        piece = jnp.concatenate([ref[:, first : first + HEAD].astype(f32)] * 2, axis=1)
    return pltpu.roll(piece, HEAD, 1) if start != first else piece


def project_rows(x_ref, index, counts, weight_ref, bias_ref, value_ref, qkv_ref):
    rows = value_ref.shape[0]
    width = weight_ref.shape[2]
    for part in range(3):
        value = dot(x_ref[0:rows, :], weight_ref[part], NN)
        if part == 0:
            value = (value + bias_ref[0:1, :].astype(f32)) * (LOG2E / math.sqrt(HEAD))
        if part == 2:
            value = value + bias_ref[1:2, :].astype(f32)
        value_ref[:, part * width : (part + 1) * width] = value.astype(bf16)

    def place(tile, _):
        to_group(value_ref[aligned(tile, TILE), :], qkv_ref, tile_moves(counts, rows, index, tile))
        return 0

    lax.fori_loop(0, rows // TILE, place, 0)


def weight_cut(rows):
    part = rows * 3 // 8
    return part, rows - 2 * part


def project_kernel(
    weight_ref, bias_ref, x0_ref, x1_ref, place_ref, out_ref, up_ref, down_ref,
    qkv_ref, counts_ref, common_ref, up_part_ref, down_part_ref, value_ref,
):
    part, middle = weight_cut(up_ref.shape[0])
    first = out_ref.shape[0]
    common_ref[0:first, :] = out_ref[...]
    for index, (ref, part_ref, at) in enumerate(
        ((down_ref, down_part_ref, place_ref[0]), (up_ref, up_part_ref, place_ref[1]))
    ):
        common_ref[first + index * middle : first + (index + 1) * middle, :] = ref[part : part + middle, :]
        part_ref[...] = ref[pl.ds(pl.multiple_of(at * (part + middle), PAD), part), :]
    qkv_ref[...] = jnp.zeros(qkv_ref.shape, qkv_ref.dtype)
    counts = []
    for index, ref in enumerate((x0_ref, x1_ref)):
        counts.append(read_count(ref, value_ref.shape[0]))
        counts_ref[index] = counts[index]
        project_rows(ref, index, counts, weight_ref, bias_ref, value_ref, qkv_ref)


def attend_kernel(
    weight_ref, bias_ref, early_ref, part_ref, x2_ref, x3_ref,
    att_ref, lse_ref, counts_ref, a0_ref, a1_ref, a2_ref, a3_ref, q_out, k_out, v_out,
    x_buf, qkv_ref, value_ref, q_ref, k_ref, v_ref, scores_ref, load_sems, store_sems,
):
    rows = x2_ref.shape[0] - PAD
    group = 4 * rows
    long = 2 * group // 3
    width = weight_ref.shape[2]
    heads = width // HEAD
    loads = [
        pltpu.make_async_copy(source, target, load_sems.at[i])
        for i, (source, target) in enumerate(
            ((part_ref, qkv_ref), (x2_ref, x_buf.at[0]), (x3_ref, x_buf.at[1]))
        )
    ]
    for load in loads:
        load.start()
    loads[0].wait()
    counts = [early_ref[0], early_ref[1]]
    for index in (2, 3):
        loads[index - 1].wait()
        block_ref = x_buf.at[index - 2]
        counts.append(read_count(block_ref, rows))
        project_rows(block_ref, index, counts, weight_ref, bias_ref, value_ref, qkv_ref)
    for index, count in enumerate(counts):
        counts_ref[index] = count
    lane = iota((group, 128), 1)
    stores = []
    for part, ref, out, fill in ((1, k_ref, k_out, 0.0), (2, v_ref, v_out, 1.0), (0, q_ref, q_out, 0.0)):
        for head in range(heads):
            piece = head_columns(qkv_ref, part * width + head * HEAD, 3 * width)
            ref[head] = jnp.where(lane < HEAD, piece, fill).astype(bf16)
        store = pltpu.make_async_copy(ref, out, store_sems.at[part])
        store.start()
        stores.append(store)

    block = 512
    row = iota((128, block), 0)
    half = iota((block, 128), 1)
    tasks = [
        (head, first, low, high)
        for low, high in ((0, long), (long, group))
        for first in range(low, high, block)
        for head in range(heads)
    ]

    def scores(task, part):
        head, first, low, high = tasks[task]
        keys = slice(low + part * block, low + (part + 1) * block)
        value = dot(k_ref[head, keys, :], q_ref[head, first : first + block, :], NT)
        scores_ref[task % 2, part * block : (part + 1) * block, :] = value
        return jnp.max(value.reshape(block // 8, 8, block), axis=0)

    def parts_of(task):
        return (tasks[task][3] - tasks[task][2]) // block if task < len(tasks) else 0

    largest = functools.reduce(jnp.maximum, [scores(0, part) for part in range(parts_of(0))])
    outs = []
    for task, (head, first, low, high) in enumerate(tasks):
        top = jnp.max(largest, axis=0, keepdims=True)
        following, mixed = [], None
        for part in range(max(parts_of(task), parts_of(task + 1))):
            if part < parts_of(task + 1):
                following.append(scores(task + 1, part))
            if part < parts_of(task):
                raised = jnp.exp2(scores_ref[task % 2, part * block : (part + 1) * block, :] - top)
                keys = slice(low + part * block, low + (part + 1) * block)
                value = dot(v_ref[head, keys, :], raised.astype(bf16), TN)
                mixed = value if mixed is None else mixed + value
        if following:
            largest = functools.reduce(jnp.maximum, following)
        totals = mixed[HEAD : HEAD + 1, :]
        lse_ref[head : head + 1, first : first + block] = top + jnp.log2(totals)
        outs.append(jnp.where(row < HEAD, mixed / totals, 0.0))
        if head == heads - 1:
            for pair in range((heads + 1) // 2):
                value = outs[2 * pair].T
                if 2 * pair + 1 < heads:
                    value = value + pltpu.roll(outs[2 * pair + 1].T, HEAD, 1)
                att_ref[first : first + block, pair * 128 : (pair + 1) * 128] = value.astype(bf16)
            outs = []
    for index, out in enumerate((a0_ref, a1_ref, a2_ref, a3_ref)):

        def hand_back(tile, _, index=index):
            moves = tile_moves(counts, rows, index, tile)
            from_group((att_ref,), (qkv_ref.at[aligned(tile, TILE), 0 : att_ref.shape[1]],), moves)
            return 0

        lax.fori_loop(0, rows // TILE, hand_back, 0)
        pack_heads(qkv_ref.at[0:rows, 0 : att_ref.shape[1]], out)
    for store in stores:
        store.wait()


def middle_kernel(
    tok_ref, frame_ref, lead_ref, table_ref, perm_ref,
    at0_ref, at1_ref, at2_ref, at3_ref,
    gain_ref, shift_ref, out_bias_ref, down_bias_ref, place_ref,
    og_in, wo0_ref, wo1_ref, common2_ref, common3_ref,
    x0_ref, x1_ref, x2_ref, x3_ref, up0_ref, up1_ref, up2_ref, up3_ref,
    ux2_ref, ux3_ref, dn0_ref, dn1_ref, dn2_ref, dn3_ref, dx2_ref, dx3_ref,
    s0_ref, s1_ref, s2_ref, s3_ref, sums_ref, upb_ref,
    layer_out, xgrad_out, agrad_out, normed_out, attu_out, act_out, hid_out,
    y_ref, back_ref, at_ref, attu_ref, wo_ref, og_ref, normed_ref, layer_ref, agrad_ref, bias_buf, up_buf, dn_buf,
    act_ref, hid_ref, load_sems, store_sems,
):
    ats = (at0_ref, at1_ref, at2_ref, at3_ref)
    blocks = (x0_ref, x1_ref, x2_ref, x3_ref)
    sends = (s0_ref, s1_ref, s2_ref, s3_ref)
    rows, wide = tok_ref.shape
    hidden = up_buf.shape[2]
    width = wo0_ref.shape[0]
    span = wo_ref.shape[0] // 4
    part, middle = weight_cut(hidden)
    x, z = place_ref[0], place_ref[1]
    mine, other = (pl.ds(pl.multiple_of(at * (part + middle), PAD), part) for at in (x, 1 - x))
    up_mine, up_other = (pl.ds(pl.multiple_of(at * (part + middle), PAD), part) for at in (z, 1 - z))
    both = pl.ds(part, middle)
    wos = (wo0_ref, wo1_ref, common2_ref.at[0:width], common3_ref.at[0:width])
    first_loads = [
        pltpu.make_async_copy(wos[i], wo_ref.at[i * span : i * span + width], load_sems.at[14 + i]) for i in range(4)
    ]
    loads = [[], [], [], []]
    loads[0].append(pltpu.make_async_copy(og_in, og_ref, load_sems.at[18]))
    for index, ref, target, sem in (
        (0, up0_ref, up_buf.at[0], 0),
        (1, up1_ref, up_buf.at[1], 1),
        (2, common2_ref.at[width : width + middle], dn_buf.at[2, both], 21),
        (3, common3_ref.at[width : width + middle], dn_buf.at[3, both], 22),
        (2, common2_ref.at[width + middle :], up_buf.at[2, both], 23),
        (3, common3_ref.at[width + middle :], up_buf.at[3, both], 24),
        (2, up2_ref, up_buf.at[2, up_mine], 2),
        (2, ux2_ref, up_buf.at[2, up_other], 19),
        (3, up3_ref, up_buf.at[3, up_mine], 3),
        (3, ux3_ref, up_buf.at[3, up_other], 20),
        (0, dn0_ref, dn_buf.at[0], 4),
        (1, dn1_ref, dn_buf.at[1], 5),
        (2, dn2_ref, dn_buf.at[2, mine], 6),
        (2, dx2_ref, dn_buf.at[2, other], 7),
        (3, dn3_ref, dn_buf.at[3, mine], 8),
        (3, dx3_ref, dn_buf.at[3, other], 9),
    ):
        loads[index].append(pltpu.make_async_copy(ref, target, load_sems.at[sem]))
    for index in range(4):
        tail = blocks[index].at[rows : rows + PAD]
        loads[index].append(pltpu.make_async_copy(tail, bias_buf.at[index], load_sems.at[10 + index]))
    for load in first_loads + sum(loads, []):
        load.start()
    stores = []

    def store(source, target):
        copy = pltpu.make_async_copy(source, target, store_sems.at[len(stores)])
        copy.start()
        stores.append(copy)

    gain = row_of(gain_ref)
    perm = perm_ref[...]
    for index in range(4):
        unpack_heads(ats[index], at_ref.at[:, index * span : (index + 1) * span])
        wo_ref[index * span + width : (index + 1) * span, :] = jnp.zeros((span - width, wide), bf16)
    attu_ref[...] = dot(perm, at_ref[...], TN).astype(bf16)
    store(attu_ref, attu_out)
    values, _ = rows_with_lead(tok_ref, frame_ref, lead_ref, table_ref)
    for load in first_loads:
        load.wait()
    x_one = values + row_of(out_bias_ref) + dot(attu_ref[...], wo_ref[...], NN)
    unit, inverse = norm_stats(x_one)
    normed_ref[...] = (unit * gain + row_of(shift_ref)).astype(bf16)
    store(normed_ref, normed_out)
    y_ref[...] = x_one + row_of(down_bias_ref)
    for index in range(4):
        for load in loads[index]:
            load.wait()
        up = up_buf[index]
        down = dn_buf[index]
        h = dot(normed_ref[...], up, NN) + bias_buf[index][2:3].astype(f32)
        g = dot(og_ref[...], down, NT)
        c = math.sqrt(2.0 / math.pi)
        h2 = h * h
        t = jnp.tanh(h * (c + (c * 0.044715) * h2))
        half = 0.5 + 0.5 * t
        act = h * half
        slope = half + act * (1.0 - t) * (c + (3 * c * 0.044715) * h2)
        hid = (slope * g).astype(bf16)
        actb = act.astype(bf16)
        act_ref[index] = actb
        hid_ref[index] = hid
        upb_ref[index] = jnp.broadcast_to(jnp.sum(hid.astype(f32), axis=0, keepdims=True), (8, hidden))
        if index < 3:
            y_ref[...] += dot(actb, down, NN)
        else:
            layer_ref[...] = (y_ref[...] + dot(actb, down, NN)).astype(bf16)
            store(layer_ref, layer_out)
        if index == 0:
            back_ref[...] = dot(hid, up, NT)
        else:
            back_ref[...] += dot(hid, up, NT)
        store(act_ref.at[index], act_out.at[index])
        store(hid_ref.at[index], hid_out.at[index])
    grad = back_ref[...]
    e = grad * gain
    spread_mean = jnp.mean(e, axis=-1, keepdims=True)
    along = jnp.mean(e * unit, axis=-1, keepdims=True)
    og = og_ref[...].astype(f32)
    xgrad = og + inverse * (e - spread_mean - unit * along)
    y_ref[...] = xgrad
    store(y_ref, xgrad_out)
    agrad = xgrad.astype(bf16)
    agrad_ref[...] = agrad
    store(agrad_ref, agrad_out)
    at_ref[...] = dot(agrad, wo_ref[...], NT).astype(bf16)
    at_ref[...] = dot(perm, at_ref[...], NN).astype(bf16)
    for index in range(4):
        pack_heads(at_ref.at[:, index * span : (index + 1) * span], sends[index])
    sums_ref[...] = jnp.concatenate(
        [
            jnp.sum(grad * unit, axis=0, keepdims=True),
            jnp.sum(grad, axis=0, keepdims=True),
            jnp.sum(agrad.astype(f32), axis=0, keepdims=True),
            jnp.sum(og, axis=0, keepdims=True),
            jnp.zeros((4, og.shape[1]), f32),
        ],
        axis=0,
    )
    for copy in stores:
        copy.wait()


def weight_grad_kernel(
    normed_ref, og_ref, agrad_ref, act_ref, hid_ref, attu_ref, up_send_ref, up_keep_ref, down_send_ref, down_keep_ref,
    turned_ref,
):
    @pl.when(pl.program_id(0) == 0)
    def _():
        turned_ref[...] = normed_ref[...].T

    up = dot(turned_ref[...], hid_ref[0], NN).astype(bf16)
    out = dot(attu_ref[...], agrad_ref[...], TN).astype(bf16)[0 : up_send_ref.shape[1] - up.shape[0]]
    down = dot(act_ref[0], og_ref[...], TN).astype(bf16)
    rows = up.shape[0]
    step = pl.program_id(0)
    for chosen, up_ref, down_ref in (
        (step < 2, up_send_ref, down_send_ref), (step >= 2, up_keep_ref, down_keep_ref),
    ):

        @pl.when(chosen)
        def _(up_ref=up_ref, down_ref=down_ref):
            up_ref[0, 0:rows, :] = up
            up_ref[0, rows:, :] = out
            down_ref[0] = down


def gather_grad_kernel(counts_ref, b0_ref, b1_ref, b2_ref, b3_ref, att_ref, out_ref, inner_ref, sorted_ref, block_ref):
    blocks = (b0_ref, b1_ref, b2_ref, b3_ref)
    rows = block_ref.shape[0]
    group = 4 * rows
    heads = out_ref.shape[0]
    counts = [counts_ref[i] for i in range(4)]
    sorted_ref[...] = jnp.zeros(sorted_ref.shape, sorted_ref.dtype)
    for index, ref in enumerate(blocks):

        unpack_heads(ref, block_ref)

        def place(tile, _, index=index):
            to_group(block_ref[aligned(tile, TILE), :], sorted_ref, tile_moves(counts, rows, index, tile))
            return 0

        lax.fori_loop(0, rows // TILE, place, 0)
    lane = iota((group, 128), 1)
    pick_row, pick_lane = iota((8, 128), 0), iota((8, 128), 1)
    inner_ref[...] = jnp.zeros(inner_ref.shape, f32)
    for pair in range((heads + 1) // 2):
        columns = slice(pair * 128, (pair + 1) * 128)
        grad = sorted_ref[:, columns].astype(f32)
        product = grad * att_ref[:, columns].astype(f32)
        high = product.astype(bf16)
        low = (product - high.astype(f32)).astype(bf16)
        pick = (pick_row == 2 * pair + pick_lane // HEAD).astype(bf16)
        inner_ref[...] += dot(pick, high, NT) + dot(pick, low, NT)
        out_ref[2 * pair] = jnp.where(lane < HEAD, grad, 0.0).astype(bf16)
        if 2 * pair + 1 < heads:
            out_ref[2 * pair + 1] = jnp.where(lane < HEAD, pltpu.roll(grad, HEAD, 1), 0.0).astype(bf16)


def attend_back_kernel(first_head, first_lse, lse_ref, inner_ref, q_ref, k_ref, v_ref, g_ref, out_ref, dq_ref):
    group = q_ref.shape[1]
    long = 2 * group // 3
    block = 1024
    lane = iota((block, 128), 1)
    head = first_head + pl.program_id(0)
    lse = jnp.sum(jnp.where(iota(lse_ref.shape, 0) == first_lse + pl.program_id(0), lse_ref[...], 0.0), axis=0, keepdims=True)
    inner = jnp.sum(jnp.where(iota(inner_ref.shape, 0) == head, inner_ref[...], 0.0), axis=0, keepdims=True)
    done = set()
    for low, high in ((0, long), (long, group)):
        for keys in range(low, high, block):
            key = k_ref[0, keys : keys + block, :]
            value = v_ref[0, keys : keys + block, :]
            key_grad, value_grad = None, None
            for queries in range(low, high, block):
                query = q_ref[0, queries : queries + block, :]
                grad = g_ref[0, queries : queries + block, :]
                probs = jnp.exp2(dot(key, query, NT) - lse[:, queries : queries + block])
                inside = dot(value, grad, NT) - inner[:, queries : queries + block]
                score_grad = (probs * inside).astype(bf16)
                value_part = dot(probs.astype(bf16), grad, NN)
                key_part = dot(score_grad, query, NN)
                query_part = dot(key, score_grad, TN)
                value_grad = value_part if value_grad is None else value_grad + value_part
                key_grad = key_part if key_grad is None else key_grad + key_part
                place = (slice(None), slice(queries, queries + block))
                dq_ref[place] = query_part if queries not in done else dq_ref[place] + query_part
                done.add(queries)
            out_ref[0, keys : keys + block, 0:128] = pltpu.roll(key_grad * LN2, HEAD, 1).astype(bf16)
            out_ref[0, keys : keys + block, 128:256] = value_grad.astype(bf16)
    wide = iota((group, 128), 1)
    query_grad = dq_ref[...].T * (1.0 / math.sqrt(HEAD))
    pair = jnp.where(wide < HEAD, query_grad, out_ref[0, :, 0:128].astype(f32))
    out_ref[0, :, 0:128] = pair.astype(bf16)


def project_back_kernel(chosen, counts_ref, h01_ref, h2_ref, weight_ref, local_ref, one_ref, two_ref, *acc_refs):
    refs = [h01_ref.at[i] for i in range(h01_ref.shape[0])] + [h2_ref.at[i] for i in range(h2_ref.shape[0])]
    rows = local_ref.shape[1]
    counts = [counts_ref[i] for i in range(4)]
    pairs = len(refs) * 128
    lane = iota((TILE, 128), 1)
    for slot, (index, back_ref) in enumerate(zip(chosen, (one_ref, two_ref))):

        def step(tile, _, index=index, slot=slot):
            here = aligned(tile, TILE)
            from_group(refs, acc_refs, tile_moves(counts, rows, index, tile))
            for head, ref in enumerate(acc_refs):
                local_ref[slot, here, head * 128 : (head + 1) * 128] = ref[:, 0:128]
            for pair in range((len(refs) + 1) // 2):
                value = acc_refs[2 * pair][:, 128:256]
                if 2 * pair + 1 < len(refs):
                    other = acc_refs[2 * pair + 1][:, 128:256].astype(f32)
                    value = jnp.where(lane < HEAD, value.astype(f32), pltpu.roll(other, HEAD, 1)).astype(bf16)
                first = pairs + pair * 128
                local_ref[slot, here, first : first + 128] = value
            return 0

        lax.fori_loop(0, rows // TILE, step, 0)
        back_ref[...] = dot(local_ref[slot], weight_ref[...], NT).astype(bf16)


def project_grad_kernel(x3_ref, x2_ref, x1_ref, x0_ref, far_ref, near_ref, out_ref, sums_ref):
    rows = far_ref.shape[1]
    total, sums = None, None
    for ref, local_ref, slot in (
        (x3_ref, far_ref, 0), (x2_ref, far_ref, 1), (x1_ref, near_ref, 0), (x0_ref, near_ref, 1)
    ):
        value = local_ref[slot]
        part = dot(ref[0:rows, :], value, TN)
        total = part if total is None else total + part
        one = jnp.sum(value.astype(f32), axis=0, keepdims=True)
        sums = one if sums is None else sums + one
    out_ref[...] = total.astype(bf16)
    sums_ref[...] = jnp.broadcast_to(sums, sums_ref.shape)


def last_kernel(
    tok_ref, frame_ref, lead_ref, table_ref, gain_ref, perm_ref, mine_ref, near_ref, one_ref, more_ref, xgrad_ref,
    two_ref, upb_ref, qkv_ref, me_ref, out_ref, sums_ref,
):
    values, hot = rows_with_lead(tok_ref, frame_ref, lead_ref, table_ref)
    unit, inverse = norm_stats(values)
    other = jnp.concatenate([one_ref[...], more_ref[...]], axis=0)
    local = (mine_ref[...].astype(f32) + near_ref[...].astype(f32) + other.astype(f32)).astype(bf16)
    grad = dot(perm_ref[...], local, TN)
    e = grad * row_of(gain_ref)
    mean_e = jnp.mean(e, axis=-1, keepdims=True)
    along = jnp.mean(e * unit, axis=-1, keepdims=True)
    out = xgrad_ref[...] + inverse * (e - mean_e - unit * along)
    out_ref[...] = out
    leads = table_ref.shape[0]
    one = out.astype(bf16)
    rest = out - one.astype(f32)
    two = rest.astype(bf16)
    three = (rest - two.astype(f32)).astype(bf16)
    sums_ref[0:leads, :] = (dot(hot, one, NN) + dot(hot, two, NN) + dot(hot, three, NN)).astype(bf16)
    row = iota((16, grad.shape[1]), 0)
    me = me_ref[0]
    small = jnp.zeros((16, grad.shape[1]), f32)
    small = jnp.where(row == 0, jnp.sum(grad * unit, axis=0, keepdims=True), small)
    small = jnp.where(row == 1, jnp.sum(grad, axis=0, keepdims=True), small)
    for i in range(4):
        small = jnp.where(row == 2 + i, two_ref[i : i + 1, :], small)
        small = jnp.where(row == 6 + (me ^ i), upb_ref[i, 0:1, :], small)
    heads = (qkv_ref.shape[1] * 2 // 128) // 3
    bias = [qkv_ref[0:1, head * 128 : head * 128 + HEAD] for head in range(heads)]
    bias.append(qkv_ref[0:1, heads * 128 : heads * 128 + heads * HEAD])
    bias.append(jnp.zeros((1, grad.shape[1] - 2 * heads * HEAD), f32))
    small = jnp.where(row == 10 + me, jnp.concatenate(bias, axis=1), small)
    sums_ref[leads : leads + 16, :] = small.astype(bf16)


def finish_kernel(left_ref, right_ref, me_ref, lead_ref, g1_ref, b1_ref, g2_ref, b2_ref, ob_ref, db_ref, ub_ref, qv_ref):
    total = left_ref[...].astype(f32) + right_ref[...].astype(f32)
    leads = lead_ref.shape[0]
    lead_ref[...] = total[0:leads]
    for place, ref in enumerate((g1_ref, b1_ref, g2_ref, b2_ref, ob_ref, db_ref)):
        ref[...] = total[leads + place].reshape(ref.shape)
    me = me_ref[0]
    up, qv = total[leads + 6 : leads + 7], total[leads + 10 : leads + 11]
    for i in range(1, 4):
        up = jnp.where(me == i, total[leads + 6 + i : leads + 7 + i], up)
        qv = jnp.where(me == i, total[leads + 10 + i : leads + 11 + i], qv)
    ub_ref[...] = up.reshape(ub_ref.shape)
    width = qv_ref.shape[1]
    qv_ref[...] = jnp.concatenate([qv[:, 0:width], qv[:, width : 2 * width]], axis=0)


def join_kernel(one_ref, one_got_ref, two_ref, two_got_ref, place_ref, up_ref, out_ref):
    cut, rows = up_ref.shape[0], one_ref.shape[1]
    x, z = place_ref[0], place_ref[1]
    for at_x in range(2):
        for at_z in range(2):
            one = jnp.where(z == at_z, one_ref[at_x].astype(f32), one_got_ref[at_x].astype(f32))
            two = jnp.where(x == at_x, two_ref[at_z].astype(f32), two_got_ref[at_z].astype(f32))
            for part, value in enumerate((one, two)):
                first = ((2 * at_x + at_z) * 2 + part) * rows
                inside = min(max(cut - first, 0), rows)
                if inside:
                    up_ref[first : first + inside, :] = value[:inside]
                if inside < rows:
                    start = max(first - cut, 0)
                    out_ref[start : start + rows - inside, :] = value[inside:]


def bits_of(size):
    bits = []
    step = 1
    while step < size:
        bits.append(step)
        step *= 2
    return bits


def after(value, *others):
    return lax.optimization_barrier((value, *others))[0]


def swap(value, size, bit):
    return lax.ppermute(value, "rows", [(i, i ^ bit) for i in range(size)])


def add_low(left, right):
    return (left.astype(f32) + right.astype(f32)).astype(bf16)


def halves(value, bit, axis=0):
    half = value.shape[axis] // 2
    high = (lax.axis_index("rows") // bit) % 2
    return (
        lax.dynamic_slice_in_dim(value, high * half, half, axis),
        lax.dynamic_slice_in_dim(value, (1 - high) * half, half, axis),
    )


def joined(mine, other, bit, axis=0):
    high = (lax.axis_index("rows") // bit) % 2
    low_part, high_part = jnp.where(high == 1, other, mine), jnp.where(high == 1, mine, other)
    return jnp.concatenate([low_part, high_part], axis)


def on_device(
    rows_size,
    tokens, frame_id, lead_index, lead_embed, ln1_gain, ln1_bias, qkv_weight, qv_bias,
    out_weight, out_bias, ln2_gain, ln2_bias, up_weight, up_bias, down_weight, down_bias, out_grad,
):
    rows, width_all = tokens.shape
    width = qkv_weight.shape[2]
    heads = width // HEAD
    hidden = up_weight.shape[1]
    leads = lead_embed.shape[0]
    group = 4 * rows
    wide = (heads + 1) // 2 * 128
    bits = bits_of(rows_size)
    me = lax.axis_index("tp").reshape(1)
    near_z, far_z = bits[1], bits[2:]
    place = jnp.stack([lax.axis_index("rows") % 2, lax.axis_index("rows") // near_z % 2])

    def over(value, ring):
        return lax.ppermute(value, "tp", ring)

    def full(shape):
        return pl.BlockSpec(shape, lambda s: (0,) * len(shape))

    mine, perm = call(
        pre_kernel,
        (shape_of((rows + PAD, width_all), bf16), shape_of((rows, rows), bf16)),
        [VMEM, VMEM, SMEM, VMEM, VMEM, VMEM, VMEM], (VMEM, VMEM), "pre", 5,
    )(tokens, frame_id, lead_index, lead_embed, ln1_gain, ln1_bias, up_bias)
    near = over(mine, CORE)
    far = over(mine, NEXT)
    part, middle = weight_cut(width_all)
    early, early_counts, common, up_part, down_part = call(
        project_kernel,
        (
            shape_of((group, 3 * width), bf16),
            shape_of((8,), i32),
            shape_of((width + 2 * middle, width_all), bf16),
            shape_of((part, hidden), bf16),
            shape_of((part, width_all), bf16),
        ),
        whole_specs(4) + [SMEM] + whole_specs(3), (VMEM, SMEM) + (VMEM,) * 3, "project", 8,
        scratch=[pltpu.VMEM((rows, 3 * width), bf16)],
    )(qkv_weight, qv_bias, mine, near, place, out_weight, up_weight, down_weight)
    far, up_weight, down_weight, out_weight, common, up_part, down_part = lax.optimization_barrier(
        (far, up_weight, down_weight, out_weight, common, up_part, down_part)
    )
    across = over(far, CORE)
    parts = (mine, near, far, across)

    common_far, down_far, up_far = over(common, NEXT), over(down_part, NEXT), over(up_part, NEXT)
    out_near = over(out_weight, CORE)
    across, up_weight, down_weight, out_near = lax.optimization_barrier((across, up_weight, down_weight, out_near))
    up_near, down_near = over(up_weight, CORE), over(down_weight, CORE)

    att, lse, counts, a0, a1, a2, a3, q_all, k_all, v_all = call(
        attend_kernel,
        (
            shape_of((group, wide), bf16),
            shape_of((8, group), f32),
            shape_of((8,), i32),
        )
        + (shape_of((rows * 3 // 2, 128), bf16),) * 4
        + (shape_of((heads, group, 128), bf16),) * 3,
        whole_specs(2) + [SMEM] + [HBM] * 3, (VMEM, VMEM, SMEM) + (VMEM,) * 4 + (HBM,) * 3, "attend", 40,
        scratch=[
            pltpu.VMEM((2, rows + PAD, width_all), bf16),
            pltpu.VMEM((group, 3 * width), bf16),
            pltpu.VMEM((rows, 3 * width), bf16),
            pltpu.VMEM((heads, group, 128), bf16),
            pltpu.VMEM((heads, group, 128), bf16),
            pltpu.VMEM((heads, group, 128), bf16),
            pltpu.VMEM((2, 2 * group // 3, 512), f32),
            pltpu.SemaphoreType.DMA((3,)),
            pltpu.SemaphoreType.DMA((3,)),
        ],
    )(qkv_weight, qv_bias, early_counts, early, far, across)

    counts, up_far, down_far, up_near, down_near, common_far, pair_weight = lax.optimization_barrier(
        (counts, up_far, down_far, up_near, down_near, common_far, qkv_weight)
    )
    got = [a0, over(a1, CORE), over(a2, NEXT), over(a3, DIAG)]
    down_side, up_side = swap(down_far, rows_size, 1), swap(up_far, rows_size, near_z)
    got[1], common_far, down_far, up_far = lax.optimization_barrier((got[1], common_far, down_far, up_far))
    common_across, down_across, up_across = over(common_far, CORE), over(down_far, CORE), over(up_far, CORE)
    value_weight = pair_weight[2]
    pair_weight = pair_weight[0:2].reshape(2, width_all, heads, HEAD).transpose(1, 2, 0, 3)
    weight_heads = jnp.concatenate(
        [pair_weight.reshape(width_all, heads * 128), jnp.pad(value_weight, ((0, 0), (0, wide - width)))], axis=1
    )
    *got[2:], down_side, up_side, weight_heads = lax.optimization_barrier((*got[2:], down_side, up_side, weight_heads))
    up_side_across, down_side_across = over(up_side, CORE), over(down_side, CORE)

    s0, s1, s2, s3, sums_two, up_b, layer_out, xgrad, agrad, normed_two, attu, act, hid = call(
        middle_kernel,
        (shape_of((rows * 3 // 2, 128), bf16),) * 4
        + (
            shape_of((8, width_all), f32),
            shape_of((4, 8, hidden), f32),
            shape_of((rows, width_all), bf16),
            shape_of((rows, width_all), f32),
            shape_of((rows, width_all), bf16),
            shape_of((rows, width_all), bf16),
            shape_of((rows, 4 * wide), bf16),
            shape_of((4, rows, hidden), bf16),
            shape_of((4, rows, hidden), bf16),
        ),
        [VMEM, VMEM, SMEM] + whole_specs(10) + [SMEM] + [HBM] * 21, (VMEM,) * 6 + (HBM,) * 7, "middle", 32,
        scratch=[
            pltpu.VMEM((rows, width_all), f32),
            pltpu.VMEM((rows, width_all), f32),
            pltpu.VMEM((rows, 4 * wide), bf16),
            pltpu.VMEM((rows, 4 * wide), bf16),
            pltpu.VMEM((4 * wide, width_all), bf16),
            pltpu.VMEM((rows, width_all), bf16),
            pltpu.VMEM((rows, width_all), bf16),
            pltpu.VMEM((rows, width_all), bf16),
            pltpu.VMEM((rows, width_all), bf16),
            pltpu.VMEM((4, PAD, width_all), bf16),
            pltpu.VMEM((4, width_all, hidden), bf16),
            pltpu.VMEM((4, hidden, width_all), bf16),
            pltpu.VMEM((4, rows, hidden), bf16),
            pltpu.VMEM((4, rows, hidden), bf16),
            pltpu.SemaphoreType.DMA((25,)),
            pltpu.SemaphoreType.DMA((13,)),
        ],
    )(
        tokens, frame_id, lead_index, lead_embed, perm, *got, ln2_gain, ln2_bias, out_bias, down_bias, place,
        out_grad, out_weight, out_near, common_far, common_across, *parts, up_weight, up_near, up_far, up_across,
        up_side, up_side_across, down_weight, down_near, down_far, down_across, down_side, down_side_across,
    )

    got_grad = [s0, over(s1, CORE), over(s2, NEXT), over(s3, DIAG)]

    def block_of(step):
        return jnp.where(step < 2, 2 * step + 1, 2 * step - 4)

    def picked(shape):
        return pl.BlockSpec((1,) + shape, lambda s: (block_of(s), 0, 0))

    cut = width_all + width
    first_two, last_two = lambda s: (jnp.minimum(s, 1), 0, 0), lambda s: (jnp.maximum(s - 2, 0), 0, 0)
    up_share, down_share = (1, cut, hidden), (1, hidden, width_all)
    up_send, up_keep, down_send, down_keep = call(
        weight_grad_kernel,
        (shape_of((2, cut, hidden), bf16),) * 2 + (shape_of((2, hidden, width_all), bf16),) * 2,
        [full((rows, width_all))] * 3 + [picked((rows, hidden))] * 2 + [pl.BlockSpec((rows, wide), lambda s: (0, block_of(s)))],
        (
            pl.BlockSpec(up_share, first_two), pl.BlockSpec(up_share, last_two),
            pl.BlockSpec(down_share, first_two), pl.BlockSpec(down_share, last_two),
        ),
        "weight_grad", 18, grid=(4,), scratch=[pltpu.VMEM((width_all, rows), bf16)],
    )(normed_two, out_grad, agrad, act, hid, attu)
    *got_grad[1:], up_send, up_keep, down_send, down_keep = lax.optimization_barrier(
        (*got_grad[1:], up_send, up_keep, down_send, down_keep)
    )
    up_got, down_got = over(up_send, CORE), over(down_send, CORE)
    grad_all, inner = call(
        gather_grad_kernel,
        (shape_of((heads, group, 128), bf16), shape_of((8, group), f32)),
        [SMEM] + whole_specs(5), (VMEM, VMEM), "gather_grad", 6,
        scratch=[pltpu.VMEM((group, wide), bf16), pltpu.VMEM((rows, wide), bf16)],
    )(after(counts, up_send), *got_grad, att)

    up_got = after(up_got, inner)
    (up_keep, up_give), (up_keep_two, up_give_two) = halves(up_keep, 1, 1), halves(up_got, 1, 1)
    up_mine, up_away = add_low(up_keep, up_keep_two), add_low(up_give, up_give_two)
    down_got = after(down_got, up_away)
    down_mine = add_low(down_keep[0], down_got[0])
    down_other = add_low(down_keep[1], down_got[1])
    down_y = over(down_other, NEXT)
    up_x = swap(up_away, rows_size, 1)

    def attend_back(first, count, lse, first_lse, grads):
        spec = pl.BlockSpec((1, group, 128), lambda s: (first + s, 0, 0))
        return call(
            functools.partial(attend_back_kernel, first, first_lse),
            shape_of((count, group, 256), bf16),
            [full((8, group))] * 2 + [spec] * 4,
            pl.BlockSpec((1, group, 256), lambda s: (s, 0, 0)), "attend_back", 15 * count,
            scratch=[pltpu.VMEM((128, group), f32)], grid=(count,),
        )(lse, inner, q_all, k_all, v_all, grads)

    back_01 = attend_back(0, heads - 1, lse, 0, after(grad_all, down_other, up_away, down_mine, up_mine))
    down_y, up_x = after(down_y, back_01), after(up_x, back_01)
    (down_keep, down_give), (down_keep_two, down_give_two) = halves(down_mine, near_z), halves(down_y, near_z)
    down_half_sum, down_away = add_low(down_keep, down_keep_two), add_low(down_give, down_give_two)
    up_half_sum = add_low(up_mine[0], up_x[0])
    up_other = add_low(up_mine[1], up_x[1])
    down_x = swap(down_away, rows_size, near_z)
    up_y = over(up_other, NEXT)
    back_2 = attend_back(heads - 1, 1, lse, heads - 1, after(grad_all, back_01, down_away, up_other, up_half_sum, down_half_sum))
    down_x, up_y = after(down_x, back_2), after(up_y, back_2)
    (down_keep, down_give), (down_keep_two, down_give_two) = halves(down_half_sum, 1), halves(down_x, 1)
    (up_keep, up_give), (up_keep_two, up_give_two) = halves(up_half_sum, near_z), halves(up_y, near_z)
    down_z, down_away = add_low(down_keep, down_keep_two), add_low(down_give, down_give_two)
    up_z, up_away = add_low(up_keep, up_keep_two), add_low(up_give, up_give_two)
    up_got, down_got = swap(up_away, rows_size, near_z), swap(down_away, rows_size, 1)

    def project_back(chosen, counts):
        return call(
            functools.partial(project_back_kernel, chosen),
            (shape_of((2, rows, heads * 128 + wide), bf16),) + (shape_of((rows, width_all), bf16),) * 2,
            [SMEM] + whole_specs(3), (VMEM,) * 3, "project_back", 6,
            scratch=[pltpu.VMEM((TILE, 256), bf16)] * heads,
        )(counts, back_01, back_2, weight_heads)

    local_far, b3, b2 = project_back((3, 2), after(counts, up_away, up_z, down_away, down_z))

    up_got, down_got, b3 = lax.optimization_barrier((up_got, down_got, b3))
    split = down_z.shape[0]
    mixed = jnp.concatenate([add_low(down_z, down_got), add_low(up_z, up_got)], axis=0)

    def over_far_z(value):
        for bit in far_z:
            value = add_low(value, swap(value, rows_size, bit))
        return value

    over_far = over(b3, CORE)
    mixed_z = over_far_z(mixed)
    local_near, b1, b0 = project_back((1, 0), after(counts, mixed, b2))
    over_far, b2, b1 = lax.optimization_barrier((over_far, b2, b1))
    over_near = over(b1, CORE)
    first = rows * 3 // 4
    back_one, back_two = add_low(b2[:first], over_far[:first]), add_low(b2[first:], over_far[first:])
    far_one = over(back_one, NEXT)
    qkv_grad, qkv_sums = call(
        project_grad_kernel,
        (shape_of((width_all, heads * 128 + wide), bf16), shape_of((8, heads * 128 + wide), f32)),
        whole_specs(6), (VMEM, VMEM), "project_grad", 6,
    )(*parts[::-1], after(local_far, back_one), local_near)
    q_keep, q_give = halves(qkv_grad, 1)
    q_got = swap(q_give, rows_size, 1)
    far_one, back_two, mixed, q_got = lax.optimization_barrier((far_one, back_two, mixed_z, q_got))
    far_two = over(back_two, NEXT)
    down_z, up_z = mixed[:split], mixed[split:]
    cut_up = up_z.shape[0] // 2
    up_one, up_two = up_z[:cut_up], up_z[cut_up:]
    down_got = swap(down_z, rows_size, near_z)
    one_got, two_got = swap(up_one, rows_size, 1), swap(after(up_two, down_z), rows_size, near_z)
    q_keep, q_give = halves(after(add_low(q_keep, q_got), down_z), near_z)
    q_got = swap(q_give, rows_size, near_z)
    far_two, down_got = lax.optimization_barrier((far_two, down_got))
    down_z = joined(down_z[None], down_got[None], near_z)
    down_got = swap(down_z, rows_size, 1)

    tokens_grad, small = call(
        last_kernel,
        (shape_of((rows, width_all), f32), shape_of((leads + 16, width_all), bf16)),
        [VMEM, VMEM, SMEM] + whole_specs(11) + [SMEM], (VMEM, VMEM), "last", 7,
    )(
        tokens, frame_id, lead_index, lead_embed, ln1_gain, perm, after(b0, q_give, up_one, up_two, down_z), over_near, far_one, far_two, xgrad,
        sums_two, up_b, qkv_sums, me,
    )

    small, one_got, two_got, q_got = lax.optimization_barrier((small, one_got, two_got, q_got))
    up_one = joined(up_one[None], one_got[None], 1)
    up_two = joined(up_two[None], two_got[None], near_z)
    q_z = add_low(q_keep, q_got)
    q_far = swap(q_z, rows_size, far_z[0])
    two_got = swap(up_two, rows_size, 1)
    small = add_low(small, over(small, CORE))
    small = add_low(small, over(small, NEXT))
    small = add_low(small, swap(small, rows_size, near_z))
    small, q_far = lax.optimization_barrier((small, q_far))
    q_z = add_low(q_z, q_far)
    for bit in far_z[1:]:
        q_z = add_low(q_z, swap(q_z, rows_size, bit))
    q_got = swap(q_z, rows_size, near_z)
    for bit in far_z:
        small = add_low(small, swap(small, rows_size, bit))
    one_got = swap(after(up_one, q_z), rows_size, near_z)
    q_z = joined(q_z, q_got, near_z)
    q_got = swap(q_z, rows_size, 1)
    down_sum = joined(down_z, down_got, 1, 1).astype(f32).reshape(hidden, width_all)
    up_sum, out_sum = call(
        join_kernel,
        (shape_of((width_all, hidden), f32), shape_of((width, hidden), f32)),
        whole_specs(4) + [SMEM], (VMEM, VMEM), "join", 2,
    )(up_one, one_got, up_two, two_got, place)
    qkv_sum = joined(q_z, q_got, 1)

    pairs_sum = qkv_sum[:, 0 : heads * 128].reshape(width_all, heads, 2, HEAD).transpose(2, 0, 1, 3)
    qkv_out = jnp.concatenate(
        [
            pairs_sum.reshape(2, width_all, width),
            qkv_sum[:, heads * 128 : heads * 128 + width].reshape(1, width_all, width),
        ],
        axis=0,
    ).astype(f32)
    vector = shape_of((width_all,), f32)
    lead_sum, g1, b1, g2, b2, out_b, down_b, up_b_sum, qv_sum = call(
        finish_kernel,
        (shape_of((leads, width_all), f32),) + (vector,) * 6 + (shape_of((hidden,), f32), shape_of((2, width), f32)),
        [VMEM, VMEM, SMEM], (VMEM,) * 9, "finish", 1,
    )(small, swap(small, rows_size, 1), me)
    return (
        layer_out, tokens_grad, lead_sum, g1, b1, qkv_out, qv_sum, out_sum, out_b, g2, b2,
        up_sum, up_b_sum, down_sum, down_b,
    )


def solution(mesh):
    rows_size = mesh.shape["rows"]
    split = P(("rows", "tp"), None)
    placed = (
        split, P(("rows", "tp")), P("rows"), P(), P(), P(), P(None, None, "tp"), P(None, "tp"),
        P("tp", None), P(), P(), P(), P(None, "tp"), P("tp"), P("tp", None), P(), split,
    )
    return jax.shard_map(
        functools.partial(on_device, rows_size),
        mesh=mesh,
        in_specs=placed,
        out_specs=(
            split, split, P(), P(), P(), P(None, None, "tp"), P(None, "tp"), P("tp", None), P(), P(), P(),
            P(None, "tp"), P("tp"), P("tp", None), P(),
        ),
        check_vma=False,
    )
```

```python
import functools
import math

import jax
import jax.numpy as jnp
from jax import lax
from jax.experimental import pallas as pl
from jax.experimental.pallas import tpu as pltpu
from jax.sharding import PartitionSpec as P

HEAD = 64
EPS = 1e-05
LOG2E = math.log2(math.e)
LN2 = math.log(2.0)
TILE = 256
PAD = 16
VMEM_LIMIT = 60 * 1024 * 1024

f32 = jnp.float32
bf16 = jnp.bfloat16
i32 = jnp.int32

CORE = ((0, 1), (1, 0), (2, 3), (3, 2))
NEXT = ((0, 2), (2, 0), (1, 3), (3, 1))
DIAG = ((0, 3), (3, 0), (1, 2), (2, 1))

LIMITS = {
    "pre": 60, "project": 60, "attend": 48, "attend_last": 60, "middle": 60, "weight_grad": 60, "gather_grad": 24, "attend_back": 36,
    "project_back": 32, "project_grad": 40, "last": 32, "join": 16, "finish": 8,
}


def iota(shape, axis):
    return lax.broadcasted_iota(i32, shape, axis)


def dot(left, right, dims):
    return lax.dot_general(left, right, (dims, ((), ())), preferred_element_type=f32)


NN = ((1,), (0,))
NT = ((1,), (1,))
TN = ((0,), (0,))


def shape_of(shape, dtype):
    return jax.ShapeDtypeStruct(shape, dtype)


def whole_specs(count):
    return [pl.BlockSpec(memory_space=pltpu.VMEM)] * count


SMEM = pl.BlockSpec(memory_space=pltpu.SMEM)
VMEM = pl.BlockSpec(memory_space=pltpu.VMEM)
HBM = pl.BlockSpec(memory_space=pl.ANY)


def call(body, out_shape, in_specs, out_specs, name, micros, scratch=(), grid=()):
    return pl.pallas_call(
        body,
        out_shape=out_shape,
        grid=grid,
        in_specs=in_specs,
        out_specs=out_specs,
        scratch_shapes=scratch,
        compiler_params=pltpu.CompilerParams(vmem_limit_bytes=LIMITS[name] * 1024 * 1024),
        name=name,
        cost_estimate=pl.CostEstimate(
            flops=int(micros * 1.15e9), bytes_accessed=1024, transcendentals=0
        ),
    )


def local_frame(frame_ref):
    return frame_ref[...].reshape(1, frame_ref.shape[0]) % 2


def row_of(ref):
    return ref[...].astype(f32).reshape(1, ref.shape[0])


def rows_with_lead(tok_ref, frame_ref, lead_ref, table_ref):
    frame = local_frame(frame_ref)
    lead = jnp.where(frame == 0, lead_ref[0], lead_ref[1])
    hot = (iota((table_ref.shape[0], frame.shape[1]), 0) == lead).astype(bf16)
    return tok_ref[...].astype(f32) + dot(hot, table_ref[...], TN), hot


def norm_stats(values):
    average = jnp.mean(values, axis=-1, keepdims=True)
    centred = values - average
    spread = jnp.mean(centred * centred, axis=-1, keepdims=True)
    inverse = lax.rsqrt(spread + EPS)
    return centred * inverse, inverse


def pre_kernel(tok_ref, frame_ref, lead_ref, table_ref, gain_ref, shift_ref, up_bias_ref, out_ref, perm_ref):
    rows = tok_ref.shape[0]
    values, _ = rows_with_lead(tok_ref, frame_ref, lead_ref, table_ref)
    unit, _ = norm_stats(values)
    normed = (unit * row_of(gain_ref) + row_of(shift_ref)).astype(bf16)
    first = (local_frame(frame_ref) == 0).astype(f32)
    before = (iota((rows, rows), 0) < iota((rows, rows), 1)).astype(bf16)
    earlier = dot(jnp.broadcast_to(first, (8, rows)).astype(bf16), before, NN)[0:1]
    count = jnp.sum(first, axis=1, keepdims=True)
    place = jnp.where(first > 0, earlier, count + iota((1, rows), 1).astype(f32) - earlier)
    perm = (iota((rows, rows), 0) == place.astype(i32)).astype(bf16)
    perm_ref[...] = perm
    out_ref[0:rows, :] = dot(perm, normed, NN).astype(bf16)
    high = jnp.floor(count * (1.0 / 16))
    low = count - 16 * high
    tail = iota((PAD, out_ref.shape[1]), 0)
    out_ref[rows : rows + PAD, :] = jnp.where(
        tail == 0, high, jnp.where(tail == 1, low, jnp.where(tail == 2, row_of(up_bias_ref), 0.0))
    ).astype(bf16)


def read_count(block_ref, rows):
    part = block_ref[rows : rows + PAD, 0:128].astype(f32)
    place, lane = iota(part.shape, 0), iota(part.shape, 1)
    worth = jnp.where(place == 0, 16.0, jnp.where(place == 1, 1.0, 0.0))
    return jnp.sum(jnp.where(lane == 0, part * worth, 0.0)).astype(i32)


def tile_moves(counts, rows, block, tile):
    group = 4 * rows
    count = counts[block]
    longs_before = sum(counts[:block], jnp.int32(0))
    limit = jnp.clip(count - tile * TILE, 0, TILE)
    moves = []
    for some, base, low, high in (
        (limit > 0, longs_before + tile * TILE, 0, limit),
        (limit < TILE, 2 * group // 3 + block * rows - longs_before - count + tile * TILE, limit, TILE),
    ):
        spot = jnp.minimum(base // TILE, group // TILE - 2)
        window = pl.ds(pl.multiple_of(spot * TILE, TILE), 2 * TILE)
        moves.append((some, window, base - spot * TILE, low, high))
    return moves


def aligned(index, size):
    return pl.ds(pl.multiple_of(index * size, size), size)


def to_group(value, dst_ref, moves):
    width = value.shape[1]
    for some, window, shift, low, high in moves:

        @pl.when(some)
        def _():
            dest, source = iota((2 * TILE, TILE), 0), iota((2 * TILE, TILE), 1)
            hot = (dest - source == shift) & (source >= low) & (source < high)
            moved = dot(hot.astype(bf16), value, NN).astype(bf16)
            dst_ref[window, 0:width] = dst_ref[window, 0:width] + moved


def from_group(src_refs, acc_refs, moves):
    (some_long, *long), (some_short, *short) = moves

    def moved(window, shift, low, high):
        source, dest = iota((TILE, 2 * TILE), 0), iota((TILE, 2 * TILE), 1)
        hot = ((dest - source == shift) & (source >= low) & (source < high)).astype(bf16)
        return [dot(hot, ref[window, :], NN).astype(bf16) for ref in src_refs]

    @pl.when(some_long)
    def _():
        for ref, value in zip(acc_refs, moved(*long)):
            ref[...] = value

    @pl.when(jnp.logical_not(some_long))
    def _():
        for ref, value in zip(acc_refs, moved(*short)):
            ref[...] = value

    @pl.when(some_long & some_short)
    def _():
        for ref, value in zip(acc_refs, moved(*short)):
            ref[...] = ref[...] + value


def pack_heads(src_ref, out_ref):
    rows = src_ref.shape[0]
    half = rows // 2
    lane = iota((half, 128), 1)
    out_ref[0:rows, :] = src_ref[:, 0:128]
    upper = src_ref[0:half, 128:256].astype(f32)
    lower = pltpu.roll(src_ref[half:rows, 128:256].astype(f32), HEAD, 1)
    out_ref[rows:, :] = jnp.where(lane < HEAD, upper, lower).astype(bf16)


def unpack_heads(src_ref, out_ref):
    rows = out_ref.shape[0]
    half = rows // 2
    lane = iota((half, 128), 1)
    out_ref[:, 0:128] = src_ref[0:rows, :]
    both = src_ref[rows:, :].astype(f32)
    out_ref[0:half, 128:256] = jnp.where(lane < HEAD, both, 0.0).astype(bf16)
    out_ref[half:rows, 128:256] = jnp.where(lane < HEAD, pltpu.roll(both, HEAD, 1), 0.0).astype(bf16)


def head_columns(ref, start, width):
    first = start // 128 * 128
    if first + 128 <= width:
        piece = ref[:, first : first + 128].astype(f32)
    else:
        piece = jnp.concatenate([ref[:, first : first + HEAD].astype(f32)] * 2, axis=1)
    return pltpu.roll(piece, HEAD, 1) if start != first else piece


def project_rows(x_ref, index, counts, weight_ref, bias_ref, value_ref, qkv_ref):
    rows = value_ref.shape[0]
    width = weight_ref.shape[2]
    for part in range(3):
        value = dot(x_ref[0:rows, :], weight_ref[part], NN)
        if part == 0:
            value = (value + bias_ref[0:1, :].astype(f32)) * (LOG2E / math.sqrt(HEAD))
        if part == 2:
            value = value + bias_ref[1:2, :].astype(f32)
        value_ref[:, part * width : (part + 1) * width] = value.astype(bf16)

    def place(tile, _):
        to_group(value_ref[aligned(tile, TILE), :], qkv_ref, tile_moves(counts, rows, index, tile))
        return 0

    lax.fori_loop(0, rows // TILE, place, 0)


def weight_cut(rows):
    part = rows * 3 // 8
    return part, rows - 2 * part


def project_kernel(
    weight_ref, bias_ref, x0_ref, x1_ref, place_ref, out_ref, up_ref, down_ref,
    qkv_ref, counts_ref, common_ref, up_part_ref, down_part_ref, value_ref,
):
    part, middle = weight_cut(up_ref.shape[0])
    first = out_ref.shape[0]
    common_ref[0:first, :] = out_ref[...]
    for index, (ref, part_ref, at) in enumerate(
        ((down_ref, down_part_ref, place_ref[0]), (up_ref, up_part_ref, place_ref[1]))
    ):
        common_ref[first + index * middle : first + (index + 1) * middle, :] = ref[part : part + middle, :]
        part_ref[...] = ref[pl.ds(pl.multiple_of(at * (part + middle), PAD), part), :]
    qkv_ref[...] = jnp.zeros(qkv_ref.shape, qkv_ref.dtype)
    counts = []
    for index, ref in enumerate((x0_ref, x1_ref)):
        counts.append(read_count(ref, value_ref.shape[0]))
        counts_ref[index] = counts[index]
        project_rows(ref, index, counts, weight_ref, bias_ref, value_ref, qkv_ref)


def attend_kernel(
    weight_ref, bias_ref, early_ref, part_ref, x2_ref, x3_ref,
    att_ref, lse_ref, counts_ref, a0_ref, a1_ref, a2_ref, a3_ref, q_out, k_out, v_out,
    x_buf, qkv_ref, value_ref, q_ref, k_ref, v_ref, scores_ref, load_sems, store_sems,
):
    rows = x2_ref.shape[0] - PAD
    group = 4 * rows
    long = 2 * group // 3
    width = weight_ref.shape[2]
    heads = width // HEAD
    loads = [
        pltpu.make_async_copy(source, target, load_sems.at[i])
        for i, (source, target) in enumerate(
            ((part_ref, qkv_ref), (x2_ref, x_buf.at[0]), (x3_ref, x_buf.at[1]))
        )
    ]
    for load in loads:
        load.start()
    loads[0].wait()
    counts = [early_ref[0], early_ref[1]]
    for index in (2, 3):
        loads[index - 1].wait()
        block_ref = x_buf.at[index - 2]
        counts.append(read_count(block_ref, rows))
        project_rows(block_ref, index, counts, weight_ref, bias_ref, value_ref, qkv_ref)
    for index, count in enumerate(counts):
        counts_ref[index] = count
    lane = iota((group, 128), 1)
    stores = []
    for part, ref, out, fill in ((1, k_ref, k_out, 0.0), (2, v_ref, v_out, 1.0), (0, q_ref, q_out, 0.0)):
        for head in range(heads):
            piece = head_columns(qkv_ref, part * width + head * HEAD, 3 * width)
            ref[head] = jnp.where(lane < HEAD, piece, fill).astype(bf16)
        store = pltpu.make_async_copy(ref, out, store_sems.at[part])
        store.start()
        stores.append(store)

    block = 512
    row = iota((128, block), 0)
    half = iota((block, 128), 1)
    tasks = [
        (head, first, low, high)
        for low, high in ((0, long), (long, group))
        for first in range(low, high, block)
        for head in range(heads)
    ]

    def scores(task, part):
        head, first, low, high = tasks[task]
        keys = slice(low + part * block, low + (part + 1) * block)
        value = dot(k_ref[head, keys, :], q_ref[head, first : first + block, :], NT)
        scores_ref[task % 2, part * block : (part + 1) * block, :] = value
        return jnp.max(value.reshape(block // 8, 8, block), axis=0)

    def parts_of(task):
        return (tasks[task][3] - tasks[task][2]) // block if task < len(tasks) else 0

    largest = functools.reduce(jnp.maximum, [scores(0, part) for part in range(parts_of(0))])
    outs = []
    for task, (head, first, low, high) in enumerate(tasks):
        top = jnp.max(largest, axis=0, keepdims=True)
        following, mixed = [], None
        for part in range(max(parts_of(task), parts_of(task + 1))):
            if part < parts_of(task + 1):
                following.append(scores(task + 1, part))
            if part < parts_of(task):
                raised = jnp.exp2(scores_ref[task % 2, part * block : (part + 1) * block, :] - top)
                keys = slice(low + part * block, low + (part + 1) * block)
                value = dot(v_ref[head, keys, :], raised.astype(bf16), TN)
                mixed = value if mixed is None else mixed + value
        if following:
            largest = functools.reduce(jnp.maximum, following)
        totals = mixed[HEAD : HEAD + 1, :]
        lse_ref[head : head + 1, first : first + block] = top + jnp.log2(totals)
        outs.append(jnp.where(row < HEAD, mixed / totals, 0.0))
        if head == heads - 1:
            for pair in range((heads + 1) // 2):
                value = outs[2 * pair].T
                if 2 * pair + 1 < heads:
                    value = value + pltpu.roll(outs[2 * pair + 1].T, HEAD, 1)
                att_ref[first : first + block, pair * 128 : (pair + 1) * 128] = value.astype(bf16)
            outs = []
    for index, out in enumerate((a0_ref, a1_ref, a2_ref, a3_ref)):

        def hand_back(tile, _, index=index):
            moves = tile_moves(counts, rows, index, tile)
            from_group((att_ref,), (qkv_ref.at[aligned(tile, TILE), 0 : att_ref.shape[1]],), moves)
            return 0

        lax.fori_loop(0, rows // TILE, hand_back, 0)
        pack_heads(qkv_ref.at[0:rows, 0 : att_ref.shape[1]], out)
    for store in stores:
        store.wait()


def middle_kernel(
    tok_ref, frame_ref, lead_ref, table_ref, perm_ref,
    at0_ref, at1_ref, at2_ref, at3_ref,
    gain_ref, shift_ref, out_bias_ref, down_bias_ref, place_ref,
    og_in, wo0_ref, wo1_ref, common2_ref, common3_ref,
    x0_ref, x1_ref, x2_ref, x3_ref, up0_ref, up1_ref, up2_ref, up3_ref,
    ux2_ref, ux3_ref, dn0_ref, dn1_ref, dn2_ref, dn3_ref, dx2_ref, dx3_ref,
    s0_ref, s1_ref, s2_ref, s3_ref, sums_ref, upb_ref,
    layer_out, xgrad_out, agrad_out, normed_out, attu_out, act_out, hid_out,
    y_ref, back_ref, at_ref, attu_ref, wo_ref, og_ref, normed_ref, layer_ref, agrad_ref, bias_buf, up_buf, dn_buf,
    act_ref, hid_ref, load_sems, store_sems,
):
    ats = (at0_ref, at1_ref, at2_ref, at3_ref)
    blocks = (x0_ref, x1_ref, x2_ref, x3_ref)
    sends = (s0_ref, s1_ref, s2_ref, s3_ref)
    rows, wide = tok_ref.shape
    hidden = up_buf.shape[2]
    width = wo0_ref.shape[0]
    span = wo_ref.shape[0] // 4
    part, middle = weight_cut(hidden)
    x, z = place_ref[0], place_ref[1]
    mine, other = (pl.ds(pl.multiple_of(at * (part + middle), PAD), part) for at in (x, 1 - x))
    up_mine, up_other = (pl.ds(pl.multiple_of(at * (part + middle), PAD), part) for at in (z, 1 - z))
    both = pl.ds(part, middle)
    wos = (wo0_ref, wo1_ref, common2_ref.at[0:width], common3_ref.at[0:width])
    first_loads = [
        pltpu.make_async_copy(wos[i], wo_ref.at[i * span : i * span + width], load_sems.at[14 + i]) for i in range(4)
    ]
    loads = [[], [], [], []]
    loads[0].append(pltpu.make_async_copy(og_in, og_ref, load_sems.at[18]))
    for index, ref, target, sem in (
        (0, up0_ref, up_buf.at[0], 0),
        (1, up1_ref, up_buf.at[1], 1),
        (2, common2_ref.at[width : width + middle], dn_buf.at[2, both], 21),
        (3, common3_ref.at[width : width + middle], dn_buf.at[3, both], 22),
        (2, common2_ref.at[width + middle :], up_buf.at[2, both], 23),
        (3, common3_ref.at[width + middle :], up_buf.at[3, both], 24),
        (2, up2_ref, up_buf.at[2, up_mine], 2),
        (2, ux2_ref, up_buf.at[2, up_other], 19),
        (3, up3_ref, up_buf.at[3, up_mine], 3),
        (3, ux3_ref, up_buf.at[3, up_other], 20),
        (0, dn0_ref, dn_buf.at[0], 4),
        (1, dn1_ref, dn_buf.at[1], 5),
        (2, dn2_ref, dn_buf.at[2, mine], 6),
        (2, dx2_ref, dn_buf.at[2, other], 7),
        (3, dn3_ref, dn_buf.at[3, mine], 8),
        (3, dx3_ref, dn_buf.at[3, other], 9),
    ):
        loads[index].append(pltpu.make_async_copy(ref, target, load_sems.at[sem]))
    for index in range(4):
        tail = blocks[index].at[rows : rows + PAD]
        loads[index].append(pltpu.make_async_copy(tail, bias_buf.at[index], load_sems.at[10 + index]))
    for load in first_loads + sum(loads, []):
        load.start()
    stores = []

    def store(source, target):
        copy = pltpu.make_async_copy(source, target, store_sems.at[len(stores)])
        copy.start()
        stores.append(copy)

    gain = row_of(gain_ref)
    perm = perm_ref[...]
    for index in range(4):
        unpack_heads(ats[index], at_ref.at[:, index * span : (index + 1) * span])
        wo_ref[index * span + width : (index + 1) * span, :] = jnp.zeros((span - width, wide), bf16)
    attu_ref[...] = dot(perm, at_ref[...], TN).astype(bf16)
    store(attu_ref, attu_out)
    values, _ = rows_with_lead(tok_ref, frame_ref, lead_ref, table_ref)
    for load in first_loads:
        load.wait()
    x_one = values + row_of(out_bias_ref) + dot(attu_ref[...], wo_ref[...], NN)
    unit, inverse = norm_stats(x_one)
    normed_ref[...] = (unit * gain + row_of(shift_ref)).astype(bf16)
    store(normed_ref, normed_out)
    y_ref[...] = x_one + row_of(down_bias_ref)
    for index in range(4):
        for load in loads[index]:
            load.wait()
        up = up_buf[index]
        down = dn_buf[index]
        h = dot(normed_ref[...], up, NN) + bias_buf[index][2:3].astype(f32)
        g = dot(og_ref[...], down, NT)
        c = math.sqrt(2.0 / math.pi)
        h2 = h * h
        t = jnp.tanh(h * (c + (c * 0.044715) * h2))
        half = 0.5 + 0.5 * t
        act = h * half
        slope = half + act * (1.0 - t) * (c + (3 * c * 0.044715) * h2)
        hid = (slope * g).astype(bf16)
        actb = act.astype(bf16)
        act_ref[index] = actb
        hid_ref[index] = hid
        upb_ref[index] = jnp.broadcast_to(jnp.sum(hid.astype(f32), axis=0, keepdims=True), (8, hidden))
        if index < 3:
            y_ref[...] += dot(actb, down, NN)
        else:
            layer_ref[...] = (y_ref[...] + dot(actb, down, NN)).astype(bf16)
            store(layer_ref, layer_out)
        if index == 0:
            back_ref[...] = dot(hid, up, NT)
        else:
            back_ref[...] += dot(hid, up, NT)
        store(act_ref.at[index], act_out.at[index])
        store(hid_ref.at[index], hid_out.at[index])
    grad = back_ref[...]
    e = grad * gain
    spread_mean = jnp.mean(e, axis=-1, keepdims=True)
    along = jnp.mean(e * unit, axis=-1, keepdims=True)
    og = og_ref[...].astype(f32)
    xgrad = og + inverse * (e - spread_mean - unit * along)
    y_ref[...] = xgrad
    store(y_ref, xgrad_out)
    agrad = xgrad.astype(bf16)
    agrad_ref[...] = agrad
    store(agrad_ref, agrad_out)
    at_ref[...] = dot(agrad, wo_ref[...], NT).astype(bf16)
    at_ref[...] = dot(perm, at_ref[...], NN).astype(bf16)
    for index in range(4):
        pack_heads(at_ref.at[:, index * span : (index + 1) * span], sends[index])
    sums_ref[...] = jnp.concatenate(
        [
            jnp.sum(grad * unit, axis=0, keepdims=True),
            jnp.sum(grad, axis=0, keepdims=True),
            jnp.sum(agrad.astype(f32), axis=0, keepdims=True),
            jnp.sum(og, axis=0, keepdims=True),
            jnp.zeros((4, og.shape[1]), f32),
        ],
        axis=0,
    )
    for copy in stores:
        copy.wait()


def weight_grad_kernel(
    normed_ref, og_ref, agrad_ref, act_ref, hid_ref, attu_ref, up_send_ref, up_keep_ref, down_send_ref, down_keep_ref,
    turned_ref,
):
    @pl.when(pl.program_id(0) == 0)
    def _():
        turned_ref[...] = normed_ref[...].T

    up = dot(turned_ref[...], hid_ref[0], NN).astype(bf16)
    out = dot(attu_ref[...], agrad_ref[...], TN).astype(bf16)[0 : up_send_ref.shape[1] - up.shape[0]]
    down = dot(act_ref[0], og_ref[...], TN).astype(bf16)
    rows = up.shape[0]
    step = pl.program_id(0)
    for chosen, up_ref, down_ref in (
        (step < 2, up_send_ref, down_send_ref), (step >= 2, up_keep_ref, down_keep_ref),
    ):

        @pl.when(chosen)
        def _(up_ref=up_ref, down_ref=down_ref):
            up_ref[0, 0:rows, :] = up
            up_ref[0, rows:, :] = out
            down_ref[0] = down


def gather_grad_kernel(counts_ref, b0_ref, b1_ref, b2_ref, b3_ref, att_ref, out_ref, inner_ref, sorted_ref, block_ref):
    blocks = (b0_ref, b1_ref, b2_ref, b3_ref)
    rows = block_ref.shape[0]
    group = 4 * rows
    heads = out_ref.shape[0]
    counts = [counts_ref[i] for i in range(4)]
    sorted_ref[...] = jnp.zeros(sorted_ref.shape, sorted_ref.dtype)
    for index, ref in enumerate(blocks):

        unpack_heads(ref, block_ref)

        def place(tile, _, index=index):
            to_group(block_ref[aligned(tile, TILE), :], sorted_ref, tile_moves(counts, rows, index, tile))
            return 0

        lax.fori_loop(0, rows // TILE, place, 0)
    lane = iota((group, 128), 1)
    pick_row, pick_lane = iota((8, 128), 0), iota((8, 128), 1)
    inner_ref[...] = jnp.zeros(inner_ref.shape, f32)
    for pair in range((heads + 1) // 2):
        columns = slice(pair * 128, (pair + 1) * 128)
        grad = sorted_ref[:, columns].astype(f32)
        product = grad * att_ref[:, columns].astype(f32)
        high = product.astype(bf16)
        low = (product - high.astype(f32)).astype(bf16)
        pick = (pick_row == 2 * pair + pick_lane // HEAD).astype(bf16)
        inner_ref[...] += dot(pick, high, NT) + dot(pick, low, NT)
        out_ref[2 * pair] = jnp.where(lane < HEAD, grad, 0.0).astype(bf16)
        if 2 * pair + 1 < heads:
            out_ref[2 * pair + 1] = jnp.where(lane < HEAD, pltpu.roll(grad, HEAD, 1), 0.0).astype(bf16)


def attend_back_kernel(first_head, first_lse, lse_ref, inner_ref, q_ref, k_ref, v_ref, g_ref, out_ref, dq_ref):
    group = q_ref.shape[1]
    long = 2 * group // 3
    block = 1024
    lane = iota((block, 128), 1)
    head = first_head + pl.program_id(0)
    lse = jnp.sum(jnp.where(iota(lse_ref.shape, 0) == first_lse + pl.program_id(0), lse_ref[...], 0.0), axis=0, keepdims=True)
    inner = jnp.sum(jnp.where(iota(inner_ref.shape, 0) == head, inner_ref[...], 0.0), axis=0, keepdims=True)
    done = set()
    for low, high in ((0, long), (long, group)):
        for keys in range(low, high, block):
            key = k_ref[0, keys : keys + block, :]
            value = v_ref[0, keys : keys + block, :]
            key_grad, value_grad = None, None
            for queries in range(low, high, block):
                query = q_ref[0, queries : queries + block, :]
                grad = g_ref[0, queries : queries + block, :]
                probs = jnp.exp2(dot(key, query, NT) - lse[:, queries : queries + block])
                inside = dot(value, grad, NT) - inner[:, queries : queries + block]
                score_grad = (probs * inside).astype(bf16)
                value_part = dot(probs.astype(bf16), grad, NN)
                key_part = dot(score_grad, query, NN)
                query_part = dot(key, score_grad, TN)
                value_grad = value_part if value_grad is None else value_grad + value_part
                key_grad = key_part if key_grad is None else key_grad + key_part
                place = (slice(None), slice(queries, queries + block))
                dq_ref[place] = query_part if queries not in done else dq_ref[place] + query_part
                done.add(queries)
            out_ref[0, keys : keys + block, 0:128] = pltpu.roll(key_grad * LN2, HEAD, 1).astype(bf16)
            out_ref[0, keys : keys + block, 128:256] = value_grad.astype(bf16)
    wide = iota((group, 128), 1)
    query_grad = dq_ref[...].T * (1.0 / math.sqrt(HEAD))
    pair = jnp.where(wide < HEAD, query_grad, out_ref[0, :, 0:128].astype(f32))
    out_ref[0, :, 0:128] = pair.astype(bf16)


def project_back_kernel(chosen, counts_ref, h01_ref, h2_ref, weight_ref, local_ref, one_ref, two_ref, *acc_refs):
    refs = [h01_ref.at[i] for i in range(h01_ref.shape[0])] + [h2_ref.at[i] for i in range(h2_ref.shape[0])]
    rows = local_ref.shape[1]
    counts = [counts_ref[i] for i in range(4)]
    pairs = len(refs) * 128
    lane = iota((TILE, 128), 1)
    for slot, (index, back_ref) in enumerate(zip(chosen, (one_ref, two_ref))):

        def step(tile, _, index=index, slot=slot):
            here = aligned(tile, TILE)
            from_group(refs, acc_refs, tile_moves(counts, rows, index, tile))
            for head, ref in enumerate(acc_refs):
                local_ref[slot, here, head * 128 : (head + 1) * 128] = ref[:, 0:128]
            for pair in range((len(refs) + 1) // 2):
                value = acc_refs[2 * pair][:, 128:256]
                if 2 * pair + 1 < len(refs):
                    other = acc_refs[2 * pair + 1][:, 128:256].astype(f32)
                    value = jnp.where(lane < HEAD, value.astype(f32), pltpu.roll(other, HEAD, 1)).astype(bf16)
                first = pairs + pair * 128
                local_ref[slot, here, first : first + 128] = value
            return 0

        lax.fori_loop(0, rows // TILE, step, 0)
        back_ref[...] = dot(local_ref[slot], weight_ref[...], NT).astype(bf16)


def project_grad_kernel(x3_ref, x2_ref, x1_ref, x0_ref, far_ref, near_ref, out_ref, sums_ref):
    rows = far_ref.shape[1]
    total, sums = None, None
    for ref, local_ref, slot in (
        (x3_ref, far_ref, 0), (x2_ref, far_ref, 1), (x1_ref, near_ref, 0), (x0_ref, near_ref, 1)
    ):
        value = local_ref[slot]
        part = dot(ref[0:rows, :], value, TN)
        total = part if total is None else total + part
        one = jnp.sum(value.astype(f32), axis=0, keepdims=True)
        sums = one if sums is None else sums + one
    out_ref[...] = total.astype(bf16)
    sums_ref[...] = jnp.broadcast_to(sums, sums_ref.shape)


def last_kernel(
    tok_ref, frame_ref, lead_ref, table_ref, gain_ref, perm_ref, mine_ref, near_ref, one_ref, more_ref, xgrad_ref,
    two_ref, upb_ref, qkv_ref, me_ref, out_ref, sums_ref,
):
    values, hot = rows_with_lead(tok_ref, frame_ref, lead_ref, table_ref)
    unit, inverse = norm_stats(values)
    other = jnp.concatenate([one_ref[...], more_ref[...]], axis=0)
    local = (mine_ref[...].astype(f32) + near_ref[...].astype(f32) + other.astype(f32)).astype(bf16)
    grad = dot(perm_ref[...], local, TN)
    e = grad * row_of(gain_ref)
    mean_e = jnp.mean(e, axis=-1, keepdims=True)
    along = jnp.mean(e * unit, axis=-1, keepdims=True)
    out = xgrad_ref[...] + inverse * (e - mean_e - unit * along)
    out_ref[...] = out
    leads = table_ref.shape[0]
    one = out.astype(bf16)
    rest = out - one.astype(f32)
    two = rest.astype(bf16)
    three = (rest - two.astype(f32)).astype(bf16)
    sums_ref[0:leads, :] = (dot(hot, one, NN) + dot(hot, two, NN) + dot(hot, three, NN)).astype(bf16)
    row = iota((16, grad.shape[1]), 0)
    me = me_ref[0]
    small = jnp.zeros((16, grad.shape[1]), f32)
    small = jnp.where(row == 0, jnp.sum(grad * unit, axis=0, keepdims=True), small)
    small = jnp.where(row == 1, jnp.sum(grad, axis=0, keepdims=True), small)
    for i in range(4):
        small = jnp.where(row == 2 + i, two_ref[i : i + 1, :], small)
        small = jnp.where(row == 6 + (me ^ i), upb_ref[i, 0:1, :], small)
    heads = (qkv_ref.shape[1] * 2 // 128) // 3
    bias = [qkv_ref[0:1, head * 128 : head * 128 + HEAD] for head in range(heads)]
    bias.append(qkv_ref[0:1, heads * 128 : heads * 128 + heads * HEAD])
    bias.append(jnp.zeros((1, grad.shape[1] - 2 * heads * HEAD), f32))
    small = jnp.where(row == 10 + me, jnp.concatenate(bias, axis=1), small)
    sums_ref[leads : leads + 16, :] = small.astype(bf16)


def finish_kernel(left_ref, right_ref, me_ref, lead_ref, g1_ref, b1_ref, g2_ref, b2_ref, ob_ref, db_ref, ub_ref, qv_ref):
    total = left_ref[...].astype(f32) + right_ref[...].astype(f32)
    leads = lead_ref.shape[0]
    lead_ref[...] = total[0:leads]
    for place, ref in enumerate((g1_ref, b1_ref, g2_ref, b2_ref, ob_ref, db_ref)):
        ref[...] = total[leads + place].reshape(ref.shape)
    me = me_ref[0]
    up, qv = total[leads + 6 : leads + 7], total[leads + 10 : leads + 11]
    for i in range(1, 4):
        up = jnp.where(me == i, total[leads + 6 + i : leads + 7 + i], up)
        qv = jnp.where(me == i, total[leads + 10 + i : leads + 11 + i], qv)
    ub_ref[...] = up.reshape(ub_ref.shape)
    width = qv_ref.shape[1]
    qv_ref[...] = jnp.concatenate([qv[:, 0:width], qv[:, width : 2 * width]], axis=0)


def join_kernel(one_ref, one_got_ref, two_ref, two_got_ref, place_ref, up_ref, out_ref):
    cut, rows = up_ref.shape[0], one_ref.shape[1]
    x, z = place_ref[0], place_ref[1]
    for at_x in range(2):
        for at_z in range(2):
            one = jnp.where(z == at_z, one_ref[at_x].astype(f32), one_got_ref[at_x].astype(f32))
            two = jnp.where(x == at_x, two_ref[at_z].astype(f32), two_got_ref[at_z].astype(f32))
            for part, value in enumerate((one, two)):
                first = ((2 * at_x + at_z) * 2 + part) * rows
                inside = min(max(cut - first, 0), rows)
                if inside:
                    up_ref[first : first + inside, :] = value[:inside]
                if inside < rows:
                    start = max(first - cut, 0)
                    out_ref[start : start + rows - inside, :] = value[inside:]


def bits_of(size):
    bits = []
    step = 1
    while step < size:
        bits.append(step)
        step *= 2
    return bits


def after(value, *others):
    return lax.optimization_barrier((value, *others))[0]


def swap(value, size, bit):
    return lax.ppermute(value, "rows", [(i, i ^ bit) for i in range(size)])


def add_low(left, right):
    return (left.astype(f32) + right.astype(f32)).astype(bf16)


def halves(value, bit, axis=0):
    half = value.shape[axis] // 2
    high = (lax.axis_index("rows") // bit) % 2
    return (
        lax.dynamic_slice_in_dim(value, high * half, half, axis),
        lax.dynamic_slice_in_dim(value, (1 - high) * half, half, axis),
    )


def joined(mine, other, bit, axis=0):
    high = (lax.axis_index("rows") // bit) % 2
    low_part, high_part = jnp.where(high == 1, other, mine), jnp.where(high == 1, mine, other)
    return jnp.concatenate([low_part, high_part], axis)


def on_device(
    rows_size,
    tokens, frame_id, lead_index, lead_embed, ln1_gain, ln1_bias, qkv_weight, qv_bias,
    out_weight, out_bias, ln2_gain, ln2_bias, up_weight, up_bias, down_weight, down_bias, out_grad,
):
    rows, width_all = tokens.shape
    width = qkv_weight.shape[2]
    heads = width // HEAD
    hidden = up_weight.shape[1]
    leads = lead_embed.shape[0]
    group = 4 * rows
    wide = (heads + 1) // 2 * 128
    bits = bits_of(rows_size)
    me = lax.axis_index("tp").reshape(1)
    near_z, far_z = bits[1], bits[2:]
    place = jnp.stack([lax.axis_index("rows") % 2, lax.axis_index("rows") // near_z % 2])

    def over(value, ring):
        return lax.ppermute(value, "tp", ring)

    def full(shape):
        return pl.BlockSpec(shape, lambda s: (0,) * len(shape))

    mine, perm = call(
        pre_kernel,
        (shape_of((rows + PAD, width_all), bf16), shape_of((rows, rows), bf16)),
        [VMEM, VMEM, SMEM, VMEM, VMEM, VMEM, VMEM], (VMEM, VMEM), "pre", 5,
    )(tokens, frame_id, lead_index, lead_embed, ln1_gain, ln1_bias, up_bias)
    near = over(mine, CORE)
    far = over(mine, NEXT)
    part, middle = weight_cut(width_all)
    early, early_counts, common, up_part, down_part = call(
        project_kernel,
        (
            shape_of((group, 3 * width), bf16),
            shape_of((8,), i32),
            shape_of((width + 2 * middle, width_all), bf16),
            shape_of((part, hidden), bf16),
            shape_of((part, width_all), bf16),
        ),
        whole_specs(4) + [SMEM] + whole_specs(3), (VMEM, SMEM) + (VMEM,) * 3, "project", 8,
        scratch=[pltpu.VMEM((rows, 3 * width), bf16)],
    )(qkv_weight, qv_bias, mine, near, place, out_weight, up_weight, down_weight)
    far, up_weight, down_weight, out_weight, common, up_part, down_part = lax.optimization_barrier(
        (far, up_weight, down_weight, out_weight, common, up_part, down_part)
    )
    across = over(far, CORE)
    parts = (mine, near, far, across)

    common_far, down_far, up_far = over(common, NEXT), over(down_part, NEXT), over(up_part, NEXT)
    out_near = over(out_weight, CORE)
    across, up_weight, down_weight, out_near = lax.optimization_barrier((across, up_weight, down_weight, out_near))
    up_near, down_near = over(up_weight, CORE), over(down_weight, CORE)

    att, lse, counts, a0, a1, a2, a3, q_all, k_all, v_all = call(
        attend_kernel,
        (
            shape_of((group, wide), bf16),
            shape_of((8, group), f32),
            shape_of((8,), i32),
        )
        + (shape_of((rows * 3 // 2, 128), bf16),) * 4
        + (shape_of((heads, group, 128), bf16),) * 3,
        whole_specs(2) + [SMEM] + [HBM] * 3, (VMEM, VMEM, SMEM) + (VMEM,) * 4 + (HBM,) * 3, "attend", 40,
        scratch=[
            pltpu.VMEM((2, rows + PAD, width_all), bf16),
            pltpu.VMEM((group, 3 * width), bf16),
            pltpu.VMEM((rows, 3 * width), bf16),
            pltpu.VMEM((heads, group, 128), bf16),
            pltpu.VMEM((heads, group, 128), bf16),
            pltpu.VMEM((heads, group, 128), bf16),
            pltpu.VMEM((2, 2 * group // 3, 512), f32),
            pltpu.SemaphoreType.DMA((3,)),
            pltpu.SemaphoreType.DMA((3,)),
        ],
    )(qkv_weight, qv_bias, early_counts, early, far, across)

    counts, up_far, down_far, up_near, down_near, common_far, pair_weight = lax.optimization_barrier(
        (counts, up_far, down_far, up_near, down_near, common_far, qkv_weight)
    )
    got = [a0, over(a1, CORE), over(a2, NEXT), over(a3, DIAG)]
    down_side, up_side = swap(down_far, rows_size, 1), swap(up_far, rows_size, near_z)
    got[1], common_far, down_far, up_far = lax.optimization_barrier((got[1], common_far, down_far, up_far))
    common_across, down_across, up_across = over(common_far, CORE), over(down_far, CORE), over(up_far, CORE)
    value_weight = pair_weight[2]
    pair_weight = pair_weight[0:2].reshape(2, width_all, heads, HEAD).transpose(1, 2, 0, 3)
    weight_heads = jnp.concatenate(
        [pair_weight.reshape(width_all, heads * 128), jnp.pad(value_weight, ((0, 0), (0, wide - width)))], axis=1
    )
    *got[2:], down_side, up_side, weight_heads = lax.optimization_barrier((*got[2:], down_side, up_side, weight_heads))
    up_side_across, down_side_across = over(up_side, CORE), over(down_side, CORE)

    s0, s1, s2, s3, sums_two, up_b, layer_out, xgrad, agrad, normed_two, attu, act, hid = call(
        middle_kernel,
        (shape_of((rows * 3 // 2, 128), bf16),) * 4
        + (
            shape_of((8, width_all), f32),
            shape_of((4, 8, hidden), f32),
            shape_of((rows, width_all), bf16),
            shape_of((rows, width_all), f32),
            shape_of((rows, width_all), bf16),
            shape_of((rows, width_all), bf16),
            shape_of((rows, 4 * wide), bf16),
            shape_of((4, rows, hidden), bf16),
            shape_of((4, rows, hidden), bf16),
        ),
        [VMEM, VMEM, SMEM] + whole_specs(10) + [SMEM] + [HBM] * 21, (VMEM,) * 6 + (HBM,) * 7, "middle", 32,
        scratch=[
            pltpu.VMEM((rows, width_all), f32),
            pltpu.VMEM((rows, width_all), f32),
            pltpu.VMEM((rows, 4 * wide), bf16),
            pltpu.VMEM((rows, 4 * wide), bf16),
            pltpu.VMEM((4 * wide, width_all), bf16),
            pltpu.VMEM((rows, width_all), bf16),
            pltpu.VMEM((rows, width_all), bf16),
            pltpu.VMEM((rows, width_all), bf16),
            pltpu.VMEM((rows, width_all), bf16),
            pltpu.VMEM((4, PAD, width_all), bf16),
            pltpu.VMEM((4, width_all, hidden), bf16),
            pltpu.VMEM((4, hidden, width_all), bf16),
            pltpu.VMEM((4, rows, hidden), bf16),
            pltpu.VMEM((4, rows, hidden), bf16),
            pltpu.SemaphoreType.DMA((25,)),
            pltpu.SemaphoreType.DMA((13,)),
        ],
    )(
        tokens, frame_id, lead_index, lead_embed, perm, *got, ln2_gain, ln2_bias, out_bias, down_bias, place,
        out_grad, out_weight, out_near, common_far, common_across, *parts, up_weight, up_near, up_far, up_across,
        up_side, up_side_across, down_weight, down_near, down_far, down_across, down_side, down_side_across,
    )

    got_grad = [s0, over(s1, CORE), over(s2, NEXT), over(s3, DIAG)]

    def block_of(step):
        return jnp.where(step < 2, 2 * step + 1, 2 * step - 4)

    def picked(shape):
        return pl.BlockSpec((1,) + shape, lambda s: (block_of(s), 0, 0))

    cut = width_all + width
    first_two, last_two = lambda s: (jnp.minimum(s, 1), 0, 0), lambda s: (jnp.maximum(s - 2, 0), 0, 0)
    up_share, down_share = (1, cut, hidden), (1, hidden, width_all)
    up_send, up_keep, down_send, down_keep = call(
        weight_grad_kernel,
        (shape_of((2, cut, hidden), bf16),) * 2 + (shape_of((2, hidden, width_all), bf16),) * 2,
        [full((rows, width_all))] * 3 + [picked((rows, hidden))] * 2 + [pl.BlockSpec((rows, wide), lambda s: (0, block_of(s)))],
        (
            pl.BlockSpec(up_share, first_two), pl.BlockSpec(up_share, last_two),
            pl.BlockSpec(down_share, first_two), pl.BlockSpec(down_share, last_two),
        ),
        "weight_grad", 18, grid=(4,), scratch=[pltpu.VMEM((width_all, rows), bf16)],
    )(normed_two, out_grad, agrad, act, hid, attu)
    *got_grad[1:], up_send, up_keep, down_send, down_keep = lax.optimization_barrier(
        (*got_grad[1:], up_send, up_keep, down_send, down_keep)
    )
    up_got, down_got = over(up_send, CORE), over(down_send, CORE)
    grad_all, inner = call(
        gather_grad_kernel,
        (shape_of((heads, group, 128), bf16), shape_of((8, group), f32)),
        [SMEM] + whole_specs(5), (VMEM, VMEM), "gather_grad", 6,
        scratch=[pltpu.VMEM((group, wide), bf16), pltpu.VMEM((rows, wide), bf16)],
    )(after(counts, up_send), *got_grad, att)

    up_got = after(up_got, inner)
    (up_keep, up_give), (up_keep_two, up_give_two) = halves(up_keep, 1, 1), halves(up_got, 1, 1)
    up_mine, up_away = add_low(up_keep, up_keep_two), add_low(up_give, up_give_two)
    down_got = after(down_got, up_away)
    down_mine = add_low(down_keep[0], down_got[0])
    down_other = add_low(down_keep[1], down_got[1])
    down_y = over(down_other, NEXT)
    up_x = swap(up_away, rows_size, 1)

    def attend_back(first, count, lse, first_lse, grads):
        spec = pl.BlockSpec((1, group, 128), lambda s: (first + s, 0, 0))
        return call(
            functools.partial(attend_back_kernel, first, first_lse),
            shape_of((count, group, 256), bf16),
            [full((8, group))] * 2 + [spec] * 4,
            pl.BlockSpec((1, group, 256), lambda s: (s, 0, 0)), "attend_back", 15 * count,
            scratch=[pltpu.VMEM((128, group), f32)], grid=(count,),
        )(lse, inner, q_all, k_all, v_all, grads)

    back_01 = attend_back(0, heads - 1, lse, 0, after(grad_all, down_other, up_away, down_mine, up_mine))
    down_y, up_x = after(down_y, back_01), after(up_x, back_01)
    (down_keep, down_give), (down_keep_two, down_give_two) = halves(down_mine, near_z), halves(down_y, near_z)
    down_half_sum, down_away = add_low(down_keep, down_keep_two), add_low(down_give, down_give_two)
    up_half_sum = add_low(up_mine[0], up_x[0])
    up_other = add_low(up_mine[1], up_x[1])
    down_x = swap(down_away, rows_size, near_z)
    up_y = over(up_other, NEXT)
    back_2 = attend_back(heads - 1, 1, lse, heads - 1, after(grad_all, back_01, down_away, up_other, up_half_sum, down_half_sum))
    down_x, up_y = after(down_x, back_2), after(up_y, back_2)
    (down_keep, down_give), (down_keep_two, down_give_two) = halves(down_half_sum, 1), halves(down_x, 1)
    (up_keep, up_give), (up_keep_two, up_give_two) = halves(up_half_sum, near_z), halves(up_y, near_z)
    down_z, down_away = add_low(down_keep, down_keep_two), add_low(down_give, down_give_two)
    up_z, up_away = add_low(up_keep, up_keep_two), add_low(up_give, up_give_two)
    up_got, down_got = swap(up_away, rows_size, near_z), swap(down_away, rows_size, 1)

    def project_back(chosen, counts):
        return call(
            functools.partial(project_back_kernel, chosen),
            (shape_of((2, rows, heads * 128 + wide), bf16),) + (shape_of((rows, width_all), bf16),) * 2,
            [SMEM] + whole_specs(3), (VMEM,) * 3, "project_back", 6,
            scratch=[pltpu.VMEM((TILE, 256), bf16)] * heads,
        )(counts, back_01, back_2, weight_heads)

    local_far, b3, b2 = project_back((3, 2), after(counts, up_away, up_z, down_away, down_z))

    up_got, down_got, b3 = lax.optimization_barrier((up_got, down_got, b3))
    split = down_z.shape[0]
    mixed = jnp.concatenate([add_low(down_z, down_got), add_low(up_z, up_got)], axis=0)

    def over_far_z(value):
        for bit in far_z:
            value = add_low(value, swap(value, rows_size, bit))
        return value

    over_far = over(b3, CORE)
    mixed_z = over_far_z(mixed)
    local_near, b1, b0 = project_back((1, 0), after(counts, mixed, b2))
    over_far, b2, b1 = lax.optimization_barrier((over_far, b2, b1))
    over_near = over(b1, CORE)
    first = rows * 3 // 4
    back_one, back_two = add_low(b2[:first], over_far[:first]), add_low(b2[first:], over_far[first:])
    far_one = over(back_one, NEXT)
    qkv_grad, qkv_sums = call(
        project_grad_kernel,
        (shape_of((width_all, heads * 128 + wide), bf16), shape_of((8, heads * 128 + wide), f32)),
        whole_specs(6), (VMEM, VMEM), "project_grad", 6,
    )(*parts[::-1], after(local_far, back_one), local_near)
    q_keep, q_give = halves(qkv_grad, 1)
    q_got = swap(q_give, rows_size, 1)
    far_one, back_two, mixed = lax.optimization_barrier((far_one, back_two, mixed_z))
    q_got = after(q_got, mixed)
    far_two = over(back_two, NEXT)
    down_z, up_z = mixed[:split], mixed[split:]
    cut_up = up_z.shape[0] // 2
    up_one, up_two = up_z[:cut_up], up_z[cut_up:]
    down_got = swap(down_z, rows_size, near_z)
    one_got, two_got = swap(up_one, rows_size, 1), swap(after(up_two, down_z), rows_size, near_z)
    q_keep, q_give = halves(after(add_low(q_keep, q_got), down_z), near_z)
    q_got = swap(q_give, rows_size, near_z)
    far_two, down_got = lax.optimization_barrier((far_two, down_got))
    down_z = joined(down_z[None], down_got[None], near_z)
    down_got = swap(down_z, rows_size, 1)

    tokens_grad, small = call(
        last_kernel,
        (shape_of((rows, width_all), f32), shape_of((leads + 16, width_all), bf16)),
        [VMEM, VMEM, SMEM] + whole_specs(11) + [SMEM], (VMEM, VMEM), "last", 7,
    )(
        tokens, frame_id, lead_index, lead_embed, ln1_gain, perm, after(b0, q_give, up_one, up_two, down_z), over_near, far_one, far_two, xgrad,
        sums_two, up_b, qkv_sums, me,
    )

    small, one_got, two_got, q_got = lax.optimization_barrier((small, one_got, two_got, q_got))
    up_one = joined(up_one[None], one_got[None], 1)
    up_two = joined(up_two[None], two_got[None], near_z)
    q_z = add_low(q_keep, q_got)
    q_far = swap(q_z, rows_size, far_z[0])
    two_got = swap(up_two, rows_size, 1)
    small = add_low(small, over(small, CORE))
    small = add_low(small, over(small, NEXT))
    small = add_low(small, swap(small, rows_size, near_z))
    small, q_far = lax.optimization_barrier((small, q_far))
    q_z = add_low(q_z, q_far)
    for bit in far_z[1:]:
        q_z = add_low(q_z, swap(q_z, rows_size, bit))
    q_got = swap(q_z, rows_size, near_z)
    for bit in far_z:
        small = add_low(small, swap(small, rows_size, bit))
    one_got = swap(after(up_one, q_z), rows_size, near_z)
    q_z = joined(q_z, q_got, near_z)
    q_got = swap(q_z, rows_size, 1)
    down_sum = joined(down_z, down_got, 1, 1).astype(f32).reshape(hidden, width_all)
    up_sum, out_sum = call(
        join_kernel,
        (shape_of((width_all, hidden), f32), shape_of((width, hidden), f32)),
        whole_specs(4) + [SMEM], (VMEM, VMEM), "join", 2,
    )(up_one, one_got, up_two, two_got, place)
    qkv_sum = joined(q_z, q_got, 1)

    pairs_sum = qkv_sum[:, 0 : heads * 128].reshape(width_all, heads, 2, HEAD).transpose(2, 0, 1, 3)
    qkv_out = jnp.concatenate(
        [
            pairs_sum.reshape(2, width_all, width),
            qkv_sum[:, heads * 128 : heads * 128 + width].reshape(1, width_all, width),
        ],
        axis=0,
    ).astype(f32)
    vector = shape_of((width_all,), f32)
    lead_sum, g1, b1, g2, b2, out_b, down_b, up_b_sum, qv_sum = call(
        finish_kernel,
        (shape_of((leads, width_all), f32),) + (vector,) * 6 + (shape_of((hidden,), f32), shape_of((2, width), f32)),
        [VMEM, VMEM, SMEM], (VMEM,) * 9, "finish", 1,
    )(small, swap(small, rows_size, 1), me)
    return (
        layer_out, tokens_grad, lead_sum, g1, b1, qkv_out, qv_sum, out_sum, out_b, g2, b2,
        up_sum, up_b_sum, down_sum, down_b,
    )


def solution(mesh):
    rows_size = mesh.shape["rows"]
    split = P(("rows", "tp"), None)
    placed = (
        split, P(("rows", "tp")), P("rows"), P(), P(), P(), P(None, None, "tp"), P(None, "tp"),
        P("tp", None), P(), P(), P(), P(None, "tp"), P("tp"), P("tp", None), P(), split,
    )
    return jax.shard_map(
        functools.partial(on_device, rows_size),
        mesh=mesh,
        in_specs=placed,
        out_specs=(
            split, split, P(), P(), P(), P(None, None, "tp"), P(None, "tp"), P("tp", None), P(), P(), P(),
            P(None, "tp"), P("tp"), P("tp", None), P(),
        ),
        check_vma=False,
    )
```

```python
import functools
import math

import jax
import jax.numpy as jnp
from jax import lax
from jax.experimental import pallas as pl
from jax.experimental.pallas import tpu as pltpu
from jax.sharding import PartitionSpec as P

HEAD = 64
EPS = 1e-05
LOG2E = math.log2(math.e)
LN2 = math.log(2.0)
TILE = 256
PAD = 16
VMEM_LIMIT = 60 * 1024 * 1024

f32 = jnp.float32
bf16 = jnp.bfloat16
i32 = jnp.int32

CORE = ((0, 1), (1, 0), (2, 3), (3, 2))
NEXT = ((0, 2), (2, 0), (1, 3), (3, 1))
DIAG = ((0, 3), (3, 0), (1, 2), (2, 1))

LIMITS = {
    "pre": 60, "project": 60, "attend": 48, "attend_last": 60, "middle": 60, "weight_grad": 60, "gather_grad": 24, "attend_back": 36,
    "project_back": 32, "project_grad": 40, "layer": 32, "last": 32, "join": 16, "finish": 8,
}


def iota(shape, axis):
    return lax.broadcasted_iota(i32, shape, axis)


def dot(left, right, dims):
    return lax.dot_general(left, right, (dims, ((), ())), preferred_element_type=f32)


NN = ((1,), (0,))
NT = ((1,), (1,))
TN = ((0,), (0,))


def shape_of(shape, dtype):
    return jax.ShapeDtypeStruct(shape, dtype)


def whole_specs(count):
    return [pl.BlockSpec(memory_space=pltpu.VMEM)] * count


SMEM = pl.BlockSpec(memory_space=pltpu.SMEM)
VMEM = pl.BlockSpec(memory_space=pltpu.VMEM)
HBM = pl.BlockSpec(memory_space=pl.ANY)


def call(body, out_shape, in_specs, out_specs, name, micros, scratch=(), grid=()):
    return pl.pallas_call(
        body,
        out_shape=out_shape,
        grid=grid,
        in_specs=in_specs,
        out_specs=out_specs,
        scratch_shapes=scratch,
        compiler_params=pltpu.CompilerParams(vmem_limit_bytes=LIMITS[name] * 1024 * 1024),
        name=name,
        cost_estimate=pl.CostEstimate(
            flops=int(micros * 1.15e9), bytes_accessed=1024, transcendentals=0
        ),
    )


def local_frame(frame_ref):
    return frame_ref[...].reshape(1, frame_ref.shape[0]) % 2


def row_of(ref):
    return ref[...].astype(f32).reshape(1, ref.shape[0])


def rows_with_lead(tok_ref, frame_ref, lead_ref, table_ref):
    frame = local_frame(frame_ref)
    lead = jnp.where(frame == 0, lead_ref[0], lead_ref[1])
    hot = (iota((table_ref.shape[0], frame.shape[1]), 0) == lead).astype(bf16)
    return tok_ref[...].astype(f32) + dot(hot, table_ref[...], TN), hot


def norm_stats(values):
    average = jnp.mean(values, axis=-1, keepdims=True)
    centred = values - average
    spread = jnp.mean(centred * centred, axis=-1, keepdims=True)
    inverse = lax.rsqrt(spread + EPS)
    return centred * inverse, inverse


def pre_kernel(tok_ref, frame_ref, lead_ref, table_ref, gain_ref, shift_ref, up_bias_ref, out_ref, perm_ref):
    rows = tok_ref.shape[0]
    values, _ = rows_with_lead(tok_ref, frame_ref, lead_ref, table_ref)
    unit, _ = norm_stats(values)
    normed = (unit * row_of(gain_ref) + row_of(shift_ref)).astype(bf16)
    first = (local_frame(frame_ref) == 0).astype(f32)
    before = (iota((rows, rows), 0) < iota((rows, rows), 1)).astype(bf16)
    earlier = dot(jnp.broadcast_to(first, (8, rows)).astype(bf16), before, NN)[0:1]
    count = jnp.sum(first, axis=1, keepdims=True)
    place = jnp.where(first > 0, earlier, count + iota((1, rows), 1).astype(f32) - earlier)
    perm = (iota((rows, rows), 0) == place.astype(i32)).astype(bf16)
    perm_ref[...] = perm
    out_ref[0:rows, :] = dot(perm, normed, NN).astype(bf16)
    high = jnp.floor(count * (1.0 / 16))
    low = count - 16 * high
    tail = iota((PAD, out_ref.shape[1]), 0)
    out_ref[rows : rows + PAD, :] = jnp.where(
        tail == 0, high, jnp.where(tail == 1, low, jnp.where(tail == 2, row_of(up_bias_ref), 0.0))
    ).astype(bf16)


def read_count(block_ref, rows):
    part = block_ref[rows : rows + PAD, 0:128].astype(f32)
    place, lane = iota(part.shape, 0), iota(part.shape, 1)
    worth = jnp.where(place == 0, 16.0, jnp.where(place == 1, 1.0, 0.0))
    return jnp.sum(jnp.where(lane == 0, part * worth, 0.0)).astype(i32)


def tile_moves(counts, rows, block, tile):
    group = 4 * rows
    count = counts[block]
    longs_before = sum(counts[:block], jnp.int32(0))
    limit = jnp.clip(count - tile * TILE, 0, TILE)
    moves = []
    for some, base, low, high in (
        (limit > 0, longs_before + tile * TILE, 0, limit),
        (limit < TILE, 2 * group // 3 + block * rows - longs_before - count + tile * TILE, limit, TILE),
    ):
        spot = jnp.minimum(base // TILE, group // TILE - 2)
        window = pl.ds(pl.multiple_of(spot * TILE, TILE), 2 * TILE)
        moves.append((some, window, base - spot * TILE, low, high))
    return moves


def aligned(index, size):
    return pl.ds(pl.multiple_of(index * size, size), size)


def to_group(value, dst_ref, moves):
    width = value.shape[1]
    for some, window, shift, low, high in moves:

        @pl.when(some)
        def _():
            dest, source = iota((2 * TILE, TILE), 0), iota((2 * TILE, TILE), 1)
            hot = (dest - source == shift) & (source >= low) & (source < high)
            moved = dot(hot.astype(bf16), value, NN).astype(bf16)
            dst_ref[window, 0:width] = dst_ref[window, 0:width] + moved


def from_group(src_refs, acc_refs, moves):
    (some_long, *long), (some_short, *short) = moves

    def moved(window, shift, low, high):
        source, dest = iota((TILE, 2 * TILE), 0), iota((TILE, 2 * TILE), 1)
        hot = ((dest - source == shift) & (source >= low) & (source < high)).astype(bf16)
        return [dot(hot, ref[window, :], NN).astype(bf16) for ref in src_refs]

    @pl.when(some_long)
    def _():
        for ref, value in zip(acc_refs, moved(*long)):
            ref[...] = value

    @pl.when(jnp.logical_not(some_long))
    def _():
        for ref, value in zip(acc_refs, moved(*short)):
            ref[...] = value

    @pl.when(some_long & some_short)
    def _():
        for ref, value in zip(acc_refs, moved(*short)):
            ref[...] = ref[...] + value


def pack_heads(src_ref, out_ref):
    rows = src_ref.shape[0]
    half = rows // 2
    lane = iota((half, 128), 1)
    out_ref[0:rows, :] = src_ref[:, 0:128]
    upper = src_ref[0:half, 128:256].astype(f32)
    lower = pltpu.roll(src_ref[half:rows, 128:256].astype(f32), HEAD, 1)
    out_ref[rows:, :] = jnp.where(lane < HEAD, upper, lower).astype(bf16)


def unpack_heads(src_ref, out_ref):
    rows = out_ref.shape[0]
    half = rows // 2
    lane = iota((half, 128), 1)
    out_ref[:, 0:128] = src_ref[0:rows, :]
    both = src_ref[rows:, :].astype(f32)
    out_ref[0:half, 128:256] = jnp.where(lane < HEAD, both, 0.0).astype(bf16)
    out_ref[half:rows, 128:256] = jnp.where(lane < HEAD, pltpu.roll(both, HEAD, 1), 0.0).astype(bf16)


def head_columns(ref, start, width):
    first = start // 128 * 128
    if first + 128 <= width:
        piece = ref[:, first : first + 128].astype(f32)
    else:
        piece = jnp.concatenate([ref[:, first : first + HEAD].astype(f32)] * 2, axis=1)
    return pltpu.roll(piece, HEAD, 1) if start != first else piece


def project_rows(x_ref, index, counts, weight_ref, bias_ref, value_ref, qkv_ref):
    rows = value_ref.shape[0]
    width = weight_ref.shape[2]
    for part in range(3):
        value = dot(x_ref[0:rows, :], weight_ref[part], NN)
        if part == 0:
            value = (value + bias_ref[0:1, :].astype(f32)) * (LOG2E / math.sqrt(HEAD))
        if part == 2:
            value = value + bias_ref[1:2, :].astype(f32)
        value_ref[:, part * width : (part + 1) * width] = value.astype(bf16)

    def place(tile, _):
        to_group(value_ref[aligned(tile, TILE), :], qkv_ref, tile_moves(counts, rows, index, tile))
        return 0

    lax.fori_loop(0, rows // TILE, place, 0)


def weight_cut(rows):
    part = rows * 3 // 8
    return part, rows - 2 * part


def project_kernel(
    weight_ref, bias_ref, x0_ref, x1_ref, place_ref, out_ref, up_ref, down_ref,
    qkv_ref, counts_ref, common_ref, up_part_ref, down_part_ref, value_ref,
):
    part, middle = weight_cut(up_ref.shape[0])
    first = out_ref.shape[0]
    common_ref[0:first, :] = out_ref[...]
    for index, (ref, part_ref, at) in enumerate(
        ((down_ref, down_part_ref, place_ref[0]), (up_ref, up_part_ref, place_ref[1]))
    ):
        common_ref[first + index * middle : first + (index + 1) * middle, :] = ref[part : part + middle, :]
        part_ref[...] = ref[pl.ds(pl.multiple_of(at * (part + middle), PAD), part), :]
    qkv_ref[...] = jnp.zeros(qkv_ref.shape, qkv_ref.dtype)
    counts = []
    for index, ref in enumerate((x0_ref, x1_ref)):
        counts.append(read_count(ref, value_ref.shape[0]))
        counts_ref[index] = counts[index]
        project_rows(ref, index, counts, weight_ref, bias_ref, value_ref, qkv_ref)


def attend_kernel(
    weight_ref, bias_ref, early_ref, part_ref, x2_ref, x3_ref,
    att_ref, lse_ref, counts_ref, a0_ref, a1_ref, a2_ref, a3_ref, q_out, k_out, v_out,
    x_buf, qkv_ref, value_ref, q_ref, k_ref, v_ref, scores_ref, load_sems, store_sems,
):
    rows = x2_ref.shape[0] - PAD
    group = 4 * rows
    long = 2 * group // 3
    width = weight_ref.shape[2]
    heads = width // HEAD
    loads = [
        pltpu.make_async_copy(source, target, load_sems.at[i])
        for i, (source, target) in enumerate(
            ((part_ref, qkv_ref), (x2_ref, x_buf.at[0]), (x3_ref, x_buf.at[1]))
        )
    ]
    for load in loads:
        load.start()
    loads[0].wait()
    counts = [early_ref[0], early_ref[1]]
    for index in (2, 3):
        loads[index - 1].wait()
        block_ref = x_buf.at[index - 2]
        counts.append(read_count(block_ref, rows))
        project_rows(block_ref, index, counts, weight_ref, bias_ref, value_ref, qkv_ref)
    for index, count in enumerate(counts):
        counts_ref[index] = count
    lane = iota((group, 128), 1)
    stores = []
    for part, ref, out, fill in ((1, k_ref, k_out, 0.0), (2, v_ref, v_out, 1.0), (0, q_ref, q_out, 0.0)):
        for head in range(heads):
            piece = head_columns(qkv_ref, part * width + head * HEAD, 3 * width)
            ref[head] = jnp.where(lane < HEAD, piece, fill).astype(bf16)
        store = pltpu.make_async_copy(ref, out, store_sems.at[part])
        store.start()
        stores.append(store)

    block = 512
    row = iota((128, block), 0)
    half = iota((block, 128), 1)
    tasks = [
        (head, first, low, high)
        for low, high in ((0, long), (long, group))
        for first in range(low, high, block)
        for head in range(heads)
    ]

    span = 2 * block

    def scores(task, part):
        head, first, low, high = tasks[task]
        keys = slice(low + part * span, low + (part + 1) * span)
        value = dot(k_ref[head, keys, :], q_ref[head, first : first + block, :], NT)
        scores_ref[task % 2, part * span : (part + 1) * span, :] = value
        return jnp.max(value.reshape(span // 8, 8, block), axis=0)

    def parts_of(task):
        return (tasks[task][3] - tasks[task][2]) // span if task < len(tasks) else 0

    largest = functools.reduce(jnp.maximum, [scores(0, part) for part in range(parts_of(0))])
    outs = []
    for task, (head, first, low, high) in enumerate(tasks):
        top = jnp.max(largest, axis=0, keepdims=True)
        following, mixed = [], None
        for part in range(max(parts_of(task), parts_of(task + 1))):
            if part < parts_of(task + 1):
                following.append(scores(task + 1, part))
            if part < parts_of(task):
                raised = jnp.exp2(scores_ref[task % 2, part * span : (part + 1) * span, :] - top)
                keys = slice(low + part * span, low + (part + 1) * span)
                value = dot(v_ref[head, keys, :], raised.astype(bf16), TN)
                mixed = value if mixed is None else mixed + value
        if following:
            largest = functools.reduce(jnp.maximum, following)
        totals = mixed[HEAD : HEAD + 1, :]
        lse_ref[head : head + 1, first : first + block] = top + jnp.log2(totals)
        outs.append(jnp.where(row < HEAD, mixed / totals, 0.0))
        if head == heads - 1:
            for pair in range((heads + 1) // 2):
                value = outs[2 * pair].T
                if 2 * pair + 1 < heads:
                    value = value + pltpu.roll(outs[2 * pair + 1].T, HEAD, 1)
                att_ref[first : first + block, pair * 128 : (pair + 1) * 128] = value.astype(bf16)
            outs = []
    for index, out in enumerate((a0_ref, a1_ref, a2_ref, a3_ref)):

        def hand_back(tile, _, index=index):
            moves = tile_moves(counts, rows, index, tile)
            from_group((att_ref,), (qkv_ref.at[aligned(tile, TILE), 0 : att_ref.shape[1]],), moves)
            return 0

        lax.fori_loop(0, rows // TILE, hand_back, 0)
        pack_heads(qkv_ref.at[0:rows, 0 : att_ref.shape[1]], out)
    for store in stores:
        store.wait()


def middle_kernel(
    tok_ref, frame_ref, lead_ref, table_ref, perm_ref,
    at0_ref, at1_ref, at2_ref, at3_ref,
    gain_ref, shift_ref, out_bias_ref, down_bias_ref, place_ref,
    og_in, wo0_ref, wo1_ref, common2_ref, common3_ref,
    x0_ref, x1_ref, x2_ref, x3_ref, up0_ref, up1_ref, up2_ref, up3_ref,
    ux2_ref, ux3_ref, dn0_ref, dn1_ref, dn2_ref, dn3_ref, dx2_ref, dx3_ref,
    s0_ref, s1_ref, s2_ref, s3_ref, sums_ref, upb_ref,
    base_out, down_out, xgrad_out, agrad_out, normed_out, attu_out, act_out, hid_out,
    y_ref, back_ref, at_ref, attu_ref, wo_ref, og_ref, normed_ref, xgrad_ref, agrad_ref, bias_buf, up_buf, dn_buf,
    act_ref, hid_ref, load_sems, store_sems,
):
    ats = (at0_ref, at1_ref, at2_ref, at3_ref)
    blocks = (x0_ref, x1_ref, x2_ref, x3_ref)
    sends = (s0_ref, s1_ref, s2_ref, s3_ref)
    rows, wide = tok_ref.shape
    hidden = up_buf.shape[2]
    width = wo0_ref.shape[0]
    span = wo_ref.shape[0] // 4
    part, middle = weight_cut(hidden)
    x, z = place_ref[0], place_ref[1]
    mine, other = (pl.ds(pl.multiple_of(at * (part + middle), PAD), part) for at in (x, 1 - x))
    up_mine, up_other = (pl.ds(pl.multiple_of(at * (part + middle), PAD), part) for at in (z, 1 - z))
    both = pl.ds(part, middle)
    wos = (wo0_ref, wo1_ref, common2_ref.at[0:width], common3_ref.at[0:width])
    first_loads = [
        pltpu.make_async_copy(wos[i], wo_ref.at[i * span : i * span + width], load_sems.at[14 + i]) for i in range(4)
    ]
    loads = [[], [], [], []]
    loads[0].append(pltpu.make_async_copy(og_in, og_ref, load_sems.at[18]))
    for index, ref, target, sem in (
        (0, up0_ref, up_buf.at[0], 0),
        (1, up1_ref, up_buf.at[1], 1),
        (2, common2_ref.at[width : width + middle], dn_buf.at[2, both], 21),
        (3, common3_ref.at[width : width + middle], dn_buf.at[3, both], 22),
        (2, common2_ref.at[width + middle :], up_buf.at[2, both], 23),
        (3, common3_ref.at[width + middle :], up_buf.at[3, both], 24),
        (2, up2_ref, up_buf.at[2, up_mine], 2),
        (2, ux2_ref, up_buf.at[2, up_other], 19),
        (3, up3_ref, up_buf.at[3, up_mine], 3),
        (3, ux3_ref, up_buf.at[3, up_other], 20),
        (0, dn0_ref, dn_buf.at[0], 4),
        (1, dn1_ref, dn_buf.at[1], 5),
        (2, dn2_ref, dn_buf.at[2, mine], 6),
        (2, dx2_ref, dn_buf.at[2, other], 7),
        (3, dn3_ref, dn_buf.at[3, mine], 8),
        (3, dx3_ref, dn_buf.at[3, other], 9),
    ):
        loads[index].append(pltpu.make_async_copy(ref, target, load_sems.at[sem]))
    for index in range(4):
        tail = blocks[index].at[rows : rows + PAD]
        loads[index].append(pltpu.make_async_copy(tail, bias_buf.at[index], load_sems.at[10 + index]))
    for load in first_loads + sum(loads, []):
        load.start()
    stores = []

    def store(source, target):
        copy = pltpu.make_async_copy(source, target, store_sems.at[len(stores)])
        copy.start()
        stores.append(copy)

    gain = row_of(gain_ref)
    perm = perm_ref[...]
    for index in range(4):
        unpack_heads(ats[index], at_ref.at[:, index * span : (index + 1) * span])
        wo_ref[index * span + width : (index + 1) * span, :] = jnp.zeros((span - width, wide), bf16)
    attu_ref[...] = dot(perm, at_ref[...], TN).astype(bf16)
    store(attu_ref, attu_out)
    values, _ = rows_with_lead(tok_ref, frame_ref, lead_ref, table_ref)
    for load in first_loads:
        load.wait()
    x_one = values + row_of(out_bias_ref) + dot(attu_ref[...], wo_ref[...], NN)
    unit, inverse = norm_stats(x_one)
    normed_ref[...] = (unit * gain + row_of(shift_ref)).astype(bf16)
    store(normed_ref, normed_out)
    y_ref[...] = x_one + row_of(down_bias_ref)
    store(y_ref, base_out)
    for index in range(4):
        for load in loads[index]:
            load.wait()
        up = up_buf[index]
        down = dn_buf[index]
        store(dn_buf.at[index], down_out.at[index])
        h = dot(normed_ref[...], up, NN) + bias_buf[index][2:3].astype(f32)
        g = dot(og_ref[...], down, NT)
        c = math.sqrt(2.0 / math.pi)
        h2 = h * h
        t = jnp.tanh(h * (c + (c * 0.044715) * h2))
        half = 0.5 + 0.5 * t
        act = h * half
        slope = half + act * (1.0 - t) * (c + (3 * c * 0.044715) * h2)
        hid = (slope * g).astype(bf16)
        actb = act.astype(bf16)
        act_ref[index] = actb
        hid_ref[index] = hid
        upb_ref[index] = jnp.broadcast_to(jnp.sum(hid.astype(f32), axis=0, keepdims=True), (8, hidden))
        if index == 0:
            back_ref[...] = dot(hid, up, NT)
        else:
            back_ref[...] += dot(hid, up, NT)
        store(act_ref.at[index], act_out.at[index])
        store(hid_ref.at[index], hid_out.at[index])
    grad = back_ref[...]
    e = grad * gain
    spread_mean = jnp.mean(e, axis=-1, keepdims=True)
    along = jnp.mean(e * unit, axis=-1, keepdims=True)
    og = og_ref[...].astype(f32)
    xgrad = og + inverse * (e - spread_mean - unit * along)
    xgrad_ref[...] = xgrad
    store(xgrad_ref, xgrad_out)
    agrad = xgrad.astype(bf16)
    agrad_ref[...] = agrad
    store(agrad_ref, agrad_out)
    at_ref[...] = dot(agrad, wo_ref[...], NT).astype(bf16)
    at_ref[...] = dot(perm, at_ref[...], NN).astype(bf16)
    for index in range(4):
        pack_heads(at_ref.at[:, index * span : (index + 1) * span], sends[index])
    sums_ref[...] = jnp.concatenate(
        [
            jnp.sum(grad * unit, axis=0, keepdims=True),
            jnp.sum(grad, axis=0, keepdims=True),
            jnp.sum(agrad.astype(f32), axis=0, keepdims=True),
            jnp.sum(og, axis=0, keepdims=True),
            jnp.zeros((4, og.shape[1]), f32),
        ],
        axis=0,
    )
    for copy in stores:
        copy.wait()


def layer_kernel(base_ref, act_ref, down_ref, out_ref, sum_ref):
    step = pl.program_id(0)
    part = dot(act_ref[0], down_ref[0], NN)

    @pl.when(step == 0)
    def _():
        sum_ref[...] = base_ref[...] + part

    @pl.when((step > 0) & (step < pl.num_programs(0) - 1))
    def _():
        sum_ref[...] += part

    @pl.when(step == pl.num_programs(0) - 1)
    def _():
        out_ref[...] = (sum_ref[...] + part).astype(bf16)


def weight_grad_kernel(
    normed_ref, og_ref, agrad_ref, act_ref, hid_ref, attu_ref, up_send_ref, up_keep_ref, down_send_ref, down_keep_ref,
    turned_ref,
):
    @pl.when(pl.program_id(0) == 0)
    def _():
        turned_ref[...] = normed_ref[...].T

    up = dot(turned_ref[...], hid_ref[0], NN).astype(bf16)
    out = dot(attu_ref[...], agrad_ref[...], TN).astype(bf16)[0 : up_send_ref.shape[1] - up.shape[0]]
    down = dot(act_ref[0], og_ref[...], TN).astype(bf16)
    rows = up.shape[0]
    step = pl.program_id(0)
    for chosen, up_ref, down_ref in (
        (step < 2, up_send_ref, down_send_ref), (step >= 2, up_keep_ref, down_keep_ref),
    ):

        @pl.when(chosen)
        def _(up_ref=up_ref, down_ref=down_ref):
            up_ref[0, 0:rows, :] = up
            up_ref[0, rows:, :] = out
            down_ref[0] = down


def gather_grad_kernel(counts_ref, b0_ref, b1_ref, b2_ref, b3_ref, att_ref, out_ref, inner_ref, sorted_ref, block_ref):
    blocks = (b0_ref, b1_ref, b2_ref, b3_ref)
    rows = block_ref.shape[0]
    group = 4 * rows
    heads = out_ref.shape[0]
    counts = [counts_ref[i] for i in range(4)]
    sorted_ref[...] = jnp.zeros(sorted_ref.shape, sorted_ref.dtype)
    for index, ref in enumerate(blocks):

        unpack_heads(ref, block_ref)

        def place(tile, _, index=index):
            to_group(block_ref[aligned(tile, TILE), :], sorted_ref, tile_moves(counts, rows, index, tile))
            return 0

        lax.fori_loop(0, rows // TILE, place, 0)
    lane = iota((group, 128), 1)
    pick_row, pick_lane = iota((8, 128), 0), iota((8, 128), 1)
    inner_ref[...] = jnp.zeros(inner_ref.shape, f32)
    for pair in range((heads + 1) // 2):
        columns = slice(pair * 128, (pair + 1) * 128)
        grad = sorted_ref[:, columns].astype(f32)
        product = grad * att_ref[:, columns].astype(f32)
        high = product.astype(bf16)
        low = (product - high.astype(f32)).astype(bf16)
        pick = (pick_row == 2 * pair + pick_lane // HEAD).astype(bf16)
        inner_ref[...] += dot(pick, high, NT) + dot(pick, low, NT)
        out_ref[2 * pair] = jnp.where(lane < HEAD, grad, 0.0).astype(bf16)
        if 2 * pair + 1 < heads:
            out_ref[2 * pair + 1] = jnp.where(lane < HEAD, pltpu.roll(grad, HEAD, 1), 0.0).astype(bf16)


def attend_back_kernel(first_head, first_lse, lse_ref, inner_ref, q_ref, k_ref, v_ref, g_ref, out_ref, dq_ref):
    group = q_ref.shape[1]
    long = 2 * group // 3
    block = 1024
    lane = iota((block, 128), 1)
    head = first_head + pl.program_id(0)
    lse = jnp.sum(jnp.where(iota(lse_ref.shape, 0) == first_lse + pl.program_id(0), lse_ref[...], 0.0), axis=0, keepdims=True)
    inner = jnp.sum(jnp.where(iota(inner_ref.shape, 0) == head, inner_ref[...], 0.0), axis=0, keepdims=True)
    done = set()
    for low, high in ((0, long), (long, group)):
        for keys in range(low, high, block):
            key = k_ref[0, keys : keys + block, :]
            value = v_ref[0, keys : keys + block, :]
            key_grad, value_grad = None, None
            for queries in range(low, high, block):
                query = q_ref[0, queries : queries + block, :]
                grad = g_ref[0, queries : queries + block, :]
                probs = jnp.exp2(dot(key, query, NT) - lse[:, queries : queries + block])
                inside = dot(value, grad, NT) - inner[:, queries : queries + block]
                score_grad = (probs * inside).astype(bf16)
                value_part = dot(probs.astype(bf16), grad, NN)
                key_part = dot(score_grad, query, NN)
                query_part = dot(key, score_grad, TN)
                value_grad = value_part if value_grad is None else value_grad + value_part
                key_grad = key_part if key_grad is None else key_grad + key_part
                place = (slice(None), slice(queries, queries + block))
                dq_ref[place] = query_part if queries not in done else dq_ref[place] + query_part
                done.add(queries)
            out_ref[0, keys : keys + block, 0:128] = pltpu.roll(key_grad * LN2, HEAD, 1).astype(bf16)
            out_ref[0, keys : keys + block, 128:256] = value_grad.astype(bf16)
    wide = iota((group, 128), 1)
    query_grad = dq_ref[...].T * (1.0 / math.sqrt(HEAD))
    pair = jnp.where(wide < HEAD, query_grad, out_ref[0, :, 0:128].astype(f32))
    out_ref[0, :, 0:128] = pair.astype(bf16)


def project_back_kernel(chosen, counts_ref, h01_ref, h2_ref, weight_ref, local_ref, one_ref, two_ref, *acc_refs):
    refs = [h01_ref.at[i] for i in range(h01_ref.shape[0])] + [h2_ref.at[i] for i in range(h2_ref.shape[0])]
    rows = local_ref.shape[1]
    counts = [counts_ref[i] for i in range(4)]
    pairs = len(refs) * 128
    lane = iota((TILE, 128), 1)
    for slot, (index, back_ref) in enumerate(zip(chosen, (one_ref, two_ref))):

        def step(tile, _, index=index, slot=slot):
            here = aligned(tile, TILE)
            from_group(refs, acc_refs, tile_moves(counts, rows, index, tile))
            for head, ref in enumerate(acc_refs):
                local_ref[slot, here, head * 128 : (head + 1) * 128] = ref[:, 0:128]
            for pair in range((len(refs) + 1) // 2):
                value = acc_refs[2 * pair][:, 128:256]
                if 2 * pair + 1 < len(refs):
                    other = acc_refs[2 * pair + 1][:, 128:256].astype(f32)
                    value = jnp.where(lane < HEAD, value.astype(f32), pltpu.roll(other, HEAD, 1)).astype(bf16)
                first = pairs + pair * 128
                local_ref[slot, here, first : first + 128] = value
            return 0

        lax.fori_loop(0, rows // TILE, step, 0)
        back_ref[...] = dot(local_ref[slot], weight_ref[...], NT).astype(bf16)


def project_grad_kernel(x3_ref, x2_ref, x1_ref, x0_ref, far_ref, near_ref, out_ref, sums_ref):
    rows = far_ref.shape[1]
    total, sums = None, None
    for ref, local_ref, slot in (
        (x3_ref, far_ref, 0), (x2_ref, far_ref, 1), (x1_ref, near_ref, 0), (x0_ref, near_ref, 1)
    ):
        value = local_ref[slot]
        part = dot(ref[0:rows, :], value, TN)
        total = part if total is None else total + part
        one = jnp.sum(value.astype(f32), axis=0, keepdims=True)
        sums = one if sums is None else sums + one
    out_ref[...] = total.astype(bf16)
    sums_ref[...] = jnp.broadcast_to(sums, sums_ref.shape)


def last_kernel(
    tok_ref, frame_ref, lead_ref, table_ref, gain_ref, perm_ref, mine_ref, near_ref, one_ref, more_ref, xgrad_ref,
    two_ref, upb_ref, qkv_ref, me_ref, out_ref, sums_ref,
):
    values, hot = rows_with_lead(tok_ref, frame_ref, lead_ref, table_ref)
    unit, inverse = norm_stats(values)
    other = jnp.concatenate([one_ref[...], more_ref[...]], axis=0)
    local = (mine_ref[...].astype(f32) + near_ref[...].astype(f32) + other.astype(f32)).astype(bf16)
    grad = dot(perm_ref[...], local, TN)
    e = grad * row_of(gain_ref)
    mean_e = jnp.mean(e, axis=-1, keepdims=True)
    along = jnp.mean(e * unit, axis=-1, keepdims=True)
    out = xgrad_ref[...] + inverse * (e - mean_e - unit * along)
    out_ref[...] = out
    leads = table_ref.shape[0]
    one = out.astype(bf16)
    rest = out - one.astype(f32)
    two = rest.astype(bf16)
    three = (rest - two.astype(f32)).astype(bf16)
    sums_ref[0:leads, :] = (dot(hot, one, NN) + dot(hot, two, NN) + dot(hot, three, NN)).astype(bf16)
    row = iota((16, grad.shape[1]), 0)
    me = me_ref[0]
    small = jnp.zeros((16, grad.shape[1]), f32)
    small = jnp.where(row == 0, jnp.sum(grad * unit, axis=0, keepdims=True), small)
    small = jnp.where(row == 1, jnp.sum(grad, axis=0, keepdims=True), small)
    for i in range(4):
        small = jnp.where(row == 2 + i, two_ref[i : i + 1, :], small)
        small = jnp.where(row == 6 + (me ^ i), upb_ref[i, 0:1, :], small)
    heads = (qkv_ref.shape[1] * 2 // 128) // 3
    bias = [qkv_ref[0:1, head * 128 : head * 128 + HEAD] for head in range(heads)]
    bias.append(qkv_ref[0:1, heads * 128 : heads * 128 + heads * HEAD])
    bias.append(jnp.zeros((1, grad.shape[1] - 2 * heads * HEAD), f32))
    small = jnp.where(row == 10 + me, jnp.concatenate(bias, axis=1), small)
    sums_ref[leads : leads + 16, :] = small.astype(bf16)


def finish_kernel(left_ref, right_ref, me_ref, lead_ref, g1_ref, b1_ref, g2_ref, b2_ref, ob_ref, db_ref, ub_ref, qv_ref):
    total = left_ref[...].astype(f32) + right_ref[...].astype(f32)
    leads = lead_ref.shape[0]
    lead_ref[...] = total[0:leads]
    for place, ref in enumerate((g1_ref, b1_ref, g2_ref, b2_ref, ob_ref, db_ref)):
        ref[...] = total[leads + place].reshape(ref.shape)
    me = me_ref[0]
    up, qv = total[leads + 6 : leads + 7], total[leads + 10 : leads + 11]
    for i in range(1, 4):
        up = jnp.where(me == i, total[leads + 6 + i : leads + 7 + i], up)
        qv = jnp.where(me == i, total[leads + 10 + i : leads + 11 + i], qv)
    ub_ref[...] = up.reshape(ub_ref.shape)
    width = qv_ref.shape[1]
    qv_ref[...] = jnp.concatenate([qv[:, 0:width], qv[:, width : 2 * width]], axis=0)


def join_kernel(one_ref, one_got_ref, two_ref, two_got_ref, place_ref, up_ref, out_ref):
    cut, rows = up_ref.shape[0], one_ref.shape[1]
    x, z = place_ref[0], place_ref[1]
    for at_x in range(2):
        for at_z in range(2):
            one = jnp.where(z == at_z, one_ref[at_x].astype(f32), one_got_ref[at_x].astype(f32))
            two = jnp.where(x == at_x, two_ref[at_z].astype(f32), two_got_ref[at_z].astype(f32))
            for part, value in enumerate((one, two)):
                first = ((2 * at_x + at_z) * 2 + part) * rows
                inside = min(max(cut - first, 0), rows)
                if inside:
                    up_ref[first : first + inside, :] = value[:inside]
                if inside < rows:
                    start = max(first - cut, 0)
                    out_ref[start : start + rows - inside, :] = value[inside:]


def bits_of(size):
    bits = []
    step = 1
    while step < size:
        bits.append(step)
        step *= 2
    return bits


def after(value, *others):
    return lax.optimization_barrier((value, *others))[0]


def swap(value, size, bit):
    return lax.ppermute(value, "rows", [(i, i ^ bit) for i in range(size)])


def add_low(left, right):
    return (left.astype(f32) + right.astype(f32)).astype(bf16)


def halves(value, bit, axis=0):
    half = value.shape[axis] // 2
    high = (lax.axis_index("rows") // bit) % 2
    return (
        lax.dynamic_slice_in_dim(value, high * half, half, axis),
        lax.dynamic_slice_in_dim(value, (1 - high) * half, half, axis),
    )


def joined(mine, other, bit, axis=0):
    high = (lax.axis_index("rows") // bit) % 2
    low_part, high_part = jnp.where(high == 1, other, mine), jnp.where(high == 1, mine, other)
    return jnp.concatenate([low_part, high_part], axis)


def on_device(
    rows_size,
    tokens, frame_id, lead_index, lead_embed, ln1_gain, ln1_bias, qkv_weight, qv_bias,
    out_weight, out_bias, ln2_gain, ln2_bias, up_weight, up_bias, down_weight, down_bias, out_grad,
):
    rows, width_all = tokens.shape
    width = qkv_weight.shape[2]
    heads = width // HEAD
    hidden = up_weight.shape[1]
    leads = lead_embed.shape[0]
    group = 4 * rows
    wide = (heads + 1) // 2 * 128
    bits = bits_of(rows_size)
    me = lax.axis_index("tp").reshape(1)
    near_z, far_z = bits[1], bits[2:]
    place = jnp.stack([lax.axis_index("rows") % 2, lax.axis_index("rows") // near_z % 2])

    def over(value, ring):
        return lax.ppermute(value, "tp", ring)

    def full(shape):
        return pl.BlockSpec(shape, lambda s: (0,) * len(shape))

    mine, perm = call(
        pre_kernel,
        (shape_of((rows + PAD, width_all), bf16), shape_of((rows, rows), bf16)),
        [VMEM, VMEM, SMEM, VMEM, VMEM, VMEM, VMEM], (VMEM, VMEM), "pre", 5,
    )(tokens, frame_id, lead_index, lead_embed, ln1_gain, ln1_bias, up_bias)
    near = over(mine, CORE)
    far = over(mine, NEXT)
    part, middle = weight_cut(width_all)
    early, early_counts, common, up_part, down_part = call(
        project_kernel,
        (
            shape_of((group, 3 * width), bf16),
            shape_of((8,), i32),
            shape_of((width + 2 * middle, width_all), bf16),
            shape_of((part, hidden), bf16),
            shape_of((part, width_all), bf16),
        ),
        whole_specs(4) + [SMEM] + whole_specs(3), (VMEM, SMEM) + (VMEM,) * 3, "project", 8,
        scratch=[pltpu.VMEM((rows, 3 * width), bf16)],
    )(qkv_weight, qv_bias, mine, near, place, out_weight, up_weight, down_weight)
    far, up_weight, down_weight, out_weight = lax.optimization_barrier(
        (far, up_weight, down_weight, out_weight, early)
    )[:4]
    across = over(far, CORE)
    parts = (mine, near, far, across)

    common_far, down_far, up_far = over(common, NEXT), over(down_part, NEXT), over(up_part, NEXT)
    out_near = over(out_weight, CORE)
    across, up_weight, down_weight, out_near = lax.optimization_barrier((across, up_weight, down_weight, out_near))
    up_near, down_near = over(up_weight, CORE), over(down_weight, CORE)

    att, lse, counts, a0, a1, a2, a3, q_all, k_all, v_all = call(
        attend_kernel,
        (
            shape_of((group, wide), bf16),
            shape_of((8, group), f32),
            shape_of((8,), i32),
        )
        + (shape_of((rows * 3 // 2, 128), bf16),) * 4
        + (shape_of((heads, group, 128), bf16),) * 3,
        whole_specs(2) + [SMEM] + [HBM] * 3, (VMEM, VMEM, SMEM) + (VMEM,) * 4 + (HBM,) * 3, "attend", 40,
        scratch=[
            pltpu.VMEM((2, rows + PAD, width_all), bf16),
            pltpu.VMEM((group, 3 * width), bf16),
            pltpu.VMEM((rows, 3 * width), bf16),
            pltpu.VMEM((heads, group, 128), bf16),
            pltpu.VMEM((heads, group, 128), bf16),
            pltpu.VMEM((heads, group, 128), bf16),
            pltpu.VMEM((2, 2 * group // 3, 512), f32),
            pltpu.SemaphoreType.DMA((3,)),
            pltpu.SemaphoreType.DMA((3,)),
        ],
    )(qkv_weight, qv_bias, early_counts, early, far, across)

    counts, up_far, down_far, up_near, down_near, common_far, pair_weight = lax.optimization_barrier(
        (counts, up_far, down_far, up_near, down_near, common_far, qkv_weight)
    )
    got = [a0, over(a1, CORE), over(a2, NEXT), over(a3, DIAG)]
    down_side, up_side = swap(down_far, rows_size, 1), swap(up_far, rows_size, near_z)
    got[1], common_far, down_far, up_far = lax.optimization_barrier((got[1], common_far, down_far, up_far))
    common_across, down_across, up_across = over(common_far, CORE), over(down_far, CORE), over(up_far, CORE)
    value_weight = pair_weight[2]
    pair_weight = pair_weight[0:2].reshape(2, width_all, heads, HEAD).transpose(1, 2, 0, 3)
    weight_heads = jnp.concatenate(
        [pair_weight.reshape(width_all, heads * 128), jnp.pad(value_weight, ((0, 0), (0, wide - width)))], axis=1
    )
    *got[2:], down_side, up_side, weight_heads = lax.optimization_barrier((*got[2:], down_side, up_side, weight_heads))
    up_side_across, down_side_across = over(up_side, CORE), over(down_side, CORE)

    s0, s1, s2, s3, sums_two, up_b, base, down_all, xgrad, agrad, normed_two, attu, act, hid = call(
        middle_kernel,
        (shape_of((rows * 3 // 2, 128), bf16),) * 4
        + (
            shape_of((8, width_all), f32),
            shape_of((4, 8, hidden), f32),
            shape_of((rows, width_all), f32),
            shape_of((4, hidden, width_all), bf16),
            shape_of((rows, width_all), f32),
            shape_of((rows, width_all), bf16),
            shape_of((rows, width_all), bf16),
            shape_of((rows, 4 * wide), bf16),
            shape_of((4, rows, hidden), bf16),
            shape_of((4, rows, hidden), bf16),
        ),
        [VMEM, VMEM, SMEM] + whole_specs(10) + [SMEM] + [HBM] * 21, (VMEM,) * 6 + (HBM,) * 8, "middle", 25,
        scratch=[
            pltpu.VMEM((rows, width_all), f32),
            pltpu.VMEM((rows, width_all), f32),
            pltpu.VMEM((rows, 4 * wide), bf16),
            pltpu.VMEM((rows, 4 * wide), bf16),
            pltpu.VMEM((4 * wide, width_all), bf16),
            pltpu.VMEM((rows, width_all), bf16),
            pltpu.VMEM((rows, width_all), bf16),
            pltpu.VMEM((rows, width_all), f32),
            pltpu.VMEM((rows, width_all), bf16),
            pltpu.VMEM((4, PAD, width_all), bf16),
            pltpu.VMEM((4, width_all, hidden), bf16),
            pltpu.VMEM((4, hidden, width_all), bf16),
            pltpu.VMEM((4, rows, hidden), bf16),
            pltpu.VMEM((4, rows, hidden), bf16),
            pltpu.SemaphoreType.DMA((25,)),
            pltpu.SemaphoreType.DMA((17,)),
        ],
    )(
        tokens, frame_id, lead_index, lead_embed, perm, *got, ln2_gain, ln2_bias, out_bias, down_bias, place,
        out_grad, out_weight, out_near, common_far, common_across, *parts, up_weight, up_near, up_far, up_across,
        up_side, up_side_across, down_weight, down_near, down_far, down_across, down_side, down_side_across,
    )

    got_grad = [s0, over(s1, CORE), over(s2, NEXT), over(s3, DIAG)]

    def block_of(step):
        return jnp.where(step < 2, 2 * step + 1, 2 * step - 4)

    def picked(shape):
        return pl.BlockSpec((1,) + shape, lambda s: (block_of(s), 0, 0))

    cut = width_all + width
    first_two, last_two = lambda s: (jnp.minimum(s, 1), 0, 0), lambda s: (jnp.maximum(s - 2, 0), 0, 0)
    up_share, down_share = (1, cut, hidden), (1, hidden, width_all)
    up_send, up_keep, down_send, down_keep = call(
        weight_grad_kernel,
        (shape_of((2, cut, hidden), bf16),) * 2 + (shape_of((2, hidden, width_all), bf16),) * 2,
        [full((rows, width_all))] * 3 + [picked((rows, hidden))] * 2 + [pl.BlockSpec((rows, wide), lambda s: (0, block_of(s)))],
        (
            pl.BlockSpec(up_share, first_two), pl.BlockSpec(up_share, last_two),
            pl.BlockSpec(down_share, first_two), pl.BlockSpec(down_share, last_two),
        ),
        "weight_grad", 18, grid=(4,), scratch=[pltpu.VMEM((width_all, rows), bf16)],
    )(normed_two, out_grad, agrad, act, hid, attu)
    *got_grad[1:], up_send, up_keep, down_send, down_keep = lax.optimization_barrier(
        (*got_grad[1:], up_send, up_keep, down_send, down_keep)
    )
    up_got, down_got = over(up_send, CORE), over(down_send, CORE)
    grad_all, inner = call(
        gather_grad_kernel,
        (shape_of((heads, group, 128), bf16), shape_of((8, group), f32)),
        [SMEM] + whole_specs(5), (VMEM, VMEM), "gather_grad", 6,
        scratch=[pltpu.VMEM((group, wide), bf16), pltpu.VMEM((rows, wide), bf16)],
    )(after(counts, up_send), *got_grad, att)

    up_got = after(up_got, inner)
    (up_keep, up_give), (up_keep_two, up_give_two) = halves(up_keep, 1, 1), halves(up_got, 1, 1)
    up_mine, up_away = add_low(up_keep, up_keep_two), add_low(up_give, up_give_two)
    down_got = after(down_got, up_away)
    down_mine = add_low(down_keep[0], down_got[0])
    down_other = add_low(down_keep[1], down_got[1])
    down_y = over(down_other, NEXT)
    up_x = swap(up_away, rows_size, 1)

    def attend_back(first, count, lse, first_lse, grads):
        spec = pl.BlockSpec((1, group, 128), lambda s: (first + s, 0, 0))
        return call(
            functools.partial(attend_back_kernel, first, first_lse),
            shape_of((count, group, 256), bf16),
            [full((8, group))] * 2 + [spec] * 4,
            pl.BlockSpec((1, group, 256), lambda s: (s, 0, 0)), "attend_back", 15 * count,
            scratch=[pltpu.VMEM((128, group), f32)], grid=(count,),
        )(lse, inner, q_all, k_all, v_all, grads)

    back_01 = attend_back(0, heads - 1, lse, 0, after(grad_all, down_other, up_away, down_mine, up_mine))
    down_y, up_x = after(down_y, back_01), after(up_x, back_01)
    (down_keep, down_give), (down_keep_two, down_give_two) = halves(down_mine, near_z), halves(down_y, near_z)
    down_half_sum, down_away = add_low(down_keep, down_keep_two), add_low(down_give, down_give_two)
    up_half_sum = add_low(up_mine[0], up_x[0])
    up_other = add_low(up_mine[1], up_x[1])
    down_x = swap(down_away, rows_size, near_z)
    up_y = over(up_other, NEXT)
    back_2 = attend_back(heads - 1, 1, lse, heads - 1, after(grad_all, back_01, down_away, up_other, up_half_sum, down_half_sum))
    down_x, up_y = after(down_x, back_2), after(up_y, back_2)
    (down_keep, down_give), (down_keep_two, down_give_two) = halves(down_half_sum, 1), halves(down_x, 1)
    (up_keep, up_give), (up_keep_two, up_give_two) = halves(up_half_sum, near_z), halves(up_y, near_z)
    down_z, down_away = add_low(down_keep, down_keep_two), add_low(down_give, down_give_two)
    up_z, up_away = add_low(up_keep, up_keep_two), add_low(up_give, up_give_two)
    up_got, down_got = swap(up_away, rows_size, near_z), swap(down_away, rows_size, 1)

    def project_back(chosen, counts):
        return call(
            functools.partial(project_back_kernel, chosen),
            (shape_of((2, rows, heads * 128 + wide), bf16),) + (shape_of((rows, width_all), bf16),) * 2,
            [SMEM] + whole_specs(3), (VMEM,) * 3, "project_back", 6,
            scratch=[pltpu.VMEM((TILE, 256), bf16)] * heads,
        )(counts, back_01, back_2, weight_heads)

    local_far, b3, b2 = project_back((3, 2), after(counts, up_away, up_z, down_away, down_z))

    up_got, down_got, b3 = lax.optimization_barrier((up_got, down_got, b3))
    split = down_z.shape[0]
    mixed = jnp.concatenate([add_low(down_z, down_got), add_low(up_z, up_got)], axis=0)

    over_far = over(b3, CORE)
    mixed_got = swap(mixed, rows_size, far_z[0])
    local_near, b1, b0 = project_back((1, 0), after(counts, mixed, b2))
    over_far, b2, b1 = lax.optimization_barrier((over_far, b2, b1))
    over_near = over(b1, CORE)
    first = rows * 3 // 4
    back_one, back_two = add_low(b2[:first], over_far[:first]), add_low(b2[first:], over_far[first:])
    far_one = over(back_one, NEXT)
    qkv_grad, qkv_sums = call(
        project_grad_kernel,
        (shape_of((width_all, heads * 128 + wide), bf16), shape_of((8, heads * 128 + wide), f32)),
        whole_specs(6), (VMEM, VMEM), "project_grad", 6,
    )(*parts[::-1], after(local_far, back_one), local_near)
    q_keep, q_give = halves(qkv_grad, 1)
    q_got = swap(q_give, rows_size, 1)
    block_spec = pl.BlockSpec((1, rows, hidden), lambda s: (s, 0, 0))
    down_spec = pl.BlockSpec((1, hidden, width_all), lambda s: (s, 0, 0))
    layer_out = call(
        layer_kernel,
        shape_of((rows, width_all), bf16),
        [full((rows, width_all)), block_spec, down_spec], full((rows, width_all)), "layer", 8,
        scratch=[pltpu.VMEM((rows, width_all), f32)], grid=(4,),
    )(after(base, q_give), act, down_all)
    far_one, back_two, layer_out, mixed_got = lax.optimization_barrier((far_one, back_two, layer_out, mixed_got))
    mixed = add_low(mixed, mixed_got)
    for bit in far_z[1:]:
        mixed = add_low(mixed, swap(mixed, rows_size, bit))
    q_got = after(q_got, mixed)
    far_two = over(back_two, NEXT)
    down_z, up_z = mixed[:split], mixed[split:]
    cut_up = up_z.shape[0] // 2
    up_one, up_two = up_z[:cut_up], up_z[cut_up:]
    down_got = swap(down_z, rows_size, near_z)
    one_got, two_got = swap(up_one, rows_size, 1), swap(after(up_two, down_z), rows_size, near_z)
    q_keep, q_give = halves(after(add_low(q_keep, q_got), down_z), near_z)
    q_got = swap(q_give, rows_size, near_z)
    far_two, down_got = lax.optimization_barrier((far_two, down_got))
    down_z = joined(down_z[None], down_got[None], near_z)
    down_got = swap(down_z, rows_size, 1)

    tokens_grad, small = call(
        last_kernel,
        (shape_of((rows, width_all), f32), shape_of((leads + 16, width_all), bf16)),
        [VMEM, VMEM, SMEM] + whole_specs(11) + [SMEM], (VMEM, VMEM), "last", 7,
    )(
        tokens, frame_id, lead_index, lead_embed, ln1_gain, perm, after(b0, q_give, up_one, up_two, down_z), over_near, far_one, far_two, xgrad,
        sums_two, up_b, qkv_sums, me,
    )

    small, one_got, two_got, q_got = lax.optimization_barrier((small, one_got, two_got, q_got))
    up_one = joined(up_one[None], one_got[None], 1)
    up_two = joined(up_two[None], two_got[None], near_z)
    q_z = add_low(q_keep, q_got)
    q_far = swap(q_z, rows_size, far_z[0])
    two_got = swap(up_two, rows_size, 1)
    small = add_low(small, over(small, CORE))
    small = add_low(small, over(small, NEXT))
    small = add_low(small, swap(small, rows_size, near_z))
    small, q_far = lax.optimization_barrier((small, q_far))
    q_z = add_low(q_z, q_far)
    for bit in far_z[1:]:
        q_z = add_low(q_z, swap(q_z, rows_size, bit))
    q_got = swap(q_z, rows_size, near_z)
    for bit in far_z:
        small = add_low(small, swap(small, rows_size, bit))
    one_got = swap(after(up_one, q_z), rows_size, near_z)
    q_z = joined(q_z, q_got, near_z)
    q_got = swap(q_z, rows_size, 1)
    down_sum = joined(down_z, down_got, 1, 1).astype(f32).reshape(hidden, width_all)
    up_sum, out_sum = call(
        join_kernel,
        (shape_of((width_all, hidden), f32), shape_of((width, hidden), f32)),
        whole_specs(4) + [SMEM], (VMEM, VMEM), "join", 2,
    )(up_one, one_got, up_two, two_got, place)
    qkv_sum = joined(q_z, q_got, 1)

    pairs_sum = qkv_sum[:, 0 : heads * 128].reshape(width_all, heads, 2, HEAD).transpose(2, 0, 1, 3)
    qkv_out = jnp.concatenate(
        [
            pairs_sum.reshape(2, width_all, width),
            qkv_sum[:, heads * 128 : heads * 128 + width].reshape(1, width_all, width),
        ],
        axis=0,
    ).astype(f32)
    vector = shape_of((width_all,), f32)
    lead_sum, g1, b1, g2, b2, out_b, down_b, up_b_sum, qv_sum = call(
        finish_kernel,
        (shape_of((leads, width_all), f32),) + (vector,) * 6 + (shape_of((hidden,), f32), shape_of((2, width), f32)),
        [VMEM, VMEM, SMEM], (VMEM,) * 9, "finish", 1,
    )(small, swap(small, rows_size, 1), me)
    return (
        layer_out, tokens_grad, lead_sum, g1, b1, qkv_out, qv_sum, out_sum, out_b, g2, b2,
        up_sum, up_b_sum, down_sum, down_b,
    )


def solution(mesh):
    rows_size = mesh.shape["rows"]
    split = P(("rows", "tp"), None)
    placed = (
        split, P(("rows", "tp")), P("rows"), P(), P(), P(), P(None, None, "tp"), P(None, "tp"),
        P("tp", None), P(), P(), P(), P(None, "tp"), P("tp"), P("tp", None), P(), split,
    )
    return jax.shard_map(
        functools.partial(on_device, rows_size),
        mesh=mesh,
        in_specs=placed,
        out_specs=(
            split, split, P(), P(), P(), P(None, None, "tp"), P(None, "tp"), P("tp", None), P(), P(), P(),
            P(None, "tp"), P("tp"), P("tp", None), P(),
        ),
        check_vma=False,
    )
```
